32 devices in a mesh: grid: 8 (over z, x), sub: 4 (over y, core).
Axes of the slice: x: 2, y: 2, z: 4, core: 2. Of those that a mesh axis runs over, the one named last changes fastest.
Arguments:
- fine_residual: float32 [8, 32, 5, 16, 256], P('grid', 'sub'), may hold values from -16 to 16
- fine_solution: float32 [8, 32, 5, 16, 256], P('grid', 'sub'), may hold values from -6 to 6
- plane_of_slot: int32 [8, 32], P('grid', 'sub'), may hold values from 0 to 31, as said below
- coarse_diagonal: float32 [8, 16, 5, 8, 128], P('grid', 'sub'), may hold values from 0.5 to 8
- coupling: float32 [5, 5], replicated, may hold values from -2.5 to 2.5
- donor_cells: int32 [8, 4, 64], P('grid', 'sub'), may hold values from 0 to 2942, as said below
- donor_offsets: float32 [8, 4, 3, 64], P('grid', 'sub'), may hold values from 0 to 1
- receptor_cells: int32 [8, 4, 64], P('grid', 'sub'), may hold values from 0 to 4095, as said below
- fringe_counts: int32 [8, 8], replicated, may hold values from 0 to 8, as said below
Outputs:
- corrected: float32 [8, 32, 5, 16, 256], P('grid', 'sub')
The draws below stay inside these ranges and needn't reach their ends.
Inputs may be any that keep to these rules, and one draw needn't show every extreme that they name: `plane_of_slot`: each row holds every fine plane number of its grid once. The 8 slots of one device (slots 8 s to 8 s + 7) hold at most 2 fine planes whose coarse planes belong to any one sub index, and exactly 2 for some pair. `donor_cells`: A donor base cell's local plane, row and column are below 3, 7 and 127, so its eight corners lie on the same device. `receptor_cells`: the 64 receptor cells of one device are distinct. `fringe_counts`: entry [g, h] counts the live rows that every device of grid g sends to the device of grid h with the same sub index; the diagonal is 0.
All inputs are finite; a program needn't handle non-finite values.
Results may differ from the reference program's by a relative error of at most 0.0003.
Values sent between devices are 32-bit elements; how exact they have to be, the bound alone decides.
No kernel may reach another device: no remote copies, remote signals or barrier semaphores. Data moves between devices by JAX's collectives and lax.ppermute only.
A program may use at most 64 MiB of HBM per device.

```python
import jax
import jax.numpy as jnp
from jax import lax

VARIABLES = 5
PLANES = 4
COARSE_Y = 8
COARSE_Z = 128
FRINGE = 8
SWEEPS = 2
GRIDS = 8
SUBS = 4
COARSE_PLANES = 16
FINE_PLANES = 32
SLOTS = 64
CELLS = 4096


def draw_plane_of_slot(key, part):
    key = jax.random.fold_in(key, 14)

    def one_grid(grid_key):
        key_off, key_rot, key_sig, key_tie = jax.random.split(grid_key, 4)
        shifts = jax.random.permutation(key_off, PLANES) % SUBS
        shifts = (shifts + jax.random.randint(key_rot, (), 0, SUBS)) % SUBS
        orders = jax.vmap(lambda one_key: jax.random.permutation(one_key, 2 * PLANES))(jax.random.split(key_sig, SUBS))
        owner = (jnp.arange(SUBS, dtype=jnp.int32)[:, None] + shifts[orders // 2]) % SUBS
        ties = jax.random.permutation(key_tie, FINE_PLANES)
        ranking = jnp.argsort(owner.reshape(-1) * FINE_PLANES + ties, stable=True)
        return jnp.zeros((FINE_PLANES,), jnp.int32).at[ranking].set(jnp.arange(FINE_PLANES, dtype=jnp.int32))
    return jax.vmap(one_grid)(jax.random.split(key, GRIDS)).astype(jnp.int32)


def draw_donor_cells(key, part):
    key = jax.random.fold_in(key, 11)
    key_x, key_y, key_z, key_top, key_low = jax.random.split(key, 5)
    dims_out = (GRIDS, SUBS, SLOTS)
    plane_part = jax.random.randint(key_x, dims_out, 0, PLANES - 1)
    row_part = jax.random.randint(key_y, dims_out, 0, COARSE_Y - 1)
    column_part = jax.random.randint(key_z, dims_out, 0, COARSE_Z - 1)
    cells_out = ((plane_part * COARSE_Y + row_part) * COARSE_Z + column_part).reshape(-1)
    total = GRIDS * SUBS * SLOTS
    top_at = jax.random.randint(key_top, (), 0, total)
    low_at = (top_at + 1 + jax.random.randint(key_low, (), 0, total - 1)) % total
    positions = jnp.arange(total, dtype=jnp.int32)
    highest = (PLANES - 2) * COARSE_Y * COARSE_Z + (COARSE_Y - 2) * COARSE_Z + COARSE_Z - 2
    cells_out = jnp.where(positions == top_at, highest, cells_out)
    cells_out = jnp.where(positions == low_at, 0, cells_out)
    return cells_out.reshape(dims_out).astype(jnp.int32)


def draw_receptor_cells(key, part):
    key = jax.random.fold_in(key, 12)
    device_keys = jax.random.split(key, GRIDS * SUBS)
    chosen = jax.vmap(lambda one_key: jax.random.permutation(one_key, CELLS)[:SLOTS])(device_keys)
    return chosen.reshape(GRIDS, SUBS, SLOTS).astype(jnp.int32)


def draw_fringe_counts(key, part):
    key = jax.random.fold_in(key, 13)
    key_counts, key_row, key_col = jax.random.split(key, 3)
    counts_out = jax.random.randint(key_counts, (GRIDS, GRIDS), 0, FRINGE + 1)
    source = jax.random.randint(key_row, (), 0, GRIDS)
    target = (source + 1 + jax.random.randint(key_col, (), 0, GRIDS - 1)) % GRIDS
    grid_ids = jnp.arange(GRIDS, dtype=jnp.int32)
    full_entry = (grid_ids[:, None] == source) & (grid_ids[None, :] == target)
    counts_out = jnp.where(full_entry, FRINGE, counts_out)
    counts_out = jnp.where(grid_ids[:, None] == grid_ids[None, :], 0, counts_out)
    return counts_out.astype(jnp.int32)


def levels(own_key, extent, cuts, smallest, high):
    loudness = 1.0
    for axis_at, shards_of in cuts:
        draws = jax.random.uniform(jax.random.fold_in(jax.random.fold_in(own_key, 6), axis_at), (shards_of,), jnp.float32, smallest / len(cuts), high / len(cuts))
        loudness = loudness * jnp.repeat(jnp.exp(draws), extent[axis_at] // shards_of).reshape((-1,) + (1,) * (len(extent) - 1 - axis_at))
    return loudness


def noise(stream_key, dims, scale, reach, pieces=(), kind=jnp.bfloat16):
    result = jax.random.normal(stream_key, dims, jnp.float32) * scale
    if len(pieces) > 0:
        result = levels(stream_key, dims, pieces, -0.22, 0.18) * result
    return jnp.clip(result, min=-reach, max=reach).astype(kind)


def setup_inputs(seed: int = 0) -> dict:
    key_of = jax.random.split(jax.random.key(seed), 10)
    fine_residual = noise(key_of[0], (GRIDS, FINE_PLANES, VARIABLES, 2 * COARSE_Y, 2 * COARSE_Z), 4.0, 16.0, ((0, 8), (1, 4)), jnp.float32)
    fine_solution = noise(key_of[1], (GRIDS, FINE_PLANES, VARIABLES, 2 * COARSE_Y, 2 * COARSE_Z), 1.0, 6.0, ((0, 8), (1, 4)), jnp.float32)
    plane_of_slot = draw_plane_of_slot(jax.random.fold_in(key_of[9], 71), 0)
    coarse_diagonal = jnp.clip(0.5 + 7.5 * jax.random.uniform(key_of[3], (GRIDS, COARSE_PLANES, VARIABLES, COARSE_Y, COARSE_Z), jnp.float32) ** levels(key_of[3], (GRIDS, COARSE_PLANES, VARIABLES, COARSE_Y, COARSE_Z), ((0, 8), (1, 4)), -0.2, 0.2), 0.5, 8.0)
    coupling = noise(key_of[4], (VARIABLES, VARIABLES), VARIABLES ** -0.5, 2.5, (), jnp.float32)
    donor_cells = draw_donor_cells(jax.random.fold_in(key_of[9], 71), 0)
    donor_offsets = jnp.clip(1.0 * jax.random.uniform(key_of[6], (GRIDS, SUBS, 3, SLOTS), jnp.float32) ** levels(key_of[6], (GRIDS, SUBS, 3, SLOTS), ((0, 8), (1, 4)), -0.2, 0.2), 0.0, 1.0)
    receptor_cells = draw_receptor_cells(jax.random.fold_in(key_of[9], 71), 0)
    fringe_counts = draw_fringe_counts(jax.random.fold_in(key_of[9], 71), 0)
    return {"fine_residual": fine_residual, "fine_solution": fine_solution, "plane_of_slot": plane_of_slot, "coarse_diagonal": coarse_diagonal, "coupling": coupling, "donor_cells": donor_cells, "donor_offsets": donor_offsets, "receptor_cells": receptor_cells, "fringe_counts": fringe_counts}


OMEGA = 0.8


def restrict_planes(fine_field):
    dims_in = fine_field.shape
    split_cells = fine_field.reshape(dims_in[:-2] + (dims_in[-2] // 2, 2, dims_in[-1] // 2, 2))
    return 0.125 * jnp.sum(split_cells, axis=(-3, -1))


def pair_sum(field, axis):
    which = axis % field.ndim
    length = field.shape[which]
    empty = jnp.zeros_like(lax.slice_in_dim(field, 0, 1, axis=which))
    below_side = jnp.concatenate([empty, lax.slice_in_dim(field, 0, length - 1, axis=which)], axis=which)
    above_side = jnp.concatenate([lax.slice_in_dim(field, 1, length, axis=which), empty], axis=which)
    return below_side + above_side


def operate(field, padded, diagonal, coupling):
    which = field.ndim - 4
    length = padded.shape[which]
    beside = lax.slice_in_dim(padded, 2, length, axis=which) + lax.slice_in_dim(padded, 0, length - 2, axis=which)
    beside = beside + pair_sum(field, field.ndim - 2)
    beside = beside + pair_sum(field, field.ndim - 1)
    coupled = jnp.einsum("vw,...wyz->...vyz", coupling, field, precision=lax.Precision.HIGHEST)
    return (6.0 + diagonal) * field - beside + 2.0 * jnp.tanh(coupled)


def corner_values(flat_field, donor_base, height, depth):
    corners = []
    for step_x in (0, 1):
        for step_y in (0, 1):
            for step_z in (0, 1):
                where_cells = donor_base + step_x * height * depth + step_y * depth + step_z
                corners.append(jnp.take_along_axis(flat_field, where_cells[..., None, :], axis=-1))
    return corners


def blend(corners, offsets):
    frac_x = offsets[..., 0:1, :]
    frac_y = offsets[..., 1:2, :]
    frac_z = offsets[..., 2:3, :]
    summed = None
    number = 0
    for step_x in (0, 1):
        for step_y in (0, 1):
            for step_z in (0, 1):
                weight_x = frac_x if step_x else 1.0 - frac_x
                weight_y = frac_y if step_y else 1.0 - frac_y
                weight_z = frac_z if step_z else 1.0 - frac_z
                term = weight_x * weight_y * weight_z * corners[number]
                summed = term if summed is None else summed + term
                number = number + 1
    return summed


def mark_cells(target_cells, cell_count):
    return jnp.zeros((cell_count,), jnp.float32).at[target_cells].set(1.0, mode="drop")


def set_cells(flat_field, target_cells, values):
    return flat_field.at[:, target_cells].set(values, mode="drop")


def refine(field, axis):
    which = axis % field.ndim
    length = field.shape[which]
    empty = jnp.zeros_like(lax.slice_in_dim(field, 0, 1, axis=which))
    below_side = jnp.concatenate([empty, lax.slice_in_dim(field, 0, length - 1, axis=which)], axis=which)
    above_side = jnp.concatenate([lax.slice_in_dim(field, 1, length, axis=which), empty], axis=which)
    first_half = 0.75 * field + 0.25 * below_side
    second_half = 0.75 * field + 0.25 * above_side
    joined = jnp.stack([first_half, second_half], axis=which + 1)
    new_dims = list(field.shape)
    new_dims[which] = 2 * length
    return joined.reshape(new_dims)


def to_flat(field):
    split_field = field.reshape(GRIDS, SUBS, PLANES, VARIABLES, COARSE_Y, COARSE_Z)
    return split_field.transpose(0, 1, 3, 2, 4, 5).reshape(GRIDS, SUBS, VARIABLES, CELLS)


def from_flat(flat_field, width):
    split_field = flat_field.reshape(GRIDS, SUBS, width, PLANES, COARSE_Y, COARSE_Z)
    return split_field.transpose(0, 1, 3, 2, 4, 5).reshape(GRIDS, COARSE_PLANES, width, COARSE_Y, COARSE_Z)


def reference(fine_residual, fine_solution, plane_of_slot, coarse_diagonal, coupling, donor_cells, donor_offsets, receptor_cells, fringe_counts):
    residual_planes = restrict_planes(fine_residual)
    solution_planes = restrict_planes(fine_solution)
    targets = (plane_of_slot // 2).astype(jnp.int32)
    grid_rows = jnp.arange(GRIDS, dtype=jnp.int32)[:, None]
    empty = jnp.zeros((GRIDS, COARSE_PLANES, VARIABLES, COARSE_Y, COARSE_Z), jnp.float32)
    restricted_solution = empty.at[grid_rows, targets].add(solution_planes)
    restricted_residual = empty.at[grid_rows, targets].add(residual_planes)

    def apply_operator(field):
        padded = jnp.pad(field, ((0, 0), (1, 1), (0, 0), (0, 0), (0, 0)))
        return operate(field, padded, coarse_diagonal, coupling)

    forcing = apply_operator(restricted_solution) + restricted_residual
    slot_ids = jnp.arange(SLOTS, dtype=jnp.int32)
    allowed = jnp.repeat(fringe_counts.T, FRINGE, axis=1)
    live_slot = (slot_ids % FRINGE)[None, :] < allowed
    target_cells = jnp.where(live_slot[:, None, :], receptor_cells, CELLS).astype(jnp.int32)
    flat_targets = target_cells.reshape(GRIDS * SUBS, SLOTS)
    receptor_mask = jax.vmap(lambda cells_here: mark_cells(cells_here, CELLS))(flat_targets)
    receptor_mask = from_flat(receptor_mask.reshape(GRIDS, SUBS, 1, CELLS), 1)
    field = restricted_solution
    for sweep_index in range(SWEEPS):
        flat_field = to_flat(field)
        values = blend(corner_values(flat_field, donor_cells, COARSE_Y, COARSE_Z), donor_offsets)
        arrived = values.reshape(GRIDS, SUBS, VARIABLES, GRIDS, FRINGE).transpose(3, 1, 2, 0, 4)
        arrived = arrived.reshape(GRIDS * SUBS, VARIABLES, SLOTS)
        flat_field = jax.vmap(set_cells)(flat_field.reshape(GRIDS * SUBS, VARIABLES, CELLS), flat_targets, arrived)
        field = from_flat(flat_field.reshape(GRIDS, SUBS, VARIABLES, CELLS), VARIABLES)
        update = field + OMEGA * (forcing - apply_operator(field)) / (6.0 + coarse_diagonal)
        field = jnp.where(receptor_mask > 0.5, field, update)
    correction = field - restricted_solution
    padded_correction = jnp.pad(correction, ((0, 0), (1, 1), (0, 0), (0, 0), (0, 0)))
    neighbour = (targets - 1 + 2 * (plane_of_slot % 2)).astype(jnp.int32)
    along_x = 0.75 * padded_correction[grid_rows, targets + 1] + 0.25 * padded_correction[grid_rows, neighbour + 1]
    prolonged = refine(refine(along_x, -2), -1)
    return fine_solution + prolonged
```

```python
import functools

import jax
import jax.numpy as jnp
from jax import lax
from jax.experimental import pallas as pl
from jax.experimental.pallas import tpu as pltpu
from jax.sharding import PartitionSpec as P

FRINGE = 8
SWEEPS = 2


OMEGA = 0.8


def padded_2(block, sides, width):
    for axis, dim in sides:
        count = lax.axis_size(axis)
        forward = [(i, i + 1) for i in range(count - 1)]
        backward = [(target, source) for source, target in forward]
        low = lax.ppermute(
            lax.slice_in_dim(block, block.shape[dim] - width, None, axis=dim), axis, forward
        )
        high = lax.ppermute(lax.slice_in_dim(block, 0, width, axis=dim), axis, backward)
        block = jnp.concatenate([low, block, high], axis=dim)
    return block


def restrict_planes(fine_field):
    dims_in = fine_field.shape
    split_cells = fine_field.reshape(dims_in[:-2] + (dims_in[-2] // 2, 2, dims_in[-1] // 2, 2))
    return 0.125 * jnp.sum(split_cells, axis=(-3, -1))


def pair_sum(field, axis):
    which = axis % field.ndim
    length = field.shape[which]
    empty = jnp.zeros_like(lax.slice_in_dim(field, 0, 1, axis=which))
    below_side = jnp.concatenate(
        [empty, lax.slice_in_dim(field, 0, length - 1, axis=which)], axis=which
    )
    above_side = jnp.concatenate(
        [lax.slice_in_dim(field, 1, length, axis=which), empty], axis=which
    )
    return below_side + above_side


def operate(field, padded, diagonal, coupling):
    which = field.ndim - 4
    length = padded.shape[which]
    beside = lax.slice_in_dim(padded, 2, length, axis=which) + lax.slice_in_dim(
        padded, 0, length - 2, axis=which
    )
    beside = beside + pair_sum(field, field.ndim - 2)
    beside = beside + pair_sum(field, field.ndim - 1)
    coupled = jnp.einsum("vw,...wyz->...vyz", coupling, field, precision=lax.Precision.HIGHEST)
    return (6.0 + diagonal) * field - beside + 2.0 * jnp.tanh(coupled)


def apply_operator(field, diagonal, coupling):
    padded = padded_2(field, (("sub", 0),), 1)
    return operate(field, padded, diagonal, coupling)


def corner_values(flat_field, donor_base, height, depth):
    corners = []
    for step_x in (0, 1):
        for step_y in (0, 1):
            for step_z in (0, 1):
                where_cells = donor_base + step_x * height * depth + step_y * depth + step_z
                corners.append(jnp.take_along_axis(flat_field, where_cells[..., None, :], axis=-1))
    return corners


def blend(corners, offsets):
    frac_x = offsets[..., 0:1, :]
    frac_y = offsets[..., 1:2, :]
    frac_z = offsets[..., 2:3, :]
    summed = None
    number = 0
    for step_x in (0, 1):
        for step_y in (0, 1):
            for step_z in (0, 1):
                weight_x = frac_x if step_x else 1.0 - frac_x
                weight_y = frac_y if step_y else 1.0 - frac_y
                weight_z = frac_z if step_z else 1.0 - frac_z
                term = weight_x * weight_y * weight_z * corners[number]
                summed = term if summed is None else summed + term
                number = number + 1
    return summed


def refine(field, axis):
    which = axis % field.ndim
    length = field.shape[which]
    empty = jnp.zeros_like(lax.slice_in_dim(field, 0, 1, axis=which))
    below_side = jnp.concatenate(
        [empty, lax.slice_in_dim(field, 0, length - 1, axis=which)], axis=which
    )
    above_side = jnp.concatenate(
        [lax.slice_in_dim(field, 1, length, axis=which), empty], axis=which
    )
    first_half = 0.75 * field + 0.25 * below_side
    second_half = 0.75 * field + 0.25 * above_side
    joined = jnp.stack([first_half, second_half], axis=which + 1)
    new_dims = list(field.shape)
    new_dims[which] = 2 * length
    return joined.reshape(new_dims)


def shards(
    fine_residual,
    fine_solution,
    plane_of_slot,
    coarse_diagonal,
    coupling,
    donor_cells,
    donor_offsets,
    receptor_cells,
    fringe_counts,
):
    grid_index = lax.axis_index("grid")
    sub_index = lax.axis_index("sub")
    diagonal = coarse_diagonal[0]
    planes, variables, height, depth_cells = diagonal.shape
    cell_count = planes * height * depth_cells
    plane_ids = plane_of_slot[0]
    blocks = plane_ids.shape[0]
    solution_planes = restrict_planes(fine_solution[0])
    residual_planes = restrict_planes(fine_residual[0])
    contrib = jnp.stack([solution_planes, residual_planes], axis=1).reshape(blocks, -1)
    targets = plane_ids // 2
    wanted = sub_index * planes + jnp.arange(planes, dtype=jnp.int32)
    gathered, gathered_ids = (
        lax.all_gather(contrib, "sub", axis=0, tiled=True),
        lax.all_gather(plane_ids, "sub", axis=0, tiled=True),
    )
    select = ((gathered_ids // 2)[None, :] == wanted[:, None]).astype(jnp.float32)
    owned_sums = jnp.dot(
        select, gathered, precision=lax.Precision.HIGHEST, preferred_element_type=jnp.float32
    )
    owned_sums = owned_sums.reshape(planes, 2, variables, height, depth_cells)
    restricted_solution = owned_sums[:, 0]
    restricted_residual = owned_sums[:, 1]
    forcing = apply_operator(restricted_solution, diagonal, coupling) + restricted_residual
    slot_count = donor_cells.shape[-1]
    column = lax.dynamic_index_in_dim(fringe_counts, grid_index, 1, keepdims=False)
    allowed = jnp.repeat(column, FRINGE)
    live_slot = jnp.arange(slot_count, dtype=jnp.int32) % FRINGE < allowed
    target_cells = jnp.where(live_slot, receptor_cells[0, 0], cell_count)
    receptor_mask = jnp.zeros((cell_count,), jnp.float32).at[target_cells].set(1.0, mode="drop")
    receptor_mask = receptor_mask.reshape(planes, 1, height, depth_cells)
    donor_base = donor_cells[0, 0]
    offsets = donor_offsets[0, 0]
    field = restricted_solution
    for sweep_index in range(SWEEPS):
        flat_field = field.transpose(1, 0, 2, 3).reshape(variables, cell_count)
        corners = corner_values(flat_field, donor_base, height, depth_cells)
        arrived = lax.all_to_all(
            blend(corners, offsets), "grid", split_axis=1, concat_axis=1, tiled=True
        )
        flat_field = flat_field.at[:, target_cells].set(arrived, mode="drop")
        field = flat_field.reshape(variables, planes, height, depth_cells).transpose(1, 0, 2, 3)
        update = field + OMEGA * (forcing - apply_operator(field, diagonal, coupling)) / (
            6.0 + diagonal
        )
        field = jnp.where(receptor_mask > 0.5, field, update)
    correction = (field - restricted_solution).reshape(planes, -1)
    neighbour = targets - 1 + 2 * (plane_ids % 2)
    shard_rows = lax.all_gather(correction, "sub", axis=0, tiled=True)
    row_ids = jnp.arange(shard_rows.shape[0], dtype=jnp.int32)
    weights = 0.75 * (targets[:, None] == row_ids[None, :]).astype(jnp.float32)
    weights = weights + 0.25 * (neighbour[:, None] == row_ids[None, :]).astype(jnp.float32)
    along_x = jnp.dot(
        weights, shard_rows, precision=lax.Precision.HIGHEST, preferred_element_type=jnp.float32
    )
    along_x = along_x.reshape(blocks, variables, height, depth_cells)
    prolonged = refine(refine(along_x, -2), -1)
    return (fine_solution[0] + prolonged)[None]


FRINGE_LANES = 64
BF16 = jnp.bfloat16
F32 = jnp.float32
HIGHEST = lax.Precision.HIGHEST
VMEM = pl.BlockSpec(memory_space=pltpu.VMEM)
SMEM = pl.BlockSpec(memory_space=pltpu.SMEM)


def dot_exact(values, matrix):
    high = values.astype(BF16)
    rest = values - high.astype(F32)
    middle = rest.astype(BF16)
    low = (rest - middle.astype(F32)).astype(BF16)
    total = jnp.dot(low, matrix, preferred_element_type=F32)
    total = total + jnp.dot(middle, matrix, preferred_element_type=F32)
    return total + jnp.dot(high, matrix, preferred_element_type=F32)


def iota(shape, dim):
    return lax.broadcasted_iota(jnp.int32, shape, dim)


def restrict_kernel(
    sizes, counts, residual, fine, diagonal, donors, offsets, receptors, ids, first, second, wide
):
    planes, variables, height, depth = sizes["coarse"]
    blocks = sizes["blocks"]
    grids = sizes["grids"]
    slots = sizes["slots"]
    grid_index = lax.axis_index("grid")
    base = lax.axis_index("sub") * (planes * height * depth)
    pair = jnp.where(
        iota((2 * depth, depth), 0) // 2 == iota((2 * depth, depth), 1), 0.125, 0.0
    ).astype(BF16)
    count = blocks * variables
    for source, target in ((fine, first), (residual, second)):
        rows = source[0].reshape(count * 2 * height, 2 * depth)
        wide[...] = dot_exact(rows, pair).reshape(count, 2 * height, depth)
        target[0:count] = (
            wide[:, pl.ds(0, height, stride=2), :] + wide[:, pl.ds(1, height, stride=2), :]
        )
    second[count : count + planes * variables] = diagonal[0].reshape(
        planes * variables, height, depth
    )
    lane = iota((1, slots), 1)
    allowed = jnp.zeros((1, slots), jnp.int32)
    for g in range(grids):
        allowed = jnp.where(lane // FRINGE == g, counts[g, grid_index], allowed)
    cell = jnp.where(lane % FRINGE < allowed, receptors[0] + base, -1)
    first[count] = jnp.zeros((height, depth), F32)
    first[count, 0:1, 0:slots] = (donors[0] + base).astype(F32)
    first[count, 1:4, 0:slots] = offsets[0, 0]
    first[count, 4:5, 0:slots] = cell.astype(F32)
    first[count, 5:6, 0:blocks] = ids[...].astype(F32)


def gather_rows(parts, at, rows, slots):
    for i, part in enumerate(parts):
        rows[:, i * slots : (i + 1) * slots] = part[at, :, 0:slots]


def split_cell(cell, height, depth):
    return cell // (height * depth), cell // depth % height, cell % depth


def interpolate(field, rows, sizes):
    total, variables, height, depth = field.shape
    count = rows.shape[1]
    cell = rows[0:1, :].astype(jnp.int32)
    plane, row, column = split_cell(cell, height, depth)
    frac_x, frac_y, frac_z = rows[1:2, :], rows[2:3, :], rows[3:4, :]

    def hats(shape, dim, start, frac):
        at = iota(shape, dim)
        return jnp.where(at == start, 1.0 - frac, 0.0) + jnp.where(at == start + 1, frac, 0.0)

    weight_z = hats((depth, count), 0, column, frac_z)
    weight_y = hats((height, count), 0, row, frac_y)
    along_z = jnp.dot(
        field.reshape(total * variables * height, depth),
        weight_z,
        precision=HIGHEST,
        preferred_element_type=F32,
    ).reshape(total, variables, height, count)
    summed = None
    for p in range(total):
        weight_x = jnp.where(plane == p, 1.0 - frac_x, 0.0) + jnp.where(
            plane + 1 == p, frac_x, 0.0
        )
        term = along_z[p] * (weight_x * weight_y)[None]
        summed = term if summed is None else summed + term
    return jnp.sum(summed, axis=1)


def send_fringe(values, out, grids):
    variables, count = values.shape
    lane = iota((8, 128), 1)
    padded = jnp.concatenate([values, jnp.zeros((8 - variables, count), F32)], axis=0)
    left, right = padded[:, 0:128], padded[:, 128:256]
    for h in range(grids):
        at_left = pltpu.roll(left, (128 - 8 * h) % 128, 1)
        at_right = pltpu.roll(right, (128 + 8 - 8 * h) % 128, 1)
        out[h] = jnp.where(lane % 64 < 8, at_left, at_right)


def receive_fringe(arrived, grids):
    lane = iota((8, 128), 1)
    left = jnp.zeros((8, 128), F32)
    right = jnp.zeros((8, 128), F32)
    for g in range(grids):
        mine = lane % 64 // 8 == g
        left = left + jnp.where(mine, pltpu.roll(arrived[g], 8 * g, 1), 0.0)
        right = right + jnp.where(mine, pltpu.roll(arrived[g], (128 + 8 * g - 8) % 128, 1), 0.0)
    return jnp.concatenate([left, right], axis=1)


def spread(values, rows, shape):
    total, variables, height, depth = shape
    count = rows.shape[1]
    cell = rows[4:5, :].astype(jnp.int32)
    plane, row, column = split_cell(cell, height, depth)
    onehot = jnp.where(
        (iota((depth, count), 0) == column) & (cell >= 0), 1.0, 0.0
    ).astype(BF16)
    row_here = (iota((height, count), 0) == row) & (cell >= 0)
    here = jnp.concatenate([jnp.where(row_here & (plane == p), 1.0, 0.0) for p in range(total)], 0)
    contract = (((1,), (1,)), ((), ()))
    mask = lax.dot_general(here.astype(BF16), onehot, contract, preferred_element_type=F32)
    mask = mask.reshape(total, 1, height, depth)
    stacked = here.reshape(total, 1, height, count) * values[:variables][None, :, None, :]
    rows_in = stacked.reshape(total * variables * height, count)
    high = rows_in.astype(BF16)
    rest = rows_in - high.astype(F32)
    middle = rest.astype(BF16)
    low = (rest - middle.astype(F32)).astype(BF16)
    field = lax.dot_general(low, onehot, contract, preferred_element_type=F32)
    field = field + lax.dot_general(middle, onehot, contract, preferred_element_type=F32)
    field = field + lax.dot_general(high, onehot, contract, preferred_element_type=F32)
    return field.reshape(shape), mask


def neighbour_sum(field):
    total, variables, height, depth = field.shape
    flat = field.reshape(total * variables, height, depth)
    at_row = iota(flat.shape, 1)
    at_column = iota(flat.shape, 2)
    beside = jnp.where(at_row > 0, pltpu.roll(flat, 1, 1), 0.0)
    beside = beside + jnp.where(at_row < height - 1, pltpu.roll(flat, height - 1, 1), 0.0)
    beside = beside + jnp.where(at_column > 0, pltpu.roll(flat, 1, 2), 0.0)
    beside = beside + jnp.where(at_column < depth - 1, pltpu.roll(flat, depth - 1, 2), 0.0)
    beside = beside.reshape(field.shape)
    empty = jnp.zeros((1, variables, height, depth), F32)
    beside = beside + jnp.concatenate([empty, field[: total - 1]], axis=0)
    return beside + jnp.concatenate([field[1:], empty], axis=0)


def plane_numbers(parts, at, numbers, sems):
    copies = [
        pltpu.make_async_copy(part.at[at, 5:6, :], numbers.at[i : i + 1, :], sems.at[i])
        for i, part in enumerate(parts)
    ]
    for copy in copies:
        copy.start()
    return copies


def assemble(parts, numbers, blocks, out):
    variables = out.shape[1]
    out[...] = jnp.zeros(out.shape, F32)
    for i, part in enumerate(parts):
        for q in range(blocks):
            coarse = numbers[i, q].astype(jnp.int32) // 2
            out[pl.ds(coarse, 1)] += part[q * variables : (q + 1) * variables][None]


def first_fringe_kernel(sizes, *refs):
    subs = sizes["subs"]
    parts = refs[:subs]
    out, restricted, rows, numbers, sems = refs[subs:]
    count = sizes["blocks"] * sizes["coarse"][1]
    copies = plane_numbers(parts, count, numbers, sems)
    gather_rows(parts, count, rows, sizes["slots"])
    for copy in copies:
        copy.wait()
    assemble(parts, numbers, sizes["blocks"], restricted)
    send_fringe(interpolate(restricted[...], rows, sizes), out, sizes["grids"])


def second_fringe_kernel(sizes, *refs):
    subs = sizes["subs"]
    sub_index = lax.axis_index("sub")
    planes, variables, height, depth = sizes["coarse"]
    parts = refs[:subs]
    seconds = refs[subs : 2 * subs]
    restricted, arrived = refs[2 * subs : 2 * subs + 2]
    out, field, residual, gain, rows, numbers, sems = refs[2 * subs + 2 :]
    count = sizes["blocks"] * variables
    copies = plane_numbers(parts, count, numbers, sems)
    gather_rows(parts, count, rows, sizes["slots"])
    values = receive_fringe(arrived, sizes["grids"])
    shape = restricted.shape
    landed, mask = spread(values, rows, shape)
    for i, part in enumerate(seconds):
        owner = (sub_index ^ sizes["order"][i]) * planes
        own = part[count : count + planes * variables].reshape(planes, variables, height, depth)
        gain[pl.ds(owner, planes)] = OMEGA / (6.0 + own)
    for copy in copies:
        copy.wait()
    assemble(seconds, numbers, sizes["blocks"], residual)
    start = restricted[...]
    change = jnp.where(mask > 0.5, landed - start, 0.0)
    update = gain[...] * (residual[...] + neighbour_sum(change))
    now = start + jnp.where(mask > 0.5, change, update)
    field[...] = now
    send_fringe(interpolate(now, rows, sizes), out, sizes["grids"])


def couple(coupling, field):
    variables = field.shape[1]
    outs = []
    for v in range(variables):
        summed = coupling[v, 0] * field[:, 0]
        for x in range(1, variables):
            summed = summed + coupling[v, x] * field[:, x]
        outs.append(jnp.tanh(summed)[:, None])
    return jnp.concatenate(outs, axis=1)


def prolong_kernel(sizes, *refs):
    subs = sizes["subs"]
    planes, variables, height, depth = sizes["coarse"]
    blocks = sizes["blocks"]
    parts = refs[:subs]
    coupling, ids, restricted, field, residual, gain, arrived, fine = refs[subs : subs + 8]
    out, rows, padded, tall = refs[subs + 8 :]
    count = blocks * variables
    gather_rows(parts, count, rows, sizes["slots"])
    values = receive_fringe(arrived, sizes["grids"])
    landed, mask = spread(values, rows, restricted.shape)
    start = restricted[...]
    now = jnp.where(mask > 0.5, landed, field[...])
    change = now - start
    source = couple(coupling, start) - couple(coupling, now)
    update = gain[...] * (residual[...] + neighbour_sum(change) + 2.0 * source)
    correction = jnp.where(mask > 0.5, change, (1.0 - OMEGA) * change + update)
    total = correction.shape[0]
    padded[0:1] = jnp.zeros((1, variables, height, depth), F32)
    padded[total + 1 : total + 2] = jnp.zeros((1, variables, height, depth), F32)
    padded[1 : total + 1] = correction
    at_row = iota((variables, height, depth), 1)
    for q in range(blocks):
        number = ids[0, q]
        coarse = number // 2
        along = 0.75 * padded[coarse + 1] + 0.25 * padded[coarse + 2 * (number % 2)]
        below = jnp.where(at_row > 0, pltpu.roll(along, 1, 1), 0.0)
        above = jnp.where(at_row < height - 1, pltpu.roll(along, height - 1, 1), 0.0)
        here = slice(q * variables, (q + 1) * variables)
        tall[here, pl.ds(0, height, stride=2), :] = 0.75 * along + 0.25 * below
        tall[here, pl.ds(1, height, stride=2), :] = 0.75 * along + 0.25 * above
    coarse_at = iota((depth, 2 * depth), 0)
    fine_at = iota((depth, 2 * depth), 1)
    beside = fine_at // 2 - 1 + 2 * (fine_at % 2)
    widen = jnp.where(
        coarse_at == fine_at // 2, 0.75, jnp.where(coarse_at == beside, 0.25, 0.0)
    ).astype(BF16)
    prolonged = dot_exact(tall[...].reshape(count * 2 * height, depth), widen)
    out[...] = fine[...] + prolonged.reshape(fine.shape)


def spread_over_sub(block, order_bits):
    held = [block]
    count = lax.axis_size("sub")
    for bit in order_bits:
        pairs = [(i, i ^ bit) for i in range(count)]
        held = held + [lax.ppermute(one, "sub", pairs) for one in held]
    return held


def fast_shards(
    fine_residual,
    fine_solution,
    plane_of_slot,
    coarse_diagonal,
    coupling,
    donor_cells,
    donor_offsets,
    receptor_cells,
    fringe_counts,
):
    subs = lax.axis_size("sub")
    grids = lax.axis_size("grid")
    coarse = coarse_diagonal.shape[1:]
    planes, variables, height, depth = coarse
    blocks = plane_of_slot.shape[1]
    slots = donor_cells.shape[-1]
    bits = [1 << k for k in reversed(range(subs.bit_length() - 1))]
    order = [0]
    for bit in bits:
        order = order + [one ^ bit for one in order]
    sizes = dict(
        coarse=coarse, blocks=blocks, slots=slots, grids=grids, subs=subs, order=tuple(order)
    )
    count = blocks * variables
    total = subs * planes
    whole = (total, variables, height, depth)
    params = pltpu.CompilerParams(vmem_limit_bytes=48 * 1024 * 1024)
    tile = jax.ShapeDtypeStruct((grids, 8, 128), F32)
    full = jax.ShapeDtypeStruct(whole, F32)
    numbers = [pltpu.SMEM((subs, depth), F32), pltpu.SemaphoreType.DMA((subs,))]
    rows = pltpu.VMEM((8, subs * slots), F32)

    first, second = pl.pallas_call(
        functools.partial(restrict_kernel, sizes),
        out_shape=[
            jax.ShapeDtypeStruct((count + 1, height, depth), F32),
            jax.ShapeDtypeStruct((count + planes * variables, height, depth), F32),
        ],
        in_specs=[SMEM] + [VMEM] * 7,
        out_specs=[VMEM] * 2,
        scratch_shapes=[pltpu.VMEM((count, 2 * height, depth), F32)],
        compiler_params=params,
        name="restrict",
    )(
        fringe_counts,
        fine_residual,
        fine_solution,
        coarse_diagonal,
        donor_cells,
        donor_offsets,
        receptor_cells,
        plane_of_slot,
    )
    firsts = spread_over_sub(first, bits)
    out, restricted = pl.pallas_call(
        functools.partial(first_fringe_kernel, sizes),
        out_shape=[tile, full],
        in_specs=[VMEM] * subs,
        out_specs=[VMEM] * 2,
        scratch_shapes=[rows] + numbers,
        compiler_params=params,
        name="first_fringe",
    )(*firsts)
    seconds = spread_over_sub(second, bits)
    arrived = lax.all_to_all(out, "grid", 0, 0, tiled=True)
    out, field, residual, gain = pl.pallas_call(
        functools.partial(second_fringe_kernel, sizes),
        out_shape=[tile, full, full, full],
        in_specs=[VMEM] * (2 * subs + 2),
        out_specs=[VMEM] * 4,
        scratch_shapes=[rows] + numbers,
        compiler_params=params,
        name="second_fringe",
    )(*firsts, *seconds, restricted, arrived)
    arrived = lax.all_to_all(out, "grid", 0, 0, tiled=True)
    return pl.pallas_call(
        functools.partial(prolong_kernel, sizes),
        out_shape=jax.ShapeDtypeStruct(fine_solution.shape, F32),
        in_specs=[VMEM] * subs + [SMEM] * 2 + [VMEM] * 6,
        out_specs=VMEM,
        scratch_shapes=[
            rows,
            pltpu.VMEM((total + 2, variables, height, depth), F32),
            pltpu.VMEM((count, 2 * height, depth), F32),
        ],
        compiler_params=params,
        name="prolong",
    )(*firsts, coupling, plane_of_slot, restricted, field, residual, gain, arrived, fine_solution)


def solution(mesh):
    in_specs = (
        P("grid", "sub", None, None, None),
        P("grid", "sub", None, None, None),
        P("grid", "sub"),
        P("grid", "sub", None, None, None),
        P(),
        P("grid", "sub", None),
        P("grid", "sub", None, None),
        P("grid", "sub", None),
        P(),
    )
    out_specs = P("grid", "sub", None, None, None)
    small = mesh.shape["sub"] == 4 and mesh.shape["grid"] * FRINGE == 64
    body = fast_shards if small else shards
    return jax.shard_map(body, mesh=mesh, in_specs=in_specs, out_specs=out_specs, check_vma=False)
```

```python
import functools

import jax
import jax.numpy as jnp
from jax import lax
from jax.experimental import pallas as pl
from jax.experimental.pallas import tpu as pltpu
from jax.sharding import PartitionSpec as P

FRINGE = 8
SWEEPS = 2


OMEGA = 0.8


def padded_2(block, sides, width):
    for axis, dim in sides:
        count = lax.axis_size(axis)
        forward = [(i, i + 1) for i in range(count - 1)]
        backward = [(target, source) for source, target in forward]
        low = lax.ppermute(
            lax.slice_in_dim(block, block.shape[dim] - width, None, axis=dim), axis, forward
        )
        high = lax.ppermute(lax.slice_in_dim(block, 0, width, axis=dim), axis, backward)
        block = jnp.concatenate([low, block, high], axis=dim)
    return block


def restrict_planes(fine_field):
    dims_in = fine_field.shape
    split_cells = fine_field.reshape(dims_in[:-2] + (dims_in[-2] // 2, 2, dims_in[-1] // 2, 2))
    return 0.125 * jnp.sum(split_cells, axis=(-3, -1))


def pair_sum(field, axis):
    which = axis % field.ndim
    length = field.shape[which]
    empty = jnp.zeros_like(lax.slice_in_dim(field, 0, 1, axis=which))
    below_side = jnp.concatenate(
        [empty, lax.slice_in_dim(field, 0, length - 1, axis=which)], axis=which
    )
    above_side = jnp.concatenate(
        [lax.slice_in_dim(field, 1, length, axis=which), empty], axis=which
    )
    return below_side + above_side


def operate(field, padded, diagonal, coupling):
    which = field.ndim - 4
    length = padded.shape[which]
    beside = lax.slice_in_dim(padded, 2, length, axis=which) + lax.slice_in_dim(
        padded, 0, length - 2, axis=which
    )
    beside = beside + pair_sum(field, field.ndim - 2)
    beside = beside + pair_sum(field, field.ndim - 1)
    coupled = jnp.einsum("vw,...wyz->...vyz", coupling, field, precision=lax.Precision.HIGHEST)
    return (6.0 + diagonal) * field - beside + 2.0 * jnp.tanh(coupled)


def apply_operator(field, diagonal, coupling):
    padded = padded_2(field, (("sub", 0),), 1)
    return operate(field, padded, diagonal, coupling)


def corner_values(flat_field, donor_base, height, depth):
    corners = []
    for step_x in (0, 1):
        for step_y in (0, 1):
            for step_z in (0, 1):
                where_cells = donor_base + step_x * height * depth + step_y * depth + step_z
                corners.append(jnp.take_along_axis(flat_field, where_cells[..., None, :], axis=-1))
    return corners


def blend(corners, offsets):
    frac_x = offsets[..., 0:1, :]
    frac_y = offsets[..., 1:2, :]
    frac_z = offsets[..., 2:3, :]
    summed = None
    number = 0
    for step_x in (0, 1):
        for step_y in (0, 1):
            for step_z in (0, 1):
                weight_x = frac_x if step_x else 1.0 - frac_x
                weight_y = frac_y if step_y else 1.0 - frac_y
                weight_z = frac_z if step_z else 1.0 - frac_z
                term = weight_x * weight_y * weight_z * corners[number]
                summed = term if summed is None else summed + term
                number = number + 1
    return summed


def refine(field, axis):
    which = axis % field.ndim
    length = field.shape[which]
    empty = jnp.zeros_like(lax.slice_in_dim(field, 0, 1, axis=which))
    below_side = jnp.concatenate(
        [empty, lax.slice_in_dim(field, 0, length - 1, axis=which)], axis=which
    )
    above_side = jnp.concatenate(
        [lax.slice_in_dim(field, 1, length, axis=which), empty], axis=which
    )
    first_half = 0.75 * field + 0.25 * below_side
    second_half = 0.75 * field + 0.25 * above_side
    joined = jnp.stack([first_half, second_half], axis=which + 1)
    new_dims = list(field.shape)
    new_dims[which] = 2 * length
    return joined.reshape(new_dims)


def shards(
    fine_residual,
    fine_solution,
    plane_of_slot,
    coarse_diagonal,
    coupling,
    donor_cells,
    donor_offsets,
    receptor_cells,
    fringe_counts,
):
    grid_index = lax.axis_index("grid")
    sub_index = lax.axis_index("sub")
    diagonal = coarse_diagonal[0]
    planes, variables, height, depth_cells = diagonal.shape
    cell_count = planes * height * depth_cells
    plane_ids = plane_of_slot[0]
    blocks = plane_ids.shape[0]
    solution_planes = restrict_planes(fine_solution[0])
    residual_planes = restrict_planes(fine_residual[0])
    contrib = jnp.stack([solution_planes, residual_planes], axis=1).reshape(blocks, -1)
    targets = plane_ids // 2
    wanted = sub_index * planes + jnp.arange(planes, dtype=jnp.int32)
    gathered, gathered_ids = (
        lax.all_gather(contrib, "sub", axis=0, tiled=True),
        lax.all_gather(plane_ids, "sub", axis=0, tiled=True),
    )
    select = ((gathered_ids // 2)[None, :] == wanted[:, None]).astype(jnp.float32)
    owned_sums = jnp.dot(
        select, gathered, precision=lax.Precision.HIGHEST, preferred_element_type=jnp.float32
    )
    owned_sums = owned_sums.reshape(planes, 2, variables, height, depth_cells)
    restricted_solution = owned_sums[:, 0]
    restricted_residual = owned_sums[:, 1]
    forcing = apply_operator(restricted_solution, diagonal, coupling) + restricted_residual
    slot_count = donor_cells.shape[-1]
    column = lax.dynamic_index_in_dim(fringe_counts, grid_index, 1, keepdims=False)
    allowed = jnp.repeat(column, FRINGE)
    live_slot = jnp.arange(slot_count, dtype=jnp.int32) % FRINGE < allowed
    target_cells = jnp.where(live_slot, receptor_cells[0, 0], cell_count)
    receptor_mask = jnp.zeros((cell_count,), jnp.float32).at[target_cells].set(1.0, mode="drop")
    receptor_mask = receptor_mask.reshape(planes, 1, height, depth_cells)
    donor_base = donor_cells[0, 0]
    offsets = donor_offsets[0, 0]
    field = restricted_solution
    for sweep_index in range(SWEEPS):
        flat_field = field.transpose(1, 0, 2, 3).reshape(variables, cell_count)
        corners = corner_values(flat_field, donor_base, height, depth_cells)
        arrived = lax.all_to_all(
            blend(corners, offsets), "grid", split_axis=1, concat_axis=1, tiled=True
        )
        flat_field = flat_field.at[:, target_cells].set(arrived, mode="drop")
        field = flat_field.reshape(variables, planes, height, depth_cells).transpose(1, 0, 2, 3)
        update = field + OMEGA * (forcing - apply_operator(field, diagonal, coupling)) / (
            6.0 + diagonal
        )
        field = jnp.where(receptor_mask > 0.5, field, update)
    correction = (field - restricted_solution).reshape(planes, -1)
    neighbour = targets - 1 + 2 * (plane_ids % 2)
    shard_rows = lax.all_gather(correction, "sub", axis=0, tiled=True)
    row_ids = jnp.arange(shard_rows.shape[0], dtype=jnp.int32)
    weights = 0.75 * (targets[:, None] == row_ids[None, :]).astype(jnp.float32)
    weights = weights + 0.25 * (neighbour[:, None] == row_ids[None, :]).astype(jnp.float32)
    along_x = jnp.dot(
        weights, shard_rows, precision=lax.Precision.HIGHEST, preferred_element_type=jnp.float32
    )
    along_x = along_x.reshape(blocks, variables, height, depth_cells)
    prolonged = refine(refine(along_x, -2), -1)
    return (fine_solution[0] + prolonged)[None]


BF16 = jnp.bfloat16
F32 = jnp.float32
HIGHEST = lax.Precision.HIGHEST
VMEM = pl.BlockSpec(memory_space=pltpu.VMEM)
SMEM = pl.BlockSpec(memory_space=pltpu.SMEM)
LANES = 128
ROW = 256
PLANE = 4096
NOWHERE = -(1 << 20)


def pieces(values):
    high = values.astype(BF16).astype(F32)
    middle = (values - high).astype(BF16).astype(F32)
    low = (values - high - middle).astype(BF16).astype(F32)
    return high, middle, low


def dot_exact(values, matrix, contract=(((1,), (0,)), ((), ()))):
    total = None
    for piece in reversed(pieces(values)):
        term = lax.dot_general(piece.astype(BF16), matrix, contract, preferred_element_type=F32)
        total = term if total is None else total + term
    return total


def iota(shape, dim):
    return lax.broadcasted_iota(jnp.int32, shape, dim)


def split_cell(cell, height, depth):
    return cell // (height * depth), cell // depth % height, cell % depth


def neighbour_sum(field):
    total, variables, height, depth = field.shape
    flat = field.reshape(total * variables, height, depth)
    at_row = iota(flat.shape, 1)
    at_column = iota(flat.shape, 2)
    beside = jnp.where(at_row > 0, pltpu.roll(flat, 1, 1), 0.0)
    beside = beside + jnp.where(at_row < height - 1, pltpu.roll(flat, height - 1, 1), 0.0)
    beside = beside + jnp.where(at_column > 0, pltpu.roll(flat, 1, 2), 0.0)
    beside = beside + jnp.where(at_column < depth - 1, pltpu.roll(flat, depth - 1, 2), 0.0)
    beside = beside.reshape(field.shape)
    empty = jnp.zeros((1, variables, height, depth), F32)
    beside = beside + jnp.concatenate([empty, field[: total - 1]], axis=0)
    return beside + jnp.concatenate([field[1:], empty], axis=0)


def live_cells(counts, grid_index, grids, receptors, base):
    lane = iota(receptors.shape, 1)
    allowed = jnp.zeros(receptors.shape, jnp.int32)
    for g in range(grids):
        allowed = jnp.where(lane // FRINGE == g, counts[g, grid_index], allowed)
    return jnp.where(lane % FRINGE < allowed, receptors + base, -1)


def receptor_mask(cell, total, height, depth):
    count = cell.shape[1]
    plane, row, column = split_cell(cell, height, depth)
    onehot = jnp.where(iota((depth, count), 0) == column, 1.0, 0.0).astype(BF16)
    row_here = (iota((height, count), 0) == row) & (cell >= 0)
    here = jnp.concatenate([jnp.where(row_here & (plane == p), 1.0, 0.0) for p in range(total)], 0)
    contract = (((1,), (1,)), ((), ()))
    mask = lax.dot_general(here.astype(BF16), onehot, contract, preferred_element_type=F32)
    return mask.reshape(total, 1, height, depth), here, onehot


def pack_kernel(sizes, counts, diagonal, donors, offsets, receptors, out):
    planes, variables, height, depth = sizes["coarse"]
    slots = sizes["slots"]
    base = lax.axis_index("sub") * (planes * height * depth)
    grid_index = lax.axis_index("grid")
    count = planes * variables
    out[0:count] = diagonal[0].reshape(count, height, depth)
    cell = live_cells(counts, grid_index, sizes["grids"], receptors[0], base)
    out[count] = jnp.zeros((height, depth), F32)
    out[count, 0:1, 0:slots] = (donors[0] + base).astype(F32)
    out[count, 1:4, 0:slots] = offsets[0, 0]
    out[count, 4:5, 0:slots] = cell.astype(F32)


def restrict_kernel(sizes, residual, fine, ids, out, wide):
    planes, variables, height, depth = sizes["coarse"]
    blocks = sizes["blocks"]
    count = blocks * variables
    pair = jnp.where(
        iota((2 * depth, depth), 0) // 2 == iota((2 * depth, depth), 1), 0.125, 0.0
    ).astype(BF16)
    for at, source in ((0, fine), (count, residual)):
        rows = source[0].reshape(count * 2 * height, 2 * depth)
        wide[...] = dot_exact(rows, pair).reshape(count, 2 * height, depth)
        out[at : at + count] = (
            wide[:, pl.ds(0, height, stride=2), :] + wide[:, pl.ds(1, height, stride=2), :]
        )
    out[2 * count] = jnp.zeros((height, depth), F32)
    out[2 * count, 0:1, 0:blocks] = ids[...].astype(F32)


def corner_kernel(sizes, counts, diagonal, donors, offsets, receptors, out):
    planes, variables, height, depth = sizes["coarse"]
    slots, grids = sizes["slots"], sizes["grids"]
    sub_index = lax.axis_index("sub")
    cell = live_cells(counts, lax.axis_index("grid"), grids, receptors[0], 0)
    mask, _, _ = receptor_mask(cell, planes, height, depth)
    gain = OMEGA / (6.0 + diagonal[0])
    fields = jnp.concatenate([gain, 1.0 - mask], axis=1)
    twice = jnp.concatenate([donors[0], donors[0]], axis=1)
    step_z = iota(twice.shape, 1) // slots
    plane, row, column = split_cell(twice, height, depth)
    onehot = jnp.where(iota((depth, LANES), 0) == column + step_z, 1.0, 0.0).astype(BF16)
    count = planes * (variables + 1) * height
    at_column = dot_exact(fields.reshape(count, depth), onehot)
    at_column = at_column.reshape(planes, variables + 1, height, LANES)
    both = jnp.concatenate([offsets[0, 0], offsets[0, 0]], axis=1)
    weight_z = jnp.where(step_z == 1, both[2:3], 1.0 - both[2:3])
    at_row = iota((height, LANES), 0)
    tiles = []
    for step_x in (0, 1):
        weight_x = both[0:1] if step_x else 1.0 - both[0:1]
        by_plane = None
        for p in range(planes):
            term = jnp.where(plane + step_x == p, at_column[p], 0.0)
            by_plane = term if by_plane is None else by_plane + term
        for step_y in (0, 1):
            weight_y = both[1:2] if step_y else 1.0 - both[1:2]
            here = jnp.where(at_row == row + step_y, 1.0, 0.0)
            found = jnp.sum(by_plane * here[None], axis=1)
            weight = weight_x * weight_y * weight_z
            number = (
                (plane + step_x + sub_index * planes) * PLANE
                + (row + step_y) * ROW
                + column
                + step_z
            ).astype(F32)
            scaled = weight * found[:variables] * found[variables : variables + 1]
            tiles.append(jnp.concatenate([weight, weight, scaled, number], axis=0))
    lane = iota((8, LANES), 1)
    sublane = iota((8, LANES), 0)
    target_plane, target_row, target_column = split_cell(cell, height, depth)
    number = (target_plane + sub_index * planes) * PLANE + target_row * ROW + target_column
    number = jnp.where(cell >= 0, number, NOWHERE).astype(F32)
    number = jnp.broadcast_to(jnp.concatenate([number, number], axis=1), (8, LANES))
    half = slots // 2
    moved = jnp.where(sublane == 2, pltpu.roll(number, half, 1), number)
    targets = (sublane == 2) | (sublane == 3)
    targets = targets & (lane >= half) & (lane < slots)
    for h in range(grids):
        tile = jnp.zeros((8, LANES), F32)
        for c in range(8):
            shift = (64 + 8 * c - (c % 2) * 64 - 8 * h) % LANES
            tile = jnp.where(lane // 8 == 8 + c, pltpu.roll(tiles[c // 2], shift, 1), tile)
        weight = pltpu.roll(jnp.broadcast_to(tile[0:1], (8, LANES)), 64, 1)
        tile = jnp.where((sublane == 7) & (lane < 64), weight, tile)
        out[h] = jnp.where(targets, moved, tile)


def hats(shape, dim, start, frac):
    at = iota(shape, dim)
    return jnp.where(at == start, 1.0 - frac, 0.0) + jnp.where(at == start + 1, frac, 0.0)


def interpolate(field, rows):
    total, variables, height, depth = field.shape
    count = rows.shape[1]
    plane, row, column = split_cell(rows[0:1, :].astype(jnp.int32), height, depth)
    frac_x, frac_y, frac_z = rows[1:2, :], rows[2:3, :], rows[3:4, :]
    weight_z = hats((depth, count), 0, column, frac_z)
    weight_y = hats((height, count), 0, row, frac_y)
    along_z = jnp.dot(
        field.reshape(total * variables * height, depth),
        weight_z,
        precision=HIGHEST,
        preferred_element_type=F32,
    ).reshape(total, variables, height, count)
    summed = None
    for p in range(total):
        weight_x = jnp.where(plane == p, 1.0 - frac_x, 0.0) + jnp.where(
            plane + 1 == p, frac_x, 0.0
        )
        term = along_z[p] * (weight_x * weight_y)[None]
        summed = term if summed is None else summed + term
    return jnp.sum(summed, axis=1)


def partial_kernel(sizes, *refs):
    subs, grids, slots, blocks = sizes["subs"], sizes["grids"], sizes["slots"], sizes["blocks"]
    planes, variables, height, depth = sizes["coarse"]
    parts = refs[:subs]
    ids, own, corners = refs[subs : subs + 3]
    out, gain, mask_out, rows, stage, both = refs[subs + 3 :]
    total = subs * planes
    sub_index = lax.axis_index("sub")
    count = planes * variables
    for i, part in enumerate(parts):
        owner = sub_index ^ sizes["order"][i]
        stage[owner] = part[count]
        diagonal = part[0:count].reshape(planes, variables, height, depth)
        gain[pl.ds(owner * planes, planes)] = OMEGA / (6.0 + diagonal)
    for j in range(subs):
        rows[:, j * slots : (j + 1) * slots] = stage[j, :, 0:slots]
    both[...] = jnp.zeros(both.shape, F32)
    fine_count = blocks * variables
    for q in range(blocks):
        coarse = ids[0, q] // 2
        for k in range(2):
            at = k * fine_count + q * variables
            here = pl.ds(k * variables, variables)
            both[pl.ds(coarse, 1), here] += own[at : at + variables][None]
    mask, _, _ = receptor_mask(rows[4:5, :].astype(jnp.int32), total, height, depth)
    mask_out[...] = mask
    restricted = both[:, 0:variables]
    residual = both[:, variables:]
    wet = mask > 0.5
    beside = neighbour_sum(jnp.where(wet, restricted, 0.0))
    swept = jnp.where(wet, 0.0, restricted + gain[...] * (residual - beside))
    values = interpolate(jnp.concatenate([restricted, swept], axis=1), rows)
    first, second = values[:variables], values[variables:]
    top = jnp.concatenate(
        [first[v : v + 1, k * LANES : (k + 1) * LANES] for v in range(4) for k in range(2)], axis=0
    )
    empty = jnp.zeros((1, LANES), F32)
    last = [first[4:5, k * LANES : (k + 1) * LANES] for k in range(2)]
    low = jnp.concatenate(last + [second[:, 0:LANES], empty], axis=0)
    high = jnp.concatenate([empty, empty, second[:, LANES:], empty], axis=0)
    lane = iota((8, LANES), 1)
    sublane = iota((8, LANES), 0)
    values_at = (sublane >= 2) & (sublane < 7)
    for h in range(grids):
        tile = jnp.where(sublane < 2, low, corners[h])
        for s in range(subs):
            source = low if s < 2 else high
            moved = pltpu.roll(source, (8 * s - 8 * h - 64 * (s % 2)) % LANES, 1)
            tile = jnp.where(values_at & (lane // 8 == s), moved, tile)
        for s in range(subs):
            out[h * subs + s, 0:8] = top
            out[h * subs + s, 8:16] = tile


def assemble_kernel(sizes, *refs):
    subs, blocks = sizes["subs"], sizes["blocks"]
    planes, variables, height, depth = sizes["coarse"]
    parts = refs[:subs]
    coupling, restricted, residual, source, numbers, sems = refs[subs:]
    count = blocks * variables
    copies = [
        pltpu.make_async_copy(part.at[2 * count, 0:1, :], numbers.at[i : i + 1, :], sems.at[i])
        for i, part in enumerate(parts)
    ]
    for copy in copies:
        copy.start()
    restricted[...] = jnp.zeros(restricted.shape, F32)
    residual[...] = jnp.zeros(residual.shape, F32)
    for copy in copies:
        copy.wait()
    for i, part in enumerate(parts):
        for q in range(blocks):
            coarse = pl.ds(numbers[i, q].astype(jnp.int32) // 2, 1)
            at = q * variables
            restricted[coarse] += part[at : at + variables][None]
            residual[coarse] += part[count + at : count + at + variables][None]
    source[...] = couple(coupling, restricted[...])


def couple(coupling, field):
    variables = field.shape[1]
    outs = []
    for v in range(variables):
        summed = coupling[v, 0] * field[:, 0]
        for x in range(1, variables):
            summed = summed + coupling[v, x] * field[:, x]
        outs.append(jnp.tanh(summed)[:, None])
    return jnp.concatenate(outs, axis=1)


def fringe_values(sizes, arrived, landing):
    subs, grids = sizes["subs"], sizes["grids"]
    lane = iota((8, LANES), 1)
    sublane = iota((8, LANES), 0)
    group = lane % 64 // 8
    firsts = []
    for g in range(grids):
        top = arrived[g * subs, 0:8]
        last = arrived[g * subs, 8:16]
        for s in range(1, subs):
            top = top + arrived[g * subs + s, 0:8]
            last = last + arrived[g * subs + s, 8:16]
        halves = []
        for k in range(2):
            rows = [top[2 * v + k : 2 * v + k + 1] for v in range(4)] + [last[k : k + 1]]
            halves.append(jnp.concatenate(rows + [jnp.zeros((3, LANES), F32)], axis=0))
        firsts.append((halves, last))
    for g in range(grids):
        for k in range(2):
            sent = jnp.zeros((8, LANES), F32)
            for other in range(grids):
                moved = pltpu.roll(firsts[other][0][k], (8 * other - 8 * g) % LANES, 1)
                sent = jnp.where(group == other, moved, sent)
            landing[g, :, k * LANES : (k + 1) * LANES] = sent
    targets, numbers, scales, weights = [], [], [], []
    for g in range(grids):
        tiles = [arrived[g * subs + s, 8:16] for s in range(subs)]
        target, scale, weight = [], [], []
        for k in range(2):
            one, two = tiles[2 * k], tiles[2 * k + 1]
            scale.append(jnp.where(lane < 64, pltpu.roll(one, 64, 1), two))
            weight.append(jnp.where(lane < 64, one, pltpu.roll(two, 64, 1))[7:8])
            left = jnp.where(lane < 32, pltpu.roll(one, 96, 1)[2:3], one[3:4])
            right = jnp.where(lane < 96, pltpu.roll(two, 32, 1)[2:3], pltpu.roll(two, 64, 1)[3:4])
            target.append(jnp.where(lane < 64, left, right)[0:1])
        targets.append(jnp.concatenate(target, axis=1))
        scales.append(jnp.concatenate(scale, axis=1))
        weights.append(jnp.concatenate(weight, axis=1))
    columns = jnp.concatenate(targets, axis=0).T
    total = [jnp.zeros((8, LANES), F32), jnp.zeros((8, LANES), F32)]
    for g in range(grids):
        apart = jnp.abs(columns[:, g : g + 1] - scales[g][7:8])
        near = (apart == 1.0) | (apart == float(ROW)) | (apart == float(PLANE))
        beside = jnp.where(near, 1.0, 0.0).astype(BF16)
        equal = jnp.where(apart == 0.0, 1.0, 0.0).astype(BF16)
        stacked = jnp.concatenate(pieces(landing[g]), axis=0).astype(BF16)
        by_side = jnp.dot(stacked, beside, preferred_element_type=F32)
        by_self = jnp.dot(stacked, equal, preferred_element_type=F32)
        by_side = by_side[16:24] + by_side[8:16] + by_side[0:8]
        by_self = by_self[16:24] + by_self[8:16] + by_self[0:8]
        for k in range(2):
            here = slice(k * LANES, (k + 1) * LANES)
            scale = pltpu.roll(scales[g][:, here], 6, 0)
            value = by_side[:, here] * scale + by_self[:, here] * weights[g][:, here]
            for step in (32, 16, 8):
                value = value + pltpu.roll(value, LANES - step, 1)
            known = pltpu.roll(firsts[g][1], 6, 0)
            for s in range(2):
                mine = (group == g) & (lane // 64 == s)
                moved = pltpu.roll(value, 8 * g, 1)
                base = pltpu.roll(known, (64 * s + 8 * g - 16 * k - 8 * s) % LANES, 1)
                total[k] = jnp.where(mine, moved + base, total[k])
    return landing[lax.axis_index("grid")], jnp.concatenate(total, axis=1)


def finish_kernel(sizes, *refs):
    subs = sizes["subs"]
    planes, variables, height, depth = sizes["coarse"]
    blocks = sizes["blocks"]
    parts = refs[:subs]
    coupling, ids, arrived, restricted, residual, source, gain, mask = refs[subs : subs + 8]
    fine, out, landing, stage, rows, padded, tall = refs[subs + 8 :]
    total = subs * planes
    slots = sizes["slots"]
    count = blocks * variables
    sub_index = lax.axis_index("sub")
    for i, part in enumerate(parts):
        stage[sub_index ^ sizes["order"][i]] = part[planes * variables]
    for j in range(subs):
        rows[:, j * slots : (j + 1) * slots] = stage[j, :, 0:slots]
    first, second = fringe_values(sizes, arrived, landing)
    cell = rows[4:5, :].astype(jnp.int32)
    _, here, onehot = receptor_mask(cell, total, height, depth)
    lanes = subs * slots
    values = jnp.concatenate([first[:variables], second[:variables]], axis=0)
    stacked = here.reshape(total, 1, height, lanes) * values[None, :, None, :]
    landed = dot_exact(
        stacked.reshape(total * 2 * variables * height, lanes),
        onehot,
        (((1,), (1,)), ((), ())),
    ).reshape(total, 2 * variables, height, depth)
    wet = mask[...] > 0.5
    start = restricted[...]
    scale = gain[...]
    rest = residual[...]
    change = jnp.where(wet, landed[:, :variables] - start, 0.0)
    update = scale * (rest + neighbour_sum(change))
    change = jnp.where(wet, landed[:, variables:] - start, update)
    apart = source[...] - couple(coupling, start + change)
    update = scale * (rest + neighbour_sum(change) + 2.0 * apart)
    correction = jnp.where(wet, change, (1.0 - OMEGA) * change + update)
    padded[0:1] = jnp.zeros((1, variables, height, depth), F32)
    padded[total + 1 : total + 2] = jnp.zeros((1, variables, height, depth), F32)
    padded[1 : total + 1] = correction
    at_row = iota((variables, height, depth), 1)
    for q in range(blocks):
        number = ids[0, q]
        coarse = number // 2
        along = 0.75 * padded[coarse + 1] + 0.25 * padded[coarse + 2 * (number % 2)]
        below = jnp.where(at_row > 0, pltpu.roll(along, 1, 1), 0.0)
        above = jnp.where(at_row < height - 1, pltpu.roll(along, height - 1, 1), 0.0)
        block = slice(q * variables, (q + 1) * variables)
        tall[block, pl.ds(0, height, stride=2), :] = 0.75 * along + 0.25 * below
        tall[block, pl.ds(1, height, stride=2), :] = 0.75 * along + 0.25 * above
    coarse_at = iota((depth, 2 * depth), 0)
    fine_at = iota((depth, 2 * depth), 1)
    beside = fine_at // 2 - 1 + 2 * (fine_at % 2)
    widen = jnp.where(
        coarse_at == fine_at // 2, 0.75, jnp.where(coarse_at == beside, 0.25, 0.0)
    ).astype(BF16)
    prolonged = dot_exact(tall[...].reshape(count * 2 * height, depth), widen)
    out[...] = fine[...] + prolonged.reshape(fine.shape)


def spread_over_sub(block, order_bits):
    held = [block]
    count = lax.axis_size("sub")
    for bit in order_bits:
        pairs = [(i, i ^ bit) for i in range(count)]
        held = held + [lax.ppermute(one, "sub", pairs) for one in held]
    return held


def fast_shards(
    fine_residual,
    fine_solution,
    plane_of_slot,
    coarse_diagonal,
    coupling,
    donor_cells,
    donor_offsets,
    receptor_cells,
    fringe_counts,
):
    subs = lax.axis_size("sub")
    grids = lax.axis_size("grid")
    coarse = coarse_diagonal.shape[1:]
    planes, variables, height, depth = coarse
    blocks = plane_of_slot.shape[1]
    slots = donor_cells.shape[-1]
    bits = [1 << k for k in reversed(range(subs.bit_length() - 1))]
    order = [0]
    for bit in bits:
        order = order + [one ^ bit for one in order]
    sizes = dict(
        coarse=coarse, blocks=blocks, slots=slots, grids=grids, subs=subs, order=tuple(order)
    )
    count = blocks * variables
    total = subs * planes
    whole = (total, variables, height, depth)
    full = jax.ShapeDtypeStruct(whole, F32)
    rows = pltpu.VMEM((8, subs * slots), F32)
    stage = pltpu.VMEM((subs, 8, depth), F32)

    def call(kernel, name, out_shape, scalars, *operands, scratch=()):
        specs = [SMEM if any(one is s for s in scalars) else VMEM for one in operands]
        return pl.pallas_call(
            functools.partial(kernel, sizes),
            out_shape=out_shape,
            in_specs=specs,
            out_specs=jax.tree.map(lambda _: VMEM, out_shape),
            scratch_shapes=list(scratch),
            compiler_params=pltpu.CompilerParams(vmem_limit_bytes=48 * 1024 * 1024),
            name=name,
        )(*operands)

    scalars = (fringe_counts, coupling)
    fringe = (donor_cells, donor_offsets, receptor_cells)
    shared = call(
        pack_kernel,
        "pack",
        jax.ShapeDtypeStruct((planes * variables + 1, height, depth), F32),
        scalars,
        fringe_counts,
        coarse_diagonal,
        *fringe,
    )
    shared = spread_over_sub(shared, bits)
    own = call(
        restrict_kernel,
        "restrict",
        jax.ShapeDtypeStruct((2 * count + 1, height, depth), F32),
        scalars,
        fine_residual,
        fine_solution,
        plane_of_slot,
        scratch=[pltpu.VMEM((count, 2 * height, depth), F32)],
    )
    corners = call(
        corner_kernel,
        "corners",
        jax.ShapeDtypeStruct((grids, 8, LANES), F32),
        scalars,
        fringe_counts,
        coarse_diagonal,
        *fringe,
    )
    every = spread_over_sub(own, bits)
    scalars = scalars + (plane_of_slot,)
    out, gain, mask = call(
        partial_kernel,
        "partial",
        [
            jax.ShapeDtypeStruct((grids * subs, 16, LANES), F32),
            full,
            jax.ShapeDtypeStruct((total, 1, height, depth), F32),
        ],
        scalars,
        *shared,
        plane_of_slot,
        own,
        corners,
        scratch=[rows, stage, pltpu.VMEM((total, 2 * variables, height, depth), F32)],
    )
    arrived = lax.all_to_all(out, ("grid", "sub"), 0, 0, tiled=True)
    restricted, residual, source = call(
        assemble_kernel,
        "assemble",
        [full, full, full],
        scalars,
        *every,
        coupling,
        scratch=[pltpu.SMEM((subs, depth), F32), pltpu.SemaphoreType.DMA((subs,))],
    )
    return call(
        finish_kernel,
        "finish",
        jax.ShapeDtypeStruct(fine_solution.shape, F32),
        scalars,
        *shared,
        coupling,
        plane_of_slot,
        arrived,
        restricted,
        residual,
        source,
        gain,
        mask,
        fine_solution,
        scratch=[
            pltpu.VMEM((grids, 8, subs * slots), F32),
            stage,
            rows,
            pltpu.VMEM((total + 2, variables, height, depth), F32),
            pltpu.VMEM((count, 2 * height, depth), F32),
        ],
    )


def solution(mesh):
    in_specs = (
        P("grid", "sub", None, None, None),
        P("grid", "sub", None, None, None),
        P("grid", "sub"),
        P("grid", "sub", None, None, None),
        P(),
        P("grid", "sub", None),
        P("grid", "sub", None, None),
        P("grid", "sub", None),
        P(),
    )
    out_specs = P("grid", "sub", None, None, None)
    small = mesh.shape["sub"] == 4 and mesh.shape["grid"] * FRINGE == 64
    body = fast_shards if small else shards
    return jax.shard_map(body, mesh=mesh, in_specs=in_specs, out_specs=out_specs, check_vma=False)
```

```python
import functools

import jax
import jax.numpy as jnp
from jax import lax
from jax.experimental import pallas as pl
from jax.experimental.pallas import tpu as pltpu
from jax.sharding import PartitionSpec as P

FRINGE = 8
SWEEPS = 2


OMEGA = 0.8


def padded_2(block, sides, width):
    for axis, dim in sides:
        count = lax.axis_size(axis)
        forward = [(i, i + 1) for i in range(count - 1)]
        backward = [(target, source) for source, target in forward]
        low = lax.ppermute(
            lax.slice_in_dim(block, block.shape[dim] - width, None, axis=dim), axis, forward
        )
        high = lax.ppermute(lax.slice_in_dim(block, 0, width, axis=dim), axis, backward)
        block = jnp.concatenate([low, block, high], axis=dim)
    return block


def restrict_planes(fine_field):
    dims_in = fine_field.shape
    split_cells = fine_field.reshape(dims_in[:-2] + (dims_in[-2] // 2, 2, dims_in[-1] // 2, 2))
    return 0.125 * jnp.sum(split_cells, axis=(-3, -1))


def pair_sum(field, axis):
    which = axis % field.ndim
    length = field.shape[which]
    empty = jnp.zeros_like(lax.slice_in_dim(field, 0, 1, axis=which))
    below_side = jnp.concatenate(
        [empty, lax.slice_in_dim(field, 0, length - 1, axis=which)], axis=which
    )
    above_side = jnp.concatenate(
        [lax.slice_in_dim(field, 1, length, axis=which), empty], axis=which
    )
    return below_side + above_side


def operate(field, padded, diagonal, coupling):
    which = field.ndim - 4
    length = padded.shape[which]
    beside = lax.slice_in_dim(padded, 2, length, axis=which) + lax.slice_in_dim(
        padded, 0, length - 2, axis=which
    )
    beside = beside + pair_sum(field, field.ndim - 2)
    beside = beside + pair_sum(field, field.ndim - 1)
    coupled = jnp.einsum("vw,...wyz->...vyz", coupling, field, precision=lax.Precision.HIGHEST)
    return (6.0 + diagonal) * field - beside + 2.0 * jnp.tanh(coupled)


def apply_operator(field, diagonal, coupling):
    padded = padded_2(field, (("sub", 0),), 1)
    return operate(field, padded, diagonal, coupling)


def corner_values(flat_field, donor_base, height, depth):
    corners = []
    for step_x in (0, 1):
        for step_y in (0, 1):
            for step_z in (0, 1):
                where_cells = donor_base + step_x * height * depth + step_y * depth + step_z
                corners.append(jnp.take_along_axis(flat_field, where_cells[..., None, :], axis=-1))
    return corners


def blend(corners, offsets):
    frac_x = offsets[..., 0:1, :]
    frac_y = offsets[..., 1:2, :]
    frac_z = offsets[..., 2:3, :]
    summed = None
    number = 0
    for step_x in (0, 1):
        for step_y in (0, 1):
            for step_z in (0, 1):
                weight_x = frac_x if step_x else 1.0 - frac_x
                weight_y = frac_y if step_y else 1.0 - frac_y
                weight_z = frac_z if step_z else 1.0 - frac_z
                term = weight_x * weight_y * weight_z * corners[number]
                summed = term if summed is None else summed + term
                number = number + 1
    return summed


def refine(field, axis):
    which = axis % field.ndim
    length = field.shape[which]
    empty = jnp.zeros_like(lax.slice_in_dim(field, 0, 1, axis=which))
    below_side = jnp.concatenate(
        [empty, lax.slice_in_dim(field, 0, length - 1, axis=which)], axis=which
    )
    above_side = jnp.concatenate(
        [lax.slice_in_dim(field, 1, length, axis=which), empty], axis=which
    )
    first_half = 0.75 * field + 0.25 * below_side
    second_half = 0.75 * field + 0.25 * above_side
    joined = jnp.stack([first_half, second_half], axis=which + 1)
    new_dims = list(field.shape)
    new_dims[which] = 2 * length
    return joined.reshape(new_dims)


def shards(
    fine_residual,
    fine_solution,
    plane_of_slot,
    coarse_diagonal,
    coupling,
    donor_cells,
    donor_offsets,
    receptor_cells,
    fringe_counts,
):
    grid_index = lax.axis_index("grid")
    sub_index = lax.axis_index("sub")
    diagonal = coarse_diagonal[0]
    planes, variables, height, depth_cells = diagonal.shape
    cell_count = planes * height * depth_cells
    plane_ids = plane_of_slot[0]
    blocks = plane_ids.shape[0]
    solution_planes = restrict_planes(fine_solution[0])
    residual_planes = restrict_planes(fine_residual[0])
    contrib = jnp.stack([solution_planes, residual_planes], axis=1).reshape(blocks, -1)
    targets = plane_ids // 2
    wanted = sub_index * planes + jnp.arange(planes, dtype=jnp.int32)
    gathered, gathered_ids = (
        lax.all_gather(contrib, "sub", axis=0, tiled=True),
        lax.all_gather(plane_ids, "sub", axis=0, tiled=True),
    )
    select = ((gathered_ids // 2)[None, :] == wanted[:, None]).astype(jnp.float32)
    owned_sums = jnp.dot(
        select, gathered, precision=lax.Precision.HIGHEST, preferred_element_type=jnp.float32
    )
    owned_sums = owned_sums.reshape(planes, 2, variables, height, depth_cells)
    restricted_solution = owned_sums[:, 0]
    restricted_residual = owned_sums[:, 1]
    forcing = apply_operator(restricted_solution, diagonal, coupling) + restricted_residual
    slot_count = donor_cells.shape[-1]
    column = lax.dynamic_index_in_dim(fringe_counts, grid_index, 1, keepdims=False)
    allowed = jnp.repeat(column, FRINGE)
    live_slot = jnp.arange(slot_count, dtype=jnp.int32) % FRINGE < allowed
    target_cells = jnp.where(live_slot, receptor_cells[0, 0], cell_count)
    receptor_mask = jnp.zeros((cell_count,), jnp.float32).at[target_cells].set(1.0, mode="drop")
    receptor_mask = receptor_mask.reshape(planes, 1, height, depth_cells)
    donor_base = donor_cells[0, 0]
    offsets = donor_offsets[0, 0]
    field = restricted_solution
    for sweep_index in range(SWEEPS):
        flat_field = field.transpose(1, 0, 2, 3).reshape(variables, cell_count)
        corners = corner_values(flat_field, donor_base, height, depth_cells)
        arrived = lax.all_to_all(
            blend(corners, offsets), "grid", split_axis=1, concat_axis=1, tiled=True
        )
        flat_field = flat_field.at[:, target_cells].set(arrived, mode="drop")
        field = flat_field.reshape(variables, planes, height, depth_cells).transpose(1, 0, 2, 3)
        update = field + OMEGA * (forcing - apply_operator(field, diagonal, coupling)) / (
            6.0 + diagonal
        )
        field = jnp.where(receptor_mask > 0.5, field, update)
    correction = (field - restricted_solution).reshape(planes, -1)
    neighbour = targets - 1 + 2 * (plane_ids % 2)
    shard_rows = lax.all_gather(correction, "sub", axis=0, tiled=True)
    row_ids = jnp.arange(shard_rows.shape[0], dtype=jnp.int32)
    weights = 0.75 * (targets[:, None] == row_ids[None, :]).astype(jnp.float32)
    weights = weights + 0.25 * (neighbour[:, None] == row_ids[None, :]).astype(jnp.float32)
    along_x = jnp.dot(
        weights, shard_rows, precision=lax.Precision.HIGHEST, preferred_element_type=jnp.float32
    )
    along_x = along_x.reshape(blocks, variables, height, depth_cells)
    prolonged = refine(refine(along_x, -2), -1)
    return (fine_solution[0] + prolonged)[None]


BF16 = jnp.bfloat16
F32 = jnp.float32
HIGHEST = lax.Precision.HIGHEST
VMEM = pl.BlockSpec(memory_space=pltpu.VMEM)
SMEM = pl.BlockSpec(memory_space=pltpu.SMEM)
HBM = pl.BlockSpec(memory_space=pltpu.HBM)
LANES = 128
WET = 1 << 20


def two_pieces(values):
    high = values.astype(BF16)
    return high, (values - high.astype(F32)).astype(BF16)


def dot_exact(values, matrix, contract=(((1,), (0,)), ((), ()))):
    high, low = two_pieces(values)
    total = lax.dot_general(low, matrix, contract, preferred_element_type=F32)
    return total + lax.dot_general(high, matrix, contract, preferred_element_type=F32)


def dot_near(values, matrix):
    high, low = two_pieces(values)
    matrix_high, matrix_low = two_pieces(matrix)
    total = jnp.dot(low, matrix_high, preferred_element_type=F32)
    total = total + jnp.dot(high, matrix_low, preferred_element_type=F32)
    return total + jnp.dot(high, matrix_high, preferred_element_type=F32)


def iota(shape, dim):
    return lax.broadcasted_iota(jnp.int32, shape, dim)


def split_cell(cell, height, depth):
    return cell // (height * depth), cell // depth % height, cell % depth


def neighbour_sum(field):
    total, variables, height, depth = field.shape
    flat = field.reshape(total * variables, height, depth)
    at_row = iota(flat.shape, 1)
    at_column = iota(flat.shape, 2)
    beside = jnp.where(at_row > 0, pltpu.roll(flat, 1, 1), 0.0)
    beside = beside + jnp.where(at_row < height - 1, pltpu.roll(flat, height - 1, 1), 0.0)
    beside = beside + jnp.where(at_column > 0, pltpu.roll(flat, 1, 2), 0.0)
    beside = beside + jnp.where(at_column < depth - 1, pltpu.roll(flat, depth - 1, 2), 0.0)
    beside = beside.reshape(field.shape)
    empty = jnp.zeros((1, variables, height, depth), F32)
    beside = beside + jnp.concatenate([empty, field[: total - 1]], axis=0)
    return beside + jnp.concatenate([field[1:], empty], axis=0)


def live_cells(counts, grid_index, grids, receptors, base):
    lane = iota(receptors.shape, 1)
    allowed = jnp.zeros(receptors.shape, jnp.int32)
    for g in range(grids):
        allowed = jnp.where(lane // FRINGE == g, counts[g, grid_index], allowed)
    return jnp.where(lane % FRINGE < allowed, receptors + base, -1)


def receptor_mask(cell, total, height, depth):
    count = cell.shape[1]
    plane, row, column = split_cell(cell, height, depth)
    onehot = jnp.where(iota((depth, count), 0) == column, 1.0, 0.0).astype(BF16)
    row_here = (iota((height, count), 0) == row) & (cell >= 0)
    here = jnp.concatenate([jnp.where(row_here & (plane == p), 1.0, 0.0) for p in range(total)], 0)
    contract = (((1,), (1,)), ((), ()))
    mask = lax.dot_general(here.astype(BF16), onehot, contract, preferred_element_type=F32)
    return mask.reshape(total, 1, height, depth), here, onehot


def start_copies(pairs, sems):
    copies = [pltpu.make_async_copy(*pair, sems.at[i]) for i, pair in enumerate(pairs)]
    for copy in copies:
        copy.start()
    return copies


def pack_kernel(
    sizes, counts, diagonal, donors, offsets, receptors, out, held, rows, cells, allowed, sems
):
    planes, variables, height, depth = sizes["coarse"]
    slots = sizes["slots"]
    base = lax.axis_index("sub") * (planes * height * depth)
    grid_index = lax.axis_index("grid")
    count = planes * variables
    copies = start_copies(
        [
            (counts, allowed),
            (receptors.at[0], cells.at[0]),
            (donors.at[0], cells.at[1]),
            (offsets.at[0], rows),
            (diagonal.at[0], held),
        ],
        sems,
    )
    out[count] = jnp.zeros((height, depth), F32)
    for copy in copies:
        copy.wait()
    out[0:count] = OMEGA / (6.0 + held[...].reshape(count, height, depth))
    cell = live_cells(allowed, grid_index, sizes["grids"], cells[0], base)
    out[count, 0:1, 0:slots] = (cells[1] + base).astype(F32)
    for k in range(3):
        out[count, k + 1 : k + 2, 0:slots] = rows[k]
    out[count, 4:5, 0:slots] = cell.astype(F32)


def restrict_kernel(sizes, residual, fine, ids, first, second, out, held, wide, sems):
    planes, variables, height, depth = sizes["coarse"]
    blocks = sizes["blocks"]
    step = 8
    copies = start_copies(
        [
            (source.at[0, q : q + step], held.at[k, q : q + step])
            for k, source in enumerate((fine, residual))
            for q in range(0, blocks, step)
        ],
        sems,
    )
    pair = jnp.where(
        iota((2 * depth, depth), 0) // 2 == iota((2 * depth, depth), 1), 0.125, 0.0
    ).astype(BF16)
    count = step * variables
    out[2 * blocks * variables] = jnp.zeros((height, depth), F32)
    out[2 * blocks * variables, 0:1, 0:blocks] = ids[...].astype(F32)
    for i, copy in enumerate(copies):
        k, q = divmod(i * step, blocks)
        copy.wait()
        rows = held[k, q : q + step].reshape(count * 2 * height, 2 * depth)
        here = pl.ds(i * count, count)
        wide[here] = dot_exact(rows, pair).reshape(count, 2 * height, depth)
        out[here] = (
            wide[here, pl.ds(0, height, stride=2), :] + wide[here, pl.ds(1, height, stride=2), :]
        )


def corner_kernel(sizes, shared, out):
    planes, variables, height, depth = sizes["coarse"]
    slots, grids = sizes["slots"], sizes["grids"]
    sub_index = lax.axis_index("sub")
    meta = shared[planes * variables, :, 0:slots]
    base = sub_index * (planes * height * depth)
    cell = meta[4:5].astype(jnp.int32)
    cell = jnp.where(cell >= 0, cell - base, -1)
    mask, _, _ = receptor_mask(cell, planes, height, depth)
    gain = shared[0 : planes * variables].reshape(planes, variables, height, depth)
    fields = jnp.concatenate([gain, mask], axis=1)
    donors = meta[0:1].astype(jnp.int32) - base
    twice = jnp.concatenate([donors, donors], axis=1)
    step_z = iota(twice.shape, 1) // slots
    plane, row, column = split_cell(twice, height, depth)
    onehot = jnp.where(iota((depth, LANES), 0) == column + step_z, 1.0, 0.0).astype(BF16)
    count = planes * (variables + 1) * height
    at_column = dot_exact(fields.reshape(count, depth), onehot)
    at_column = at_column.reshape(planes, variables + 1, height, LANES)
    both = jnp.concatenate([meta[1:4], meta[1:4]], axis=1)
    weight_z = jnp.where(step_z == 1, both[2:3], 1.0 - both[2:3])
    at_row = iota((height, LANES), 0)
    empty = jnp.zeros((1, LANES), F32)
    tiles = []
    for step_x in (0, 1):
        weight_x = both[0:1] if step_x else 1.0 - both[0:1]
        by_plane = None
        for p in range(planes):
            term = jnp.where(plane + step_x == p, at_column[p], 0.0)
            by_plane = term if by_plane is None else by_plane + term
        for step_y in (0, 1):
            weight_y = both[1:2] if step_y else 1.0 - both[1:2]
            here = jnp.where(at_row == row + step_y, 1.0, 0.0)
            found = jnp.sum(by_plane * here[None], axis=1)
            weight = weight_x * weight_y * weight_z
            wet = found[variables : variables + 1]
            scaled = weight * (found[:variables] * (1.0 - wet) + wet)
            number = twice + base + (step_x * height + step_y) * depth + step_z
            number = number.astype(F32) + wet * float(WET)
            tiles.append(jnp.concatenate([empty, empty, scaled, number], axis=0))
    lane = iota((8, LANES), 1)
    sublane = iota((8, LANES), 0)
    number = meta[4:5]
    number = jnp.broadcast_to(jnp.concatenate([number, number], axis=1), (8, LANES))
    half = slots // 2
    moved = jnp.where(sublane == 2, pltpu.roll(number, half, 1), number)
    targets = (sublane == 2) | (sublane == 3)
    targets = targets & (lane >= half) & (lane < slots)
    for h in range(grids):
        tile = jnp.zeros((8, LANES), F32)
        for c in range(8):
            shift = (64 + 8 * c - (c % 2) * 64 - 8 * h) % LANES
            tile = jnp.where(lane // 8 == 8 + c, pltpu.roll(tiles[c // 2], shift, 1), tile)
        out[h] = jnp.where(targets, moved, tile)


def hats(shape, dim, start, frac):
    at = iota(shape, dim)
    return jnp.where(at == start, 1.0 - frac, 0.0) + jnp.where(at == start + 1, frac, 0.0)


def interpolate(field, rows):
    total, variables, height, depth = field.shape
    count = rows.shape[1]
    plane, row, column = split_cell(rows[0:1, :].astype(jnp.int32), height, depth)
    frac_x, frac_y, frac_z = rows[1:2, :], rows[2:3, :], rows[3:4, :]
    weight_z = hats((depth, count), 0, column, frac_z)
    weight_y = hats((height, count), 0, row, frac_y)
    along_z = dot_near(field.reshape(total * variables * height, depth), weight_z)
    along_z = along_z.reshape(total, variables, height, count)
    summed = None
    for p in range(total):
        weight_x = jnp.where(plane == p, 1.0 - frac_x, 0.0) + jnp.where(
            plane + 1 == p, frac_x, 0.0
        )
        term = along_z[p] * (weight_x * weight_y)[None]
        summed = term if summed is None else summed + term
    return jnp.sum(summed, axis=1)


def partial_kernel(sizes, *refs):
    subs, grids, slots, blocks = sizes["subs"], sizes["grids"], sizes["slots"], sizes["blocks"]
    planes, variables, height, depth = sizes["coarse"]
    parts = refs[:subs]
    ids, own, corners = refs[subs : subs + 3]
    out, gain, mask_out, rows, stage, both = refs[subs + 3 :]
    total = subs * planes
    sub_index = lax.axis_index("sub")
    count = planes * variables
    for i, part in enumerate(parts):
        owner = sub_index ^ sizes["order"][i]
        stage[owner] = part[count]
        gain[pl.ds(owner * planes, planes)] = part[0:count].reshape(sizes["coarse"])
    for j in range(subs):
        rows[:, j * slots : (j + 1) * slots] = stage[j, :, 0:slots]
    both[...] = jnp.zeros(both.shape, F32)
    fine_count = blocks * variables
    for q in range(blocks):
        coarse = ids[0, q] // 2
        for k in range(2):
            at = k * fine_count + q * variables
            here = pl.ds(k * variables, variables)
            both[pl.ds(coarse, 1), here] += own[at : at + variables][None]
    mask, _, _ = receptor_mask(rows[4:5, :].astype(jnp.int32), total, height, depth)
    mask_out[...] = mask
    restricted = both[:, 0:variables]
    residual = both[:, variables:]
    wet = mask > 0.5
    beside = neighbour_sum(jnp.where(wet, restricted, 0.0))
    swept = jnp.where(wet, 0.0, restricted + gain[...] * (residual - beside))
    values = interpolate(jnp.concatenate([restricted, swept], axis=1), rows)
    first, second = values[:variables], values[variables:]
    empty = jnp.zeros((1, LANES), F32)
    top = jnp.concatenate([first[:, 0:LANES], first[0:3, LANES:]], axis=0)
    low = jnp.concatenate([first[3:5, LANES:], second[:, 0:LANES], empty], axis=0)
    high = jnp.concatenate([empty, empty, second[:, LANES:], empty], axis=0)
    lane = iota((8, LANES), 1)
    sublane = iota((8, LANES), 0)
    values_at = (sublane >= 2) & (sublane < 7)
    for h in range(grids):
        tile = jnp.where(sublane < 2, low, corners[h])
        for s in range(subs):
            source = low if s < 2 else high
            moved = pltpu.roll(source, (8 * s - 8 * h - 64 * (s % 2)) % LANES, 1)
            tile = jnp.where(values_at & (lane // 8 == s), moved, tile)
        for s in range(subs):
            out[h * subs + s, 0:8] = top
            out[h * subs + s, 8:16] = tile


def assemble_kernel(sizes, *refs):
    subs, blocks = sizes["subs"], sizes["blocks"]
    planes, variables, height, depth = sizes["coarse"]
    parts = refs[:subs]
    coupling, restricted, residual, source, numbers, sems = refs[subs:]
    count = blocks * variables
    copies = [
        pltpu.make_async_copy(part.at[2 * count, 0:1, :], numbers.at[i : i + 1, :], sems.at[i])
        for i, part in enumerate(parts)
    ]
    for copy in copies:
        copy.start()
    restricted[...] = jnp.zeros(restricted.shape, F32)
    residual[...] = jnp.zeros(residual.shape, F32)
    for copy in copies:
        copy.wait()
    for i, part in enumerate(parts):
        for q in range(blocks):
            coarse = pl.ds(numbers[i, q].astype(jnp.int32) // 2, 1)
            at = q * variables
            restricted[coarse] += part[at : at + variables][None]
            residual[coarse] += part[count + at : count + at + variables][None]
    source[...] = couple(coupling, restricted[...])


def couple(coupling, field):
    variables = field.shape[1]
    outs = []
    for v in range(variables):
        summed = coupling[v, 0] * field[:, 0]
        for x in range(1, variables):
            summed = summed + coupling[v, x] * field[:, x]
        outs.append(jnp.tanh(summed)[:, None])
    return jnp.concatenate(outs, axis=1)


def target_features(cell, height, depth):
    plane, row, column = split_cell(jnp.maximum(cell, 0), height, depth)
    square = plane * plane + row * row + column * column
    square = jnp.where(cell >= 0, square, 1 << 15)
    coarse = square // LANES * LANES
    one = jnp.ones(cell.shape, jnp.int32)
    rows = [plane, row, column, one, one, one, -coarse, 2 + coarse - square]
    return jnp.concatenate([each.astype(F32) for each in rows], axis=0)


def corner_features(number, height, depth):
    wet = jnp.where(number >= WET, 1, 0)
    plane, row, column = split_cell(number - WET * wet, height, depth)
    square = plane * plane + row * row + column * column
    coarse = square // LANES * LANES
    one = jnp.ones(number.shape, jnp.int32)
    rows = [2 * plane, 2 * row, 2 * column, -coarse, coarse - square, -wet, one, one]
    return jnp.concatenate([each.astype(F32) for each in rows], axis=0)


def fringe_values(sizes, arrived, landing):
    subs, grids, slots = sizes["subs"], sizes["grids"], sizes["slots"]
    _, _, height, depth = sizes["coarse"]
    lane = iota((8, LANES), 1)
    sublane = iota((8, LANES), 0)
    group = lane % 64 // 8
    firsts = []
    for g in range(grids):
        top = arrived[g * subs, 0:8]
        last = arrived[g * subs, 8:16]
        for s in range(1, subs):
            top = top + arrived[g * subs + s, 0:8]
            last = last + arrived[g * subs + s, 8:16]
        right = jnp.where(sublane < 3, pltpu.roll(top, 3, 0), pltpu.roll(last, 3, 0))
        firsts.append(((top, right), last))
    for g in range(grids):
        for k in range(2):
            sent = jnp.zeros((8, LANES), F32)
            for other in range(grids):
                moved = pltpu.roll(firsts[other][0][k], (8 * other - 8 * g) % LANES, 1)
                sent = jnp.where(group == other, moved, sent)
            landing[g, :, k * LANES : (k + 1) * LANES] = sent
    targets = [jnp.zeros((8, LANES), F32)] * 2
    numbers = [jnp.zeros((8, LANES), F32)] * 2
    scales = []
    for g in range(grids):
        tiles = [arrived[g * subs + s, 8:16] for s in range(subs)]
        scale = []
        for k in range(2):
            one, two = tiles[2 * k], tiles[2 * k + 1]
            scale.append(jnp.where(lane < 64, pltpu.roll(one, 64, 1), two))
            left = jnp.where(lane < 32, pltpu.roll(pltpu.roll(one, 96, 1), 1, 0), one)
            right = pltpu.roll(two, 64, 1)
            right = jnp.where(lane < 96, pltpu.roll(pltpu.roll(two, 32, 1), 1, 0), right)
            target = jnp.where(lane < 64, left, right)
            targets[k] = jnp.where(sublane == g, pltpu.roll(target, (g + 5) % 8, 0), targets[k])
            number = pltpu.roll(scale[k], (g + 1) % 8, 0)
            numbers[k] = jnp.where(sublane == g, number, numbers[k])
        scales.append(scale)
    targets = jnp.concatenate(targets, axis=1).astype(jnp.int32)
    numbers = jnp.concatenate(numbers, axis=1).astype(jnp.int32)
    theirs = target_features(targets, height, depth).T.astype(BF16)
    ours = corner_features(numbers, height, depth)
    which = iota(ours.shape, 0) % 8
    mine = [jnp.where(which == g, ours, 0.0).astype(BF16) for g in range(grids)]
    closeness = jnp.dot(theirs, jnp.concatenate(mine, axis=1), preferred_element_type=F32)
    match = jnp.maximum(closeness.astype(BF16), 0.0)
    lanes = subs * slots
    total = [jnp.zeros((8, LANES), F32), jnp.zeros((8, LANES), F32)]
    for g in range(grids):
        sent = landing[g]
        high = sent.astype(BF16).astype(F32)
        stacked = jnp.concatenate([high, sent - high], axis=0).astype(BF16)
        near = jnp.dot(stacked, match[:, g * lanes : (g + 1) * lanes], preferred_element_type=F32)
        near = near[0:8] + near[8:16]
        known = pltpu.roll(firsts[g][1], 6, 0)
        for k in range(2):
            here = slice(k * LANES, (k + 1) * LANES)
            scale = pltpu.roll(scales[g][k], 6, 0)
            value = near[:, here] * scale
            for step in (32, 16, 8):
                value = value + pltpu.roll(value, LANES - step, 1)
            value = pltpu.roll(value, 8 * g, 1)
            for s in range(2):
                base = pltpu.roll(known, (64 * s + 8 * g - 16 * k - 8 * s) % LANES, 1)
                found = (group == g) & (lane // 64 == s)
                total[k] = jnp.where(found, value + base, total[k])
    return landing[lax.axis_index("grid")], jnp.concatenate(total, axis=1)


def spread(values, cell, total, height, depth):
    count = cell.shape[1]
    pairs = values.shape[0] // 2
    plane, row, column = split_cell(cell, height, depth)
    onehot = jnp.where(iota((depth, count), 0) == column, 1.0, 0.0).astype(BF16)
    row_here = (iota((2 * height, count), 0) % height == row) & (cell >= 0)
    tiles = []
    for i in range(pairs):
        twin = [jnp.broadcast_to(values[2 * i + k : 2 * i + k + 1], (height, count)) for k in (0, 1)]
        tiles.append(two_pieces(jnp.concatenate(twin, axis=0)))
    rows = [[], []]
    for p in range(total):
        here = jnp.where(row_here & (plane == p), 1.0, 0.0).astype(BF16)
        for tile in tiles:
            for k in (0, 1):
                rows[k].append(tile[k] * here)
    contract = (((1,), (1,)), ((), ()))
    high, low = [
        lax.dot_general(
            jnp.concatenate(rows[k], axis=0), onehot, contract, preferred_element_type=F32
        )
        for k in (0, 1)
    ]
    return (high + low).reshape(total, 2 * pairs, height, depth)


def finish_kernel(sizes, *refs):
    subs = sizes["subs"]
    planes, variables, height, depth = sizes["coarse"]
    blocks = sizes["blocks"]
    parts = refs[:subs]
    coupling, ids, arrived, restricted, residual, source, gain, mask = refs[subs : subs + 8]
    fine, out, landing, stage, rows, padded, tall, held, sems = refs[subs + 8 :]
    total = subs * planes
    slots = sizes["slots"]
    count = blocks * variables
    sub_index = lax.axis_index("sub")
    for i, part in enumerate(parts):
        stage[sub_index ^ sizes["order"][i]] = part[planes * variables]
    for j in range(subs):
        rows[:, j * slots : (j + 1) * slots] = stage[j, :, 0:slots]
    first, second = fringe_values(sizes, arrived, landing)
    cell = rows[4:5, :].astype(jnp.int32)
    values = jnp.concatenate([first[:variables], second[:variables]], axis=0)
    landed = spread(values, cell, total, height, depth)
    wet = mask[...] > 0.5
    start = restricted[...]
    scale = gain[...]
    rest = residual[...]
    change = jnp.where(wet, landed[:, :variables] - start, 0.0)
    update = scale * (rest + neighbour_sum(change))
    change = jnp.where(wet, landed[:, variables:] - start, update)
    apart = source[...] - couple(coupling, start + change)
    update = scale * (rest + neighbour_sum(change) + 2.0 * apart)
    correction = jnp.where(wet, change, (1.0 - OMEGA) * change + update)
    padded[0:1] = jnp.zeros((1, variables, height, depth), F32)
    padded[total + 1 : total + 2] = jnp.zeros((1, variables, height, depth), F32)
    padded[1 : total + 1] = correction
    at_row = iota((variables, height, depth), 1)
    coarse_at = iota((depth, 2 * depth), 0)
    fine_at = iota((depth, 2 * depth), 1)
    beside = fine_at // 2 - 1 + 2 * (fine_at % 2)
    widen = jnp.where(
        coarse_at == fine_at // 2, 0.75, jnp.where(coarse_at == beside, 0.25, 0.0)
    ).astype(BF16)
    copies = []
    step = 2
    for q in range(blocks):
        number = ids[0, q]
        coarse = number // 2
        along = 0.75 * padded[coarse + 1] + 0.25 * padded[coarse + 2 * (number % 2)]
        below = jnp.where(at_row > 0, pltpu.roll(along, 1, 1), 0.0)
        above = jnp.where(at_row < height - 1, pltpu.roll(along, height - 1, 1), 0.0)
        block = slice(q * variables, (q + 1) * variables)
        tall[block, pl.ds(0, height, stride=2), :] = 0.75 * along + 0.25 * below
        tall[block, pl.ds(1, height, stride=2), :] = 0.75 * along + 0.25 * above
        if q % step == step - 1:
            low = q + 1 - step
            rows_in = tall[low * variables : (q + 1) * variables]
            prolonged = dot_exact(rows_in.reshape(step * variables * 2 * height, depth), widen)
            shape = (step, variables, 2 * height, 2 * depth)
            held[low : q + 1] = fine[0, low : q + 1] + prolonged.reshape(shape)
            copy = pltpu.make_async_copy(
                held.at[low : q + 1], out.at[0, low : q + 1], sems.at[q // step]
            )
            copy.start()
            copies.append(copy)
    for copy in copies:
        copy.wait()


def spread_over_sub(block, order_bits):
    held = [block]
    count = lax.axis_size("sub")
    for bit in order_bits:
        pairs = [(i, i ^ bit) for i in range(count)]
        held = held + [lax.ppermute(one, "sub", pairs) for one in held]
    return held


def fast_shards(
    fine_residual,
    fine_solution,
    plane_of_slot,
    coarse_diagonal,
    coupling,
    donor_cells,
    donor_offsets,
    receptor_cells,
    fringe_counts,
):
    subs = lax.axis_size("sub")
    grids = lax.axis_size("grid")
    coarse = coarse_diagonal.shape[1:]
    planes, variables, height, depth = coarse
    blocks = plane_of_slot.shape[1]
    slots = donor_cells.shape[-1]
    bits = [1 << k for k in reversed(range(subs.bit_length() - 1))]
    order = [0]
    for bit in bits:
        order = order + [one ^ bit for one in order]
    sizes = dict(
        coarse=coarse, blocks=blocks, slots=slots, grids=grids, subs=subs, order=tuple(order)
    )
    count = blocks * variables
    total = subs * planes
    whole = (total, variables, height, depth)
    full = jax.ShapeDtypeStruct(whole, F32)
    rows = pltpu.VMEM((8, subs * slots), F32)
    stage = pltpu.VMEM((subs, 8, depth), F32)

    def call(kernel, name, out_shape, scalars, *operands, scratch=(), far=(), out_spec=VMEM, aliases={}):
        specs = [
            SMEM if any(one is s for s in scalars) else HBM if any(one is f for f in far) else VMEM
            for one in operands
        ]
        operands = [
            pltpu.with_memory_space_constraint(one, pltpu.HBM) if spec is HBM else one
            for one, spec in zip(operands, specs)
        ]
        return pl.pallas_call(
            functools.partial(kernel, sizes),
            out_shape=out_shape,
            in_specs=specs,
            out_specs=jax.tree.map(lambda _: out_spec, out_shape),
            scratch_shapes=list(scratch),
            input_output_aliases=aliases,
            compiler_params=pltpu.CompilerParams(vmem_limit_bytes=48 * 1024 * 1024),
            name=name,
        )(*operands)

    scalars = (coupling, plane_of_slot)
    offsets = donor_offsets.transpose(0, 2, 1, 3)
    inputs = (fringe_counts, coarse_diagonal, donor_cells, offsets, receptor_cells)
    shared = call(
        pack_kernel,
        "pack",
        jax.ShapeDtypeStruct((planes * variables + 1, height, depth), F32),
        scalars,
        *inputs,
        far=inputs,
        scratch=[
            pltpu.VMEM(coarse, F32),
            pltpu.VMEM(offsets.shape[1:], F32),
            pltpu.VMEM((2, 1, slots), jnp.int32),
            pltpu.SMEM(fringe_counts.shape, jnp.int32),
            pltpu.SemaphoreType.DMA((5,)),
        ],
    )
    mine = shared
    shared = spread_over_sub(shared, bits)
    corners = call(
        corner_kernel,
        "corners",
        jax.ShapeDtypeStruct((grids, 8, LANES), F32),
        scalars,
        mine,
    )
    own = call(
        restrict_kernel,
        "restrict",
        jax.ShapeDtypeStruct((2 * count + 1, height, depth), F32),
        (),
        fine_residual,
        fine_solution,
        plane_of_slot,
        corners,
        shared[2],
        far=(fine_residual, fine_solution),
        scratch=[
            pltpu.VMEM((2,) + fine_solution.shape[1:], F32),
            pltpu.VMEM((2 * count, 2 * height, depth), F32),
            pltpu.SemaphoreType.DMA((blocks,)),
        ],
    )
    every = spread_over_sub(own, bits)
    out, gain, mask = call(
        partial_kernel,
        "partial",
        [
            jax.ShapeDtypeStruct((grids * subs, 16, LANES), F32),
            full,
            jax.ShapeDtypeStruct((total, 1, height, depth), F32),
        ],
        scalars,
        *shared,
        plane_of_slot,
        own,
        corners,
        scratch=[rows, stage, pltpu.VMEM((total, 2 * variables, height, depth), F32)],
    )
    arrived = lax.all_to_all(out, ("grid", "sub"), 0, 0, tiled=True)
    restricted, residual, source = call(
        assemble_kernel,
        "assemble",
        [full, full, full],
        scalars,
        *every,
        coupling,
        scratch=[pltpu.SMEM((subs, depth), F32), pltpu.SemaphoreType.DMA((subs,))],
    )
    return call(
        finish_kernel,
        "finish",
        jax.ShapeDtypeStruct(fine_solution.shape, F32),
        scalars,
        *shared,
        coupling,
        plane_of_slot,
        arrived,
        restricted,
        residual,
        source,
        gain,
        mask,
        fine_solution,
        scratch=[
            pltpu.VMEM((grids, 8, subs * slots), F32),
            stage,
            rows,
            pltpu.VMEM((total + 2, variables, height, depth), F32),
            pltpu.VMEM((count, 2 * height, depth), F32),
            pltpu.VMEM(fine_solution.shape[1:], F32),
            pltpu.SemaphoreType.DMA((blocks // 2,)),
        ],
        out_spec=HBM,
    )


def solution(mesh):
    in_specs = (
        P("grid", "sub", None, None, None),
        P("grid", "sub", None, None, None),
        P("grid", "sub"),
        P("grid", "sub", None, None, None),
        P(),
        P("grid", "sub", None),
        P("grid", "sub", None, None),
        P("grid", "sub", None),
        P(),
    )
    out_specs = P("grid", "sub", None, None, None)
    small = mesh.shape["sub"] == 4 and mesh.shape["grid"] * FRINGE == 64
    body = fast_shards if small else shards
    return jax.shard_map(body, mesh=mesh, in_specs=in_specs, out_specs=out_specs, check_vma=False)
```

```python
import functools

import jax
import jax.numpy as jnp
from jax import lax
from jax.experimental import pallas as pl
from jax.experimental.pallas import tpu as pltpu
from jax.sharding import PartitionSpec as P

FRINGE = 8
SWEEPS = 2


OMEGA = 0.8


def padded_2(block, sides, width):
    for axis, dim in sides:
        count = lax.axis_size(axis)
        forward = [(i, i + 1) for i in range(count - 1)]
        backward = [(target, source) for source, target in forward]
        low = lax.ppermute(
            lax.slice_in_dim(block, block.shape[dim] - width, None, axis=dim), axis, forward
        )
        high = lax.ppermute(lax.slice_in_dim(block, 0, width, axis=dim), axis, backward)
        block = jnp.concatenate([low, block, high], axis=dim)
    return block


def restrict_planes(fine_field):
    dims_in = fine_field.shape
    split_cells = fine_field.reshape(dims_in[:-2] + (dims_in[-2] // 2, 2, dims_in[-1] // 2, 2))
    return 0.125 * jnp.sum(split_cells, axis=(-3, -1))


def pair_sum(field, axis):
    which = axis % field.ndim
    length = field.shape[which]
    empty = jnp.zeros_like(lax.slice_in_dim(field, 0, 1, axis=which))
    below_side = jnp.concatenate(
        [empty, lax.slice_in_dim(field, 0, length - 1, axis=which)], axis=which
    )
    above_side = jnp.concatenate(
        [lax.slice_in_dim(field, 1, length, axis=which), empty], axis=which
    )
    return below_side + above_side


def operate(field, padded, diagonal, coupling):
    which = field.ndim - 4
    length = padded.shape[which]
    beside = lax.slice_in_dim(padded, 2, length, axis=which) + lax.slice_in_dim(
        padded, 0, length - 2, axis=which
    )
    beside = beside + pair_sum(field, field.ndim - 2)
    beside = beside + pair_sum(field, field.ndim - 1)
    coupled = jnp.einsum("vw,...wyz->...vyz", coupling, field, precision=lax.Precision.HIGHEST)
    return (6.0 + diagonal) * field - beside + 2.0 * jnp.tanh(coupled)


def apply_operator(field, diagonal, coupling):
    padded = padded_2(field, (("sub", 0),), 1)
    return operate(field, padded, diagonal, coupling)


def corner_values(flat_field, donor_base, height, depth):
    corners = []
    for step_x in (0, 1):
        for step_y in (0, 1):
            for step_z in (0, 1):
                where_cells = donor_base + step_x * height * depth + step_y * depth + step_z
                corners.append(jnp.take_along_axis(flat_field, where_cells[..., None, :], axis=-1))
    return corners


def blend(corners, offsets):
    frac_x = offsets[..., 0:1, :]
    frac_y = offsets[..., 1:2, :]
    frac_z = offsets[..., 2:3, :]
    summed = None
    number = 0
    for step_x in (0, 1):
        for step_y in (0, 1):
            for step_z in (0, 1):
                weight_x = frac_x if step_x else 1.0 - frac_x
                weight_y = frac_y if step_y else 1.0 - frac_y
                weight_z = frac_z if step_z else 1.0 - frac_z
                term = weight_x * weight_y * weight_z * corners[number]
                summed = term if summed is None else summed + term
                number = number + 1
    return summed


def refine(field, axis):
    which = axis % field.ndim
    length = field.shape[which]
    empty = jnp.zeros_like(lax.slice_in_dim(field, 0, 1, axis=which))
    below_side = jnp.concatenate(
        [empty, lax.slice_in_dim(field, 0, length - 1, axis=which)], axis=which
    )
    above_side = jnp.concatenate(
        [lax.slice_in_dim(field, 1, length, axis=which), empty], axis=which
    )
    first_half = 0.75 * field + 0.25 * below_side
    second_half = 0.75 * field + 0.25 * above_side
    joined = jnp.stack([first_half, second_half], axis=which + 1)
    new_dims = list(field.shape)
    new_dims[which] = 2 * length
    return joined.reshape(new_dims)


def shards(
    fine_residual,
    fine_solution,
    plane_of_slot,
    coarse_diagonal,
    coupling,
    donor_cells,
    donor_offsets,
    receptor_cells,
    fringe_counts,
):
    grid_index = lax.axis_index("grid")
    sub_index = lax.axis_index("sub")
    diagonal = coarse_diagonal[0]
    planes, variables, height, depth_cells = diagonal.shape
    cell_count = planes * height * depth_cells
    plane_ids = plane_of_slot[0]
    blocks = plane_ids.shape[0]
    solution_planes = restrict_planes(fine_solution[0])
    residual_planes = restrict_planes(fine_residual[0])
    contrib = jnp.stack([solution_planes, residual_planes], axis=1).reshape(blocks, -1)
    targets = plane_ids // 2
    wanted = sub_index * planes + jnp.arange(planes, dtype=jnp.int32)
    gathered, gathered_ids = (
        lax.all_gather(contrib, "sub", axis=0, tiled=True),
        lax.all_gather(plane_ids, "sub", axis=0, tiled=True),
    )
    select = ((gathered_ids // 2)[None, :] == wanted[:, None]).astype(jnp.float32)
    owned_sums = jnp.dot(
        select, gathered, precision=lax.Precision.HIGHEST, preferred_element_type=jnp.float32
    )
    owned_sums = owned_sums.reshape(planes, 2, variables, height, depth_cells)
    restricted_solution = owned_sums[:, 0]
    restricted_residual = owned_sums[:, 1]
    forcing = apply_operator(restricted_solution, diagonal, coupling) + restricted_residual
    slot_count = donor_cells.shape[-1]
    column = lax.dynamic_index_in_dim(fringe_counts, grid_index, 1, keepdims=False)
    allowed = jnp.repeat(column, FRINGE)
    live_slot = jnp.arange(slot_count, dtype=jnp.int32) % FRINGE < allowed
    target_cells = jnp.where(live_slot, receptor_cells[0, 0], cell_count)
    receptor_mask = jnp.zeros((cell_count,), jnp.float32).at[target_cells].set(1.0, mode="drop")
    receptor_mask = receptor_mask.reshape(planes, 1, height, depth_cells)
    donor_base = donor_cells[0, 0]
    offsets = donor_offsets[0, 0]
    field = restricted_solution
    for sweep_index in range(SWEEPS):
        flat_field = field.transpose(1, 0, 2, 3).reshape(variables, cell_count)
        corners = corner_values(flat_field, donor_base, height, depth_cells)
        arrived = lax.all_to_all(
            blend(corners, offsets), "grid", split_axis=1, concat_axis=1, tiled=True
        )
        flat_field = flat_field.at[:, target_cells].set(arrived, mode="drop")
        field = flat_field.reshape(variables, planes, height, depth_cells).transpose(1, 0, 2, 3)
        update = field + OMEGA * (forcing - apply_operator(field, diagonal, coupling)) / (
            6.0 + diagonal
        )
        field = jnp.where(receptor_mask > 0.5, field, update)
    correction = (field - restricted_solution).reshape(planes, -1)
    neighbour = targets - 1 + 2 * (plane_ids % 2)
    shard_rows = lax.all_gather(correction, "sub", axis=0, tiled=True)
    row_ids = jnp.arange(shard_rows.shape[0], dtype=jnp.int32)
    weights = 0.75 * (targets[:, None] == row_ids[None, :]).astype(jnp.float32)
    weights = weights + 0.25 * (neighbour[:, None] == row_ids[None, :]).astype(jnp.float32)
    along_x = jnp.dot(
        weights, shard_rows, precision=lax.Precision.HIGHEST, preferred_element_type=jnp.float32
    )
    along_x = along_x.reshape(blocks, variables, height, depth_cells)
    prolonged = refine(refine(along_x, -2), -1)
    return (fine_solution[0] + prolonged)[None]


BF16 = jnp.bfloat16
F32 = jnp.float32
HIGHEST = lax.Precision.HIGHEST
VMEM = pl.BlockSpec(memory_space=pltpu.VMEM)
SMEM = pl.BlockSpec(memory_space=pltpu.SMEM)
HBM = pl.BlockSpec(memory_space=pltpu.HBM)
LANES = 128


def two_pieces(values):
    high = values.astype(BF16)
    return high, (values - high.astype(F32)).astype(BF16)


def dot_exact(values, matrix, contract=(((1,), (0,)), ((), ()))):
    high, low = two_pieces(values)
    total = lax.dot_general(low, matrix, contract, preferred_element_type=F32)
    return total + lax.dot_general(high, matrix, contract, preferred_element_type=F32)


def dot_near(values, matrix):
    high, low = two_pieces(values)
    matrix_high, matrix_low = two_pieces(matrix)
    total = jnp.dot(low, matrix_high, preferred_element_type=F32)
    total = total + jnp.dot(high, matrix_low, preferred_element_type=F32)
    return total + jnp.dot(high, matrix_high, preferred_element_type=F32)


def iota(shape, dim):
    return lax.broadcasted_iota(jnp.int32, shape, dim)


def split_cell(cell, height, depth):
    return cell // (height * depth), cell // depth % height, cell % depth


def neighbour_sum(field):
    total, variables, height, depth = field.shape
    flat = field.reshape(total * variables, height, depth)
    at_row = iota(flat.shape, 1)
    at_column = iota(flat.shape, 2)
    beside = jnp.where(at_row > 0, pltpu.roll(flat, 1, 1), 0.0)
    beside = beside + jnp.where(at_row < height - 1, pltpu.roll(flat, height - 1, 1), 0.0)
    beside = beside + jnp.where(at_column > 0, pltpu.roll(flat, 1, 2), 0.0)
    beside = beside + jnp.where(at_column < depth - 1, pltpu.roll(flat, depth - 1, 2), 0.0)
    beside = beside.reshape(field.shape)
    empty = jnp.zeros((1, variables, height, depth), F32)
    beside = beside + jnp.concatenate([empty, field[: total - 1]], axis=0)
    return beside + jnp.concatenate([field[1:], empty], axis=0)


def live_cells(counts, grid_index, grids, receptors, base):
    lane = iota(receptors.shape, 1)
    allowed = jnp.zeros(receptors.shape, jnp.int32)
    for g in range(grids):
        allowed = jnp.where(lane // FRINGE == g, counts[g, grid_index], allowed)
    return jnp.where(lane % FRINGE < allowed, receptors + base, -1)


def receptor_mask(cell, total, height, depth):
    count = cell.shape[1]
    plane, row, column = split_cell(cell, height, depth)
    onehot = jnp.where(iota((depth, count), 0) == column, 1.0, 0.0).astype(BF16)
    row_here = (iota((height, count), 0) == row) & (cell >= 0)
    here = jnp.concatenate([jnp.where(row_here & (plane == p), 1.0, 0.0) for p in range(total)], 0)
    contract = (((1,), (1,)), ((), ()))
    mask = lax.dot_general(here.astype(BF16), onehot, contract, preferred_element_type=F32)
    return mask.reshape(total, 1, height, depth), here, onehot


def start_copies(pairs, sems):
    copies = [pltpu.make_async_copy(*pair, sems.at[i]) for i, pair in enumerate(pairs)]
    for copy in copies:
        copy.start()
    return copies


def pack_kernel(
    sizes, counts, diagonal, donors, offsets, receptors, out, held, rows, cells, allowed, sems
):
    planes, variables, height, depth = sizes["coarse"]
    slots = sizes["slots"]
    base = lax.axis_index("sub") * (planes * height * depth)
    grid_index = lax.axis_index("grid")
    count = planes * variables
    copies = start_copies(
        [
            (counts, allowed),
            (receptors.at[0], cells.at[0]),
            (donors.at[0], cells.at[1]),
            (offsets.at[0], rows),
            (diagonal.at[0], held),
        ],
        sems,
    )
    out[count] = jnp.zeros((height, depth), F32)
    for copy in copies:
        copy.wait()
    out[0:count] = OMEGA / (6.0 + held[...].reshape(count, height, depth))
    cell = live_cells(allowed, grid_index, sizes["grids"], cells[0], base)
    out[count, 0:1, 0:slots] = (cells[1] + base).astype(F32)
    for k in range(3):
        out[count, k + 1 : k + 2, 0:slots] = rows[k]
    out[count, 4:5, 0:slots] = cell.astype(F32)


def restrict_kernel(sizes, residual, fine, ids, first, second, out, held, wide, sems):
    planes, variables, height, depth = sizes["coarse"]
    blocks = sizes["blocks"]
    step = 8
    copies = start_copies(
        [
            (source.at[0, q : q + step], held.at[k, q : q + step])
            for k, source in enumerate((fine, residual))
            for q in range(0, blocks, step)
        ],
        sems,
    )
    pair = jnp.where(
        iota((2 * depth, depth), 0) // 2 == iota((2 * depth, depth), 1), 0.125, 0.0
    ).astype(BF16)
    count = step * variables
    out[2 * blocks * variables] = jnp.zeros((height, depth), F32)
    out[2 * blocks * variables, 0:1, 0:blocks] = ids[...].astype(F32)
    for i, copy in enumerate(copies):
        k, q = divmod(i * step, blocks)
        copy.wait()
        rows = held[k, q : q + step].reshape(count * 2 * height, 2 * depth)
        here = pl.ds(i * count, count)
        wide[here] = dot_exact(rows, pair).reshape(count, 2 * height, depth)
        out[here] = (
            wide[here, pl.ds(0, height, stride=2), :] + wide[here, pl.ds(1, height, stride=2), :]
        )


def corner_kernel(sizes, shared, out):
    planes, variables, height, depth = sizes["coarse"]
    slots, grids = sizes["slots"], sizes["grids"]
    grid_index = lax.axis_index("grid")
    base = lax.axis_index("sub") * (planes * height * depth)
    meta = shared[planes * variables, :, 0:slots]
    cell = meta[4:5].astype(jnp.int32)
    cell = jnp.where(cell >= 0, cell - base, -1)
    mask, _, _ = receptor_mask(cell, planes, height, depth)
    gain = shared[0 : planes * variables].reshape(planes, variables, height, depth)
    fields = jnp.concatenate([gain, mask], axis=1)
    donors = meta[0:1].astype(jnp.int32) - base
    twice = jnp.concatenate([donors, donors], axis=1)
    step_z = iota(twice.shape, 1) // slots
    plane, row, column = split_cell(twice, height, depth)
    onehot = jnp.where(iota((depth, LANES), 0) == column + step_z, 1.0, 0.0).astype(BF16)
    count = planes * (variables + 1) * height
    at_column = dot_exact(fields.reshape(count, depth), onehot)
    at_column = at_column.reshape(planes, variables + 1, height, LANES)
    both = jnp.concatenate([meta[1:4], meta[1:4]], axis=1)
    weight_z = jnp.where(step_z == 1, both[2:3], 1.0 - both[2:3])
    at_row = iota((height, LANES), 0)
    empty = jnp.zeros((5, LANES), F32)
    tiles = []
    for step_x in (0, 1):
        weight_x = both[0:1] if step_x else 1.0 - both[0:1]
        by_plane = None
        for p in range(planes):
            term = jnp.where(plane + step_x == p, at_column[p], 0.0)
            by_plane = term if by_plane is None else by_plane + term
        for step_y in (0, 1):
            weight_y = both[1:2] if step_y else 1.0 - both[1:2]
            here = jnp.where(at_row == row + step_y, 1.0, 0.0)
            found = jnp.sum(by_plane * here[None], axis=1)
            wet = found[variables : variables + 1]
            scaled = weight_x * weight_y * weight_z * (found[:variables] * (1.0 - wet) + wet)
            left = jnp.concatenate([empty, scaled[0:3]], axis=0)
            right = jnp.concatenate([empty, scaled[3:5], empty[0:1]], axis=0)
            tiles.append((left, right))
    lane = iota((8, LANES), 1)
    sublane = iota((8, LANES), 0)
    cells = jnp.broadcast_to(jnp.concatenate([meta[4:5], meta[4:5]], axis=1), (8, LANES))
    starts = jnp.broadcast_to(jnp.concatenate([meta[0:1], meta[0:1]], axis=1), (8, LANES))
    starts = pltpu.roll(starts, 8 * grid_index, 1)
    last = (sublane == 7) & (lane >= 64)
    mine = last & (lane % 64 // 8 == grid_index)
    for h in range(grids):
        tile = jnp.zeros((8, LANES), F32)
        for c in range(8):
            for k in (0, 1):
                shift = (64 * k + 8 * c - (c % 2) * 64 - 8 * h) % LANES
                moved = pltpu.roll(tiles[c // 2][k], shift, 1)
                tile = jnp.where(lane // 8 == 8 * k + c, moved, tile)
        tile = jnp.where(last, cells, tile)
        out[h] = jnp.where(mine, pltpu.roll(starts, (LANES - 8 * h) % LANES, 1), tile)


def hats(shape, dim, start, frac):
    at = iota(shape, dim)
    return jnp.where(at == start, 1.0 - frac, 0.0) + jnp.where(at == start + 1, frac, 0.0)


def interpolate(field, rows):
    total, variables, height, depth = field.shape
    count = rows.shape[1]
    plane, row, column = split_cell(rows[0:1, :].astype(jnp.int32), height, depth)
    frac_x, frac_y, frac_z = rows[1:2, :], rows[2:3, :], rows[3:4, :]
    weight_z = hats((depth, count), 0, column, frac_z)
    weight_y = hats((height, count), 0, row, frac_y)
    along_z = dot_near(field.reshape(total * variables * height, depth), weight_z)
    along_z = along_z.reshape(total, variables, height, count)
    summed = None
    for p in range(total):
        weight_x = jnp.where(plane == p, 1.0 - frac_x, 0.0) + jnp.where(
            plane + 1 == p, frac_x, 0.0
        )
        term = along_z[p] * (weight_x * weight_y)[None]
        summed = term if summed is None else summed + term
    return jnp.sum(summed, axis=1)


def partial_kernel(sizes, *refs):
    subs, grids, slots, blocks = sizes["subs"], sizes["grids"], sizes["slots"], sizes["blocks"]
    planes, variables, height, depth = sizes["coarse"]
    parts = refs[:subs]
    ids, own, mate, corners = refs[subs : subs + 4]
    out, gain, mask_out, both, rows, stage, numbers, sem = refs[subs + 4 :]
    total = subs * planes
    sub_index = lax.axis_index("sub")
    grid_index = lax.axis_index("grid")
    count = planes * variables
    fine_count = blocks * variables
    copy = pltpu.make_async_copy(mate.at[2 * fine_count, 0:1, :], numbers, sem)
    copy.start()
    for i, part in enumerate(parts):
        owner = sub_index ^ sizes["order"][i]
        stage[owner] = part[count]
        gain[pl.ds(owner * planes, planes)] = part[0:count].reshape(sizes["coarse"])
    for j in range(subs):
        rows[:, j * slots : (j + 1) * slots] = stage[j, :, 0:slots]
    mask, _, _ = receptor_mask(rows[4:5, :].astype(jnp.int32), total, height, depth)
    mask_out[...] = mask
    both[...] = jnp.zeros(both.shape, F32)
    add_planes(sizes, own, ids, both)
    copy.wait()
    add_planes(sizes, mate, numbers, both)
    restricted = both[:, 0:variables]
    residual = both[:, variables:]
    wet = mask > 0.5
    beside = neighbour_sum(jnp.where(wet, restricted, 0.0))
    swept = jnp.where(wet, 0.0, restricted + gain[...] * (residual - beside))
    half = jnp.where(sub_index % 2 == 0, rows[:, 0:LANES], rows[:, LANES:])
    values = interpolate(jnp.concatenate([restricted, swept], axis=1), half)
    empty = jnp.zeros((3, LANES), F32)
    first = jnp.concatenate([values[:variables], empty], axis=0)
    second = jnp.concatenate([values[variables:], empty], axis=0)
    second = pltpu.roll(second, 8 * grid_index, 1)
    mine = iota((8, LANES), 1) % 64 // 8 == grid_index
    top = iota((8, LANES), 0) < variables
    for h in range(grids):
        tile = jnp.where(mine, pltpu.roll(second, (LANES - 8 * h) % LANES, 1), first)
        tile = jnp.where(top, tile, corners[h])
        for s in range(subs):
            out[h * subs + s] = tile


def add_planes(sizes, part, numbers, both):
    variables = sizes["coarse"][1]
    count = sizes["blocks"] * variables
    for q in range(sizes["blocks"]):
        coarse = pl.ds(numbers[0, q].astype(jnp.int32) // 2, 1)
        for k in range(2):
            at = k * count + q * variables
            both[coarse, pl.ds(k * variables, variables)] += part[at : at + variables][None]


def split_kernel(sizes, whole, *pieces):
    at = 0
    for piece in pieces:
        piece[...] = whole[at : at + piece.shape[0]]
        at = at + piece.shape[0]


def assemble_kernel(sizes, known, across, *refs):
    variables = sizes["coarse"][1]
    blocks = sizes["blocks"]
    count = blocks * variables
    pieces = refs[:-5]
    coupling, both, source, numbers, sems = refs[-5:]
    width = pieces[0].shape[0] // variables
    copies = start_copies(
        [
            (across.at[2 * count, 0:1, :], numbers.at[0]),
            (pieces[-1].at[width * variables, 0:1, :], numbers.at[1]),
        ],
        sems,
    )
    both[...] = known[...]
    copies[0].wait()
    add_planes(sizes, across, numbers.at[0], both)
    copies[1].wait()
    for q in range(2 * blocks):
        k, slot = divmod(q, blocks)
        coarse = pl.ds(numbers[1, 0, slot].astype(jnp.int32) // 2, 1)
        at = q % width * variables
        part = pieces[q // width][at : at + variables]
        both[coarse, pl.ds(k * variables, variables)] += part[None]
    source[...] = couple(coupling, both[:, 0:variables])


def couple(coupling, field):
    variables = field.shape[1]
    outs = []
    for v in range(variables):
        summed = coupling[v, 0] * field[:, 0]
        for x in range(1, variables):
            summed = summed + coupling[v, x] * field[:, x]
        outs.append(jnp.tanh(summed)[:, None])
    return jnp.concatenate(outs, axis=1)


def target_features(cell, height, depth):
    plane, row, column = split_cell(jnp.maximum(cell, 0), height, depth)
    square = plane * plane + row * row + column * column
    square = jnp.where(cell >= 0, square, 1 << 15)
    coarse = square // LANES * LANES
    one = jnp.ones(cell.shape, jnp.int32)
    rows = [plane, row, column, one, one, one, -coarse, 2 + coarse - square]
    return jnp.concatenate([each.astype(F32) for each in rows], axis=0)


def corner_features(cell, height, depth):
    plane, row, column = split_cell(cell, height, depth)
    square = plane * plane + row * row + column * column
    coarse = square // LANES * LANES
    one = jnp.ones(cell.shape, jnp.int32)
    rows = [2 * plane, 2 * row, 2 * column, -coarse, coarse - square, 0 * one, one, one]
    return jnp.concatenate([each.astype(F32) for each in rows], axis=0)


def fringe_values(sizes, arrived, landing):
    subs, grids, slots = sizes["subs"], sizes["grids"], sizes["slots"]
    _, _, height, depth = sizes["coarse"]
    lane = iota((8, LANES), 1)
    sublane = iota((8, LANES), 0)
    group = lane % 64 // 8
    firsts = []
    for g in range(grids):
        halves = []
        for k in range(2):
            half = arrived[g * subs + k]
            for s in range(k + 2, subs, 2):
                half = half + arrived[g * subs + s]
            halves.append(half)
        firsts.append(halves)
    for g in range(grids):
        for k in range(2):
            sent = firsts[g][k]
            for other in range(grids):
                if other != g:
                    moved = pltpu.roll(firsts[other][k], (8 * other - 8 * g) % LANES, 1)
                    sent = jnp.where(group == other, moved, sent)
            landing[g, :, k * LANES : (k + 1) * LANES] = sent
    cells = [jnp.zeros((8, LANES), F32)] * 2
    scales = []
    for g in range(grids):
        scale = []
        for k in range(2):
            one, two = arrived[g * subs + 2 * k], arrived[g * subs + 2 * k + 1]
            low = jnp.where(lane < 64, one, pltpu.roll(two, 64, 1))
            high = jnp.where(lane < 64, pltpu.roll(one, 64, 1), two)
            scale.append(jnp.where(sublane < 3, pltpu.roll(low, 3, 0), pltpu.roll(high, 6, 0)))
            cells[k] = jnp.where(sublane == g, pltpu.roll(high, (g + 1) % 8, 0), cells[k])
        scales.append(scale)
    targets, corners = [], []
    step = ((group // 4) * height + group // 2 % 2) * depth + group % 2
    for k in range(2):
        targets.append(jnp.where(group == sublane, -1.0, cells[k]))
        starts = jnp.where(group == sublane, cells[k], 0.0)
        parts = []
        for half in (lane < 64, lane >= 64):
            start = jnp.where(half, starts, 0.0)
            for shift in (64, 32, 16, 8):
                start = start + pltpu.roll(start, shift, 1)
            parts.append(start)
        corners.append(jnp.where(lane < 64, parts[0], parts[1]).astype(jnp.int32) + step)
    targets = jnp.concatenate(targets, axis=1).astype(jnp.int32)
    corners = jnp.concatenate(corners, axis=1)
    theirs = target_features(targets, height, depth).T.astype(BF16)
    ours = corner_features(corners, height, depth)
    which = iota(ours.shape, 0) % 8
    mine = [jnp.where(which == g, ours, 0.0).astype(BF16) for g in range(grids)]
    closeness = jnp.dot(theirs, jnp.concatenate(mine, axis=1), preferred_element_type=F32)
    wet = jnp.maximum(jnp.max(closeness, axis=0, keepdims=True) - 1.0, 0.0)
    match = jnp.maximum(closeness - wet, 0.0).astype(BF16)
    lanes = subs * slots
    total = [jnp.zeros((8, LANES), F32), jnp.zeros((8, LANES), F32)]
    for g in range(grids):
        sent = landing[g]
        high = sent.astype(BF16).astype(F32)
        stacked = jnp.concatenate([high, sent - high], axis=0).astype(BF16)
        near = jnp.dot(stacked, match[:, g * lanes : (g + 1) * lanes], preferred_element_type=F32)
        near = near[0:8] + near[8:16]
        for k in range(2):
            value = near[:, k * LANES : (k + 1) * LANES] * scales[g][k]
            for shift in (32, 16, 8):
                value = value + pltpu.roll(value, LANES - shift, 1)
            value = pltpu.roll(value, 8 * g, 1) + firsts[g][k]
            total[k] = jnp.where(group == g, value, total[k])
    return landing[lax.axis_index("grid")], jnp.concatenate(total, axis=1)


def spread(values, cell, total, height, depth):
    count = cell.shape[1]
    pairs = values.shape[0] // 2
    plane, row, column = split_cell(cell, height, depth)
    onehot = jnp.where(iota((depth, count), 0) == column, 1.0, 0.0).astype(BF16)
    row_here = (iota((2 * height, count), 0) % height == row) & (cell >= 0)
    tiles = []
    for i in range(pairs):
        twin = [jnp.broadcast_to(values[2 * i + k : 2 * i + k + 1], (height, count)) for k in (0, 1)]
        tiles.append(two_pieces(jnp.concatenate(twin, axis=0)))
    rows = [[], []]
    for p in range(total):
        here = jnp.where(row_here & (plane == p), 1.0, 0.0).astype(BF16)
        for tile in tiles:
            for k in (0, 1):
                rows[k].append(tile[k] * here)
    contract = (((1,), (1,)), ((), ()))
    high, low = [
        lax.dot_general(
            jnp.concatenate(rows[k], axis=0), onehot, contract, preferred_element_type=F32
        )
        for k in (0, 1)
    ]
    return (high + low).reshape(total, 2 * pairs, height, depth)


def finish_kernel(sizes, *refs):
    subs = sizes["subs"]
    planes, variables, height, depth = sizes["coarse"]
    blocks = sizes["blocks"]
    slots = sizes["slots"]
    parts = refs[:subs]
    coupling, ids, arrived, both, source, gain, mask, fine = refs[subs : subs + 8]
    out, landing, stage, rows, padded, tall, held, sems = refs[subs + 8 :]
    total = subs * planes
    sub_index = lax.axis_index("sub")
    for i, part in enumerate(parts):
        stage[sub_index ^ sizes["order"][i]] = part[planes * variables]
    for j in range(subs):
        rows[:, j * slots : (j + 1) * slots] = stage[j, :, 0:slots]
    first, second = fringe_values(sizes, arrived, landing)
    cell = rows[4:5, :].astype(jnp.int32)
    values = jnp.concatenate([first[:variables], second[:variables]], axis=0)
    landed = spread(values, cell, total, height, depth)
    wet = mask[...] > 0.5
    start = both[:, 0:variables]
    rest = both[:, variables:]
    scale = gain[...]
    change = jnp.where(wet, landed[:, 0:variables] - start, 0.0)
    update = scale * (rest + neighbour_sum(change))
    change = jnp.where(wet, landed[:, variables:] - start, update)
    apart = source[...] - couple(coupling, start + change)
    update = scale * (rest + neighbour_sum(change) + 2.0 * apart)
    correction = jnp.where(wet, change, (1.0 - OMEGA) * change + update)
    padded[0:1] = jnp.zeros((1, variables, height, depth), F32)
    padded[total + 1 : total + 2] = jnp.zeros((1, variables, height, depth), F32)
    padded[1 : total + 1] = correction
    at_row = iota((variables, height, depth), 1)
    coarse_at = iota((depth, 2 * depth), 0)
    fine_at = iota((depth, 2 * depth), 1)
    beside = fine_at // 2 - 1 + 2 * (fine_at % 2)
    widen = jnp.where(
        coarse_at == fine_at // 2, 0.75, jnp.where(coarse_at == beside, 0.25, 0.0)
    ).astype(BF16)
    copies = []
    step = 2
    for q in range(blocks):
        number = ids[0, q]
        coarse = number // 2
        along = 0.75 * padded[coarse + 1] + 0.25 * padded[coarse + 2 * (number % 2)]
        below = jnp.where(at_row > 0, pltpu.roll(along, 1, 1), 0.0)
        above = jnp.where(at_row < height - 1, pltpu.roll(along, height - 1, 1), 0.0)
        block = slice(q * variables, (q + 1) * variables)
        tall[block, pl.ds(0, height, stride=2), :] = 0.75 * along + 0.25 * below
        tall[block, pl.ds(1, height, stride=2), :] = 0.75 * along + 0.25 * above
        if q % step == step - 1:
            low = q + 1 - step
            rows_in = tall[low * variables : (q + 1) * variables]
            prolonged = dot_exact(rows_in.reshape(step * variables * 2 * height, depth), widen)
            shape = (step, variables, 2 * height, 2 * depth)
            held[low : q + 1] = fine[0, low : q + 1] + prolonged.reshape(shape)
            copy = pltpu.make_async_copy(
                held.at[low : q + 1], out.at[0, low : q + 1], sems.at[q // step]
            )
            copy.start()
            copies.append(copy)
    for copy in copies:
        copy.wait()


def spread_over_sub(block, order_bits):
    held = [block]
    count = lax.axis_size("sub")
    for bit in order_bits:
        pairs = [(i, i ^ bit) for i in range(count)]
        held = held + [lax.ppermute(one, "sub", pairs) for one in held]
    return held


def fast_shards(
    fine_residual,
    fine_solution,
    plane_of_slot,
    coarse_diagonal,
    coupling,
    donor_cells,
    donor_offsets,
    receptor_cells,
    fringe_counts,
):
    subs = lax.axis_size("sub")
    grids = lax.axis_size("grid")
    coarse = coarse_diagonal.shape[1:]
    planes, variables, height, depth = coarse
    blocks = plane_of_slot.shape[1]
    slots = donor_cells.shape[-1]
    bits = [1 << k for k in reversed(range(subs.bit_length() - 1))]
    order = [0]
    for bit in bits:
        order = order + [one ^ bit for one in order]
    sizes = dict(
        coarse=coarse, blocks=blocks, slots=slots, grids=grids, subs=subs, order=tuple(order)
    )
    count = blocks * variables
    total = subs * planes
    whole = (total, variables, height, depth)
    full = jax.ShapeDtypeStruct(whole, F32)
    rows = pltpu.VMEM((8, subs * slots), F32)
    stage = pltpu.VMEM((subs, 8, depth), F32)

    def call(kernel, name, out_shape, scalars, *operands, scratch=(), far=(), out_spec=VMEM, aliases={}):
        specs = [
            SMEM if any(one is s for s in scalars) else HBM if any(one is f for f in far) else VMEM
            for one in operands
        ]
        operands = [
            pltpu.with_memory_space_constraint(one, pltpu.HBM) if spec is HBM else one
            for one, spec in zip(operands, specs)
        ]
        return pl.pallas_call(
            functools.partial(kernel, sizes),
            out_shape=out_shape,
            in_specs=specs,
            out_specs=jax.tree.map(lambda _: out_spec, out_shape),
            scratch_shapes=list(scratch),
            input_output_aliases=aliases,
            compiler_params=pltpu.CompilerParams(vmem_limit_bytes=48 * 1024 * 1024),
            name=name,
        )(*operands)

    scalars = (coupling, plane_of_slot)
    offsets = donor_offsets.transpose(0, 2, 1, 3)
    inputs = (fringe_counts, coarse_diagonal, donor_cells, offsets, receptor_cells)
    shared = call(
        pack_kernel,
        "pack",
        jax.ShapeDtypeStruct((planes * variables + 1, height, depth), F32),
        scalars,
        *inputs,
        far=inputs,
        scratch=[
            pltpu.VMEM(coarse, F32),
            pltpu.VMEM(offsets.shape[1:], F32),
            pltpu.VMEM((2, 1, slots), jnp.int32),
            pltpu.SMEM(fringe_counts.shape, jnp.int32),
            pltpu.SemaphoreType.DMA((5,)),
        ],
    )
    mine = shared
    shared = spread_over_sub(shared, bits)
    corners = call(
        corner_kernel,
        "corners",
        jax.ShapeDtypeStruct((grids, 8, LANES), F32),
        scalars,
        mine,
    )
    own = call(
        restrict_kernel,
        "restrict",
        jax.ShapeDtypeStruct((2 * count + 1, height, depth), F32),
        (),
        fine_residual,
        fine_solution,
        plane_of_slot,
        corners,
        shared[order.index(1)],
        far=(fine_residual, fine_solution),
        scratch=[
            pltpu.VMEM((2,) + fine_solution.shape[1:], F32),
            pltpu.VMEM((2 * count, 2 * height, depth), F32),
            pltpu.SemaphoreType.DMA((blocks,)),
        ],
    )
    own, shared[1] = lax.optimization_barrier((own, shared[1]))
    cores = [(i, i ^ 1) for i in range(subs)]
    mate = lax.ppermute(own, "sub", cores)
    across = lax.ppermute(own, "sub", [(i, i ^ 2) for i in range(subs)])
    out, gain, mask, both = call(
        partial_kernel,
        "partial",
        [
            jax.ShapeDtypeStruct((grids * subs, 8, LANES), F32),
            full,
            jax.ShapeDtypeStruct((total, 1, height, depth), F32),
            jax.ShapeDtypeStruct((total, 2 * variables, height, depth), F32),
        ],
        scalars,
        *shared,
        plane_of_slot,
        own,
        mate,
        corners,
        scratch=[
            rows,
            stage,
            pltpu.SMEM((1, depth), F32),
            pltpu.SemaphoreType.DMA,
        ],
    )
    arrived = lax.all_to_all(out, ("grid", "sub"), 0, 0, tiled=True)
    width = blocks // 2 * variables
    sizes_of = [width, width, width, 2 * count + 1 - 3 * width]
    pieces = call(
        split_kernel,
        "split",
        [jax.ShapeDtypeStruct((each, height, depth), F32) for each in sizes_of],
        (),
        across,
    )
    pieces = [lax.ppermute(piece, "sub", cores) for piece in pieces]
    both, source = call(
        assemble_kernel,
        "assemble",
        [jax.ShapeDtypeStruct(both.shape, F32), full],
        scalars,
        both,
        across,
        *pieces,
        coupling,
        aliases={0: 0},
        scratch=[pltpu.SMEM((2, 1, depth), F32), pltpu.SemaphoreType.DMA((2,))],
    )
    return call(
        finish_kernel,
        "finish",
        jax.ShapeDtypeStruct(fine_solution.shape, F32),
        scalars,
        *shared,
        coupling,
        plane_of_slot,
        arrived,
        both,
        source,
        gain,
        mask,
        fine_solution,
        scratch=[
            pltpu.VMEM((grids, 8, subs * slots), F32),
            stage,
            rows,
            pltpu.VMEM((total + 2, variables, height, depth), F32),
            pltpu.VMEM((count, 2 * height, depth), F32),
            pltpu.VMEM(fine_solution.shape[1:], F32),
            pltpu.SemaphoreType.DMA((blocks // 2,)),
        ],
        out_spec=HBM,
    )


def solution(mesh):
    in_specs = (
        P("grid", "sub", None, None, None),
        P("grid", "sub", None, None, None),
        P("grid", "sub"),
        P("grid", "sub", None, None, None),
        P(),
        P("grid", "sub", None),
        P("grid", "sub", None, None),
        P("grid", "sub", None),
        P(),
    )
    out_specs = P("grid", "sub", None, None, None)
    small = mesh.shape["sub"] == 4 and mesh.shape["grid"] * FRINGE == 64
    body = fast_shards if small else shards
    return jax.shard_map(body, mesh=mesh, in_specs=in_specs, out_specs=out_specs, check_vma=False)
```

```python
import functools

import jax
import jax.numpy as jnp
from jax import lax
from jax.experimental import pallas as pl
from jax.experimental.pallas import tpu as pltpu
from jax.sharding import PartitionSpec as P

FRINGE = 8
SWEEPS = 2


OMEGA = 0.8


def padded_2(block, sides, width):
    for axis, dim in sides:
        count = lax.axis_size(axis)
        forward = [(i, i + 1) for i in range(count - 1)]
        backward = [(target, source) for source, target in forward]
        low = lax.ppermute(
            lax.slice_in_dim(block, block.shape[dim] - width, None, axis=dim), axis, forward
        )
        high = lax.ppermute(lax.slice_in_dim(block, 0, width, axis=dim), axis, backward)
        block = jnp.concatenate([low, block, high], axis=dim)
    return block


def restrict_planes(fine_field):
    dims_in = fine_field.shape
    split_cells = fine_field.reshape(dims_in[:-2] + (dims_in[-2] // 2, 2, dims_in[-1] // 2, 2))
    return 0.125 * jnp.sum(split_cells, axis=(-3, -1))


def pair_sum(field, axis):
    which = axis % field.ndim
    length = field.shape[which]
    empty = jnp.zeros_like(lax.slice_in_dim(field, 0, 1, axis=which))
    below_side = jnp.concatenate(
        [empty, lax.slice_in_dim(field, 0, length - 1, axis=which)], axis=which
    )
    above_side = jnp.concatenate(
        [lax.slice_in_dim(field, 1, length, axis=which), empty], axis=which
    )
    return below_side + above_side


def operate(field, padded, diagonal, coupling):
    which = field.ndim - 4
    length = padded.shape[which]
    beside = lax.slice_in_dim(padded, 2, length, axis=which) + lax.slice_in_dim(
        padded, 0, length - 2, axis=which
    )
    beside = beside + pair_sum(field, field.ndim - 2)
    beside = beside + pair_sum(field, field.ndim - 1)
    coupled = jnp.einsum("vw,...wyz->...vyz", coupling, field, precision=lax.Precision.HIGHEST)
    return (6.0 + diagonal) * field - beside + 2.0 * jnp.tanh(coupled)


def apply_operator(field, diagonal, coupling):
    padded = padded_2(field, (("sub", 0),), 1)
    return operate(field, padded, diagonal, coupling)


def corner_values(flat_field, donor_base, height, depth):
    corners = []
    for step_x in (0, 1):
        for step_y in (0, 1):
            for step_z in (0, 1):
                where_cells = donor_base + step_x * height * depth + step_y * depth + step_z
                corners.append(jnp.take_along_axis(flat_field, where_cells[..., None, :], axis=-1))
    return corners


def blend(corners, offsets):
    frac_x = offsets[..., 0:1, :]
    frac_y = offsets[..., 1:2, :]
    frac_z = offsets[..., 2:3, :]
    summed = None
    number = 0
    for step_x in (0, 1):
        for step_y in (0, 1):
            for step_z in (0, 1):
                weight_x = frac_x if step_x else 1.0 - frac_x
                weight_y = frac_y if step_y else 1.0 - frac_y
                weight_z = frac_z if step_z else 1.0 - frac_z
                term = weight_x * weight_y * weight_z * corners[number]
                summed = term if summed is None else summed + term
                number = number + 1
    return summed


def refine(field, axis):
    which = axis % field.ndim
    length = field.shape[which]
    empty = jnp.zeros_like(lax.slice_in_dim(field, 0, 1, axis=which))
    below_side = jnp.concatenate(
        [empty, lax.slice_in_dim(field, 0, length - 1, axis=which)], axis=which
    )
    above_side = jnp.concatenate(
        [lax.slice_in_dim(field, 1, length, axis=which), empty], axis=which
    )
    first_half = 0.75 * field + 0.25 * below_side
    second_half = 0.75 * field + 0.25 * above_side
    joined = jnp.stack([first_half, second_half], axis=which + 1)
    new_dims = list(field.shape)
    new_dims[which] = 2 * length
    return joined.reshape(new_dims)


def shards(
    fine_residual,
    fine_solution,
    plane_of_slot,
    coarse_diagonal,
    coupling,
    donor_cells,
    donor_offsets,
    receptor_cells,
    fringe_counts,
):
    grid_index = lax.axis_index("grid")
    sub_index = lax.axis_index("sub")
    diagonal = coarse_diagonal[0]
    planes, variables, height, depth_cells = diagonal.shape
    cell_count = planes * height * depth_cells
    plane_ids = plane_of_slot[0]
    blocks = plane_ids.shape[0]
    solution_planes = restrict_planes(fine_solution[0])
    residual_planes = restrict_planes(fine_residual[0])
    contrib = jnp.stack([solution_planes, residual_planes], axis=1).reshape(blocks, -1)
    targets = plane_ids // 2
    wanted = sub_index * planes + jnp.arange(planes, dtype=jnp.int32)
    gathered, gathered_ids = (
        lax.all_gather(contrib, "sub", axis=0, tiled=True),
        lax.all_gather(plane_ids, "sub", axis=0, tiled=True),
    )
    select = ((gathered_ids // 2)[None, :] == wanted[:, None]).astype(jnp.float32)
    owned_sums = jnp.dot(
        select, gathered, precision=lax.Precision.HIGHEST, preferred_element_type=jnp.float32
    )
    owned_sums = owned_sums.reshape(planes, 2, variables, height, depth_cells)
    restricted_solution = owned_sums[:, 0]
    restricted_residual = owned_sums[:, 1]
    forcing = apply_operator(restricted_solution, diagonal, coupling) + restricted_residual
    slot_count = donor_cells.shape[-1]
    column = lax.dynamic_index_in_dim(fringe_counts, grid_index, 1, keepdims=False)
    allowed = jnp.repeat(column, FRINGE)
    live_slot = jnp.arange(slot_count, dtype=jnp.int32) % FRINGE < allowed
    target_cells = jnp.where(live_slot, receptor_cells[0, 0], cell_count)
    receptor_mask = jnp.zeros((cell_count,), jnp.float32).at[target_cells].set(1.0, mode="drop")
    receptor_mask = receptor_mask.reshape(planes, 1, height, depth_cells)
    donor_base = donor_cells[0, 0]
    offsets = donor_offsets[0, 0]
    field = restricted_solution
    for sweep_index in range(SWEEPS):
        flat_field = field.transpose(1, 0, 2, 3).reshape(variables, cell_count)
        corners = corner_values(flat_field, donor_base, height, depth_cells)
        arrived = lax.all_to_all(
            blend(corners, offsets), "grid", split_axis=1, concat_axis=1, tiled=True
        )
        flat_field = flat_field.at[:, target_cells].set(arrived, mode="drop")
        field = flat_field.reshape(variables, planes, height, depth_cells).transpose(1, 0, 2, 3)
        update = field + OMEGA * (forcing - apply_operator(field, diagonal, coupling)) / (
            6.0 + diagonal
        )
        field = jnp.where(receptor_mask > 0.5, field, update)
    correction = (field - restricted_solution).reshape(planes, -1)
    neighbour = targets - 1 + 2 * (plane_ids % 2)
    shard_rows = lax.all_gather(correction, "sub", axis=0, tiled=True)
    row_ids = jnp.arange(shard_rows.shape[0], dtype=jnp.int32)
    weights = 0.75 * (targets[:, None] == row_ids[None, :]).astype(jnp.float32)
    weights = weights + 0.25 * (neighbour[:, None] == row_ids[None, :]).astype(jnp.float32)
    along_x = jnp.dot(
        weights, shard_rows, precision=lax.Precision.HIGHEST, preferred_element_type=jnp.float32
    )
    along_x = along_x.reshape(blocks, variables, height, depth_cells)
    prolonged = refine(refine(along_x, -2), -1)
    return (fine_solution[0] + prolonged)[None]


BF16 = jnp.bfloat16
F32 = jnp.float32
HIGHEST = lax.Precision.HIGHEST
VMEM = pl.BlockSpec(memory_space=pltpu.VMEM)
HBM = pl.BlockSpec(memory_space=pltpu.HBM)
LANES = 128


def two_pieces(values):
    high = values.astype(BF16)
    return high, (values - high.astype(F32)).astype(BF16)


def dot_exact(values, matrix, contract=(((1,), (0,)), ((), ()))):
    high, low = two_pieces(values)
    total = lax.dot_general(low, matrix, contract, preferred_element_type=F32)
    return total + lax.dot_general(high, matrix, contract, preferred_element_type=F32)


def dot_near(values, matrix):
    high, low = two_pieces(values)
    matrix_high, matrix_low = two_pieces(matrix)
    total = jnp.dot(low, matrix_high, preferred_element_type=F32)
    total = total + jnp.dot(high, matrix_low, preferred_element_type=F32)
    return total + jnp.dot(high, matrix_high, preferred_element_type=F32)


def iota(shape, dim):
    return lax.broadcasted_iota(jnp.int32, shape, dim)


def split_cell(cell, height, depth):
    return cell // (height * depth), cell // depth % height, cell % depth


def neighbour_sum(field):
    total, variables, height, depth = field.shape
    flat = field.reshape(total * variables, height, depth)
    at_row = iota(flat.shape, 1)
    at_column = iota(flat.shape, 2)
    beside = jnp.where(at_row > 0, pltpu.roll(flat, 1, 1), 0.0)
    beside = beside + jnp.where(at_row < height - 1, pltpu.roll(flat, height - 1, 1), 0.0)
    beside = beside + jnp.where(at_column > 0, pltpu.roll(flat, 1, 2), 0.0)
    beside = beside + jnp.where(at_column < depth - 1, pltpu.roll(flat, depth - 1, 2), 0.0)
    beside = beside.reshape(field.shape)
    empty = jnp.zeros((1, variables, height, depth), F32)
    beside = beside + jnp.concatenate([empty, field[: total - 1]], axis=0)
    return beside + jnp.concatenate([field[1:], empty], axis=0)


def live_cells(counts, grid_index, grids, receptors, base):
    lane = iota(receptors.shape, 1)
    allowed = jnp.zeros(receptors.shape, jnp.int32)
    for g in range(grids):
        allowed = jnp.where(lane // FRINGE == g, counts[g, grid_index], allowed)
    return jnp.where(lane % FRINGE < allowed, receptors + base, -1)


def receptor_mask(cell, total, height, depth):
    count = cell.shape[1]
    plane, row, column = split_cell(cell, height, depth)
    onehot = jnp.where(iota((depth, count), 0) == column, 1.0, 0.0).astype(BF16)
    row_here = (iota((height, count), 0) == row) & (cell >= 0)
    here = jnp.concatenate([jnp.where(row_here & (plane == p), 1.0, 0.0) for p in range(total)], 0)
    contract = (((1,), (1,)), ((), ()))
    mask = lax.dot_general(here.astype(BF16), onehot, contract, preferred_element_type=F32)
    return mask.reshape(total, 1, height, depth), here, onehot


def start_copies(pairs, sems):
    copies = [pltpu.make_async_copy(*pair, sems.at[i]) for i, pair in enumerate(pairs)]
    for copy in copies:
        copy.start()
    return copies


def pack_kernel(
    sizes, counts, ids, diagonal, donors, offsets, receptors, out, meta, held, rows, cells, planes_of, allowed, sems
):
    planes, variables, height, depth = sizes["coarse"]
    slots = sizes["slots"]
    base = lax.axis_index("sub") * (planes * height * depth)
    grid_index = lax.axis_index("grid")
    count = planes * variables
    copies = start_copies(
        [
            (counts, allowed),
            (receptors.at[0], cells.at[0]),
            (donors.at[0], cells.at[1]),
            (offsets.at[0], rows),
            (ids, planes_of),
            (diagonal.at[0], held),
        ],
        sems,
    )
    out[count] = jnp.zeros((height, depth), F32)
    for copy in copies:
        copy.wait()
    out[0:count] = OMEGA / (6.0 + held[...].reshape(count, height, depth))
    cell = live_cells(allowed, grid_index, sizes["grids"], cells[0], base)
    out[count, 0:1, 0:slots] = (cells[1] + base).astype(F32)
    for k in range(3):
        out[count, k + 1 : k + 2, 0:slots] = rows[k]
    out[count, 4:5, 0:slots] = cell.astype(F32)
    out[count, 5:6, 0 : sizes["blocks"]] = planes_of[...].astype(F32)
    meta[0] = out[count]


def find_corners(sizes, shared, out):
    planes, variables, height, depth = sizes["coarse"]
    slots, grids = sizes["slots"], sizes["grids"]
    grid_index = lax.axis_index("grid")
    base = lax.axis_index("sub") * (planes * height * depth)
    meta = shared[planes * variables, :, 0:slots]
    cell = meta[4:5].astype(jnp.int32)
    cell = jnp.where(cell >= 0, cell - base, -1)
    mask, _, _ = receptor_mask(cell, planes, height, depth)
    gain = shared[0 : planes * variables].reshape(planes, variables, height, depth)
    fields = jnp.concatenate([gain, mask], axis=1)
    donors = meta[0:1].astype(jnp.int32) - base
    twice = jnp.concatenate([donors, donors], axis=1)
    step_z = iota(twice.shape, 1) // slots
    plane, row, column = split_cell(twice, height, depth)
    onehot = jnp.where(iota((depth, LANES), 0) == column + step_z, 1.0, 0.0).astype(BF16)
    count = planes * (variables + 1) * height
    at_column = dot_exact(fields.reshape(count, depth), onehot)
    at_column = at_column.reshape(planes, variables + 1, height, LANES)
    both = jnp.concatenate([meta[1:4], meta[1:4]], axis=1)
    weight_z = jnp.where(step_z == 1, both[2:3], 1.0 - both[2:3])
    at_row = iota((height, LANES), 0)
    empty = jnp.zeros((5, LANES), F32)
    tiles = []
    for step_x in (0, 1):
        weight_x = both[0:1] if step_x else 1.0 - both[0:1]
        by_plane = None
        for p in range(planes):
            term = jnp.where(plane + step_x == p, at_column[p], 0.0)
            by_plane = term if by_plane is None else by_plane + term
        for step_y in (0, 1):
            weight_y = both[1:2] if step_y else 1.0 - both[1:2]
            here = jnp.where(at_row == row + step_y, 1.0, 0.0)
            found = jnp.sum(by_plane * here[None], axis=1)
            wet = found[variables : variables + 1]
            scaled = weight_x * weight_y * weight_z * (found[:variables] * (1.0 - wet) + wet)
            left = jnp.concatenate([empty, scaled[0:3]], axis=0)
            right = jnp.concatenate([empty, scaled[3:5], empty[0:1]], axis=0)
            tiles.append((left, right))
    lane = iota((8, LANES), 1)
    sublane = iota((8, LANES), 0)
    cells = jnp.broadcast_to(jnp.concatenate([meta[4:5], meta[4:5]], axis=1), (8, LANES))
    starts = jnp.broadcast_to(jnp.concatenate([meta[0:1], meta[0:1]], axis=1), (8, LANES))
    starts = pltpu.roll(starts, 8 * grid_index, 1)
    last = (sublane == 7) & (lane >= 64)
    mine = last & (lane % 64 // 8 == grid_index)
    for h in range(grids):
        tile = jnp.zeros((8, LANES), F32)
        for c in range(8):
            for k in (0, 1):
                shift = (64 * k + 8 * c - (c % 2) * 64 - 8 * h) % LANES
                moved = pltpu.roll(tiles[c // 2][k], shift, 1)
                tile = jnp.where(lane // 8 == 8 * k + c, moved, tile)
        tile = jnp.where(last, cells, tile)
        out[h] = jnp.where(mine, pltpu.roll(starts, (LANES - 8 * h) % LANES, 1), tile)


def restrict_kernel(sizes, residual, fine, shared, out, corners, held, wide, sems):
    planes, variables, height, depth = sizes["coarse"]
    blocks = sizes["blocks"]
    step = 8
    copies = start_copies(
        [
            (source.at[0, q : q + step], held.at[k, q : q + step])
            for k, source in enumerate((fine, residual))
            for q in range(0, blocks, step)
        ],
        sems,
    )
    find_corners(sizes, shared, corners)
    pair = jnp.where(
        iota((2 * depth, depth), 0) // 2 == iota((2 * depth, depth), 1), 0.125, 0.0
    ).astype(BF16)
    count = step * variables
    for i, copy in enumerate(copies):
        k, q = divmod(i * step, blocks)
        copy.wait()
        rows = held[k, q : q + step].reshape(count * 2 * height, 2 * depth)
        here = pl.ds(i * count, count)
        wide[here] = dot_exact(rows, pair).reshape(count, 2 * height, depth)
        out[here] = (
            wide[here, pl.ds(0, height, stride=2), :] + wide[here, pl.ds(1, height, stride=2), :]
        )


def hats(shape, dim, start, frac):
    at = iota(shape, dim)
    return jnp.where(at == start, 1.0 - frac, 0.0) + jnp.where(at == start + 1, frac, 0.0)


def interpolate(fields, rows, base):
    planes, variables, height, depth = fields[0].shape
    count = rows.shape[1]
    cell = rows[0:1, :].astype(jnp.int32) - base
    plane, row, column = split_cell(cell, height, depth)
    frac_x, frac_y, frac_z = rows[1:2, :], rows[2:3, :], rows[3:4, :]
    weight_z = hats((depth, count), 0, column, frac_z)
    weight_y = hats((height, count), 0, row, frac_y)
    lower = iota((depth, count), 1) < count // 2
    weight_z = jnp.concatenate(
        [jnp.where(lower, weight_z, 0.0), jnp.where(lower, 0.0, weight_z)], axis=0
    )
    both = jnp.concatenate([each.reshape(-1, depth) for each in fields], axis=1)
    along_z = dot_near(both, weight_z).reshape(planes, variables, height, count)
    summed = None
    for p in range(planes):
        weight_x = jnp.where(plane == p, 1.0 - frac_x, 0.0) + jnp.where(
            plane + 1 == p, frac_x, 0.0
        )
        term = along_z[p] * (weight_x * weight_y)[None]
        summed = term if summed is None else summed + term
    return jnp.sum(summed, axis=1)


def gather_rows(sizes, known, stage, rows):
    slots = sizes["slots"]
    for part, bit in zip(known, (0, 2, 1, 3)):
        stage[lax.axis_index("sub") ^ bit] = part[part.shape[0] - 1]
    for j, s in enumerate((0, 2, 1, 3)):
        rows[:, j * slots : (j + 1) * slots] = stage[s, :, 0:slots]


def partial_kernel(sizes, *refs):
    subs, grids, slots, blocks = sizes["subs"], sizes["grids"], sizes["slots"], sizes["blocks"]
    planes, variables, height, depth = sizes["coarse"]
    known = refs[:subs]
    own, mate, corners = refs[subs:-8]
    out, mask_out, both, rows, stage, pair, padded, wet = refs[-8:]
    total = subs * planes
    sub_index = lax.axis_index("sub")
    grid_index = lax.axis_index("grid")
    count = planes * variables
    gather_rows(sizes, known, stage, rows)
    pair[sub_index // 2] = known[0][...]
    pair[1 - sub_index // 2] = known[1][...]
    mask, _, _ = receptor_mask(rows[4:5, :].astype(jnp.int32), total, height, depth)
    mask_out[...] = mask
    wet[1 : total + 1] = mask
    padded[...] = jnp.zeros(padded.shape, F32)
    inner = padded.at[1 : total + 1]
    add_planes(sizes, [own], plane_numbers(known[0][count], blocks), inner)
    add_planes(sizes, [mate], plane_numbers(known[2][0], blocks), inner)
    both[...] = padded[1 : total + 1]
    core = sub_index % 2
    fields = []
    for k in range(2):
        start = (core + 2 * k) * planes
        here = padded[pl.ds(start, planes + 2)]
        dry = wet[pl.ds(start, planes + 2)] < 0.5
        drowned = jnp.where(dry, 0.0, here[:, 0:variables])
        beside = neighbour_sum(drowned)[1 : planes + 1]
        restricted, residual = here[1 : planes + 1, :variables], here[1 : planes + 1, variables:]
        gain = pair[k, 0:count].reshape(sizes["coarse"])
        swept = jnp.where(dry[1 : planes + 1], restricted + gain * (residual - beside), 0.0)
        fields.append(jnp.concatenate([restricted, swept], axis=1))
    half = jnp.concatenate([pair[0, count, :, 0:slots], pair[1, count, :, 0:slots]], axis=1)
    lane = iota((1, LANES), 1)
    base = (core + 2 * (lane // slots)) * (planes * height * depth)
    values = interpolate(fields, half, base)
    empty = jnp.zeros((3, LANES), F32)
    first = jnp.concatenate([values[:variables], empty], axis=0)
    second = jnp.concatenate([values[variables:], empty], axis=0)
    second = pltpu.roll(second, 8 * grid_index, 1)
    mine = iota((8, LANES), 1) % 64 // 8 == grid_index
    top = iota((8, LANES), 0) < variables
    for h in range(grids):
        tile = jnp.where(mine, pltpu.roll(second, (LANES - 8 * h) % LANES, 1), first)
        tile = jnp.where(top, tile, corners[h])
        for s in range(subs):
            out[h * subs + s] = tile


def plane_numbers(meta, blocks):
    row = meta[5:6, :]
    lane = iota(row.shape, 1)
    return [jnp.sum(jnp.where(lane == q, row, 0.0)).astype(jnp.int32) for q in range(blocks)]


def add_planes(sizes, pieces, numbers, both):
    variables, blocks = sizes["coarse"][1], sizes["blocks"]
    width = pieces[0].shape[0] // variables
    for q in range(blocks):
        coarse = pl.ds(numbers[q] // 2, 1)
        for k in range(2):
            i = k * blocks + q
            at = i % width * variables
            part = pieces[i // width][at : at + variables]
            both[coarse, pl.ds(k * variables, variables)] += part[None]


def split_kernel(sizes, whole, *pieces):
    at = 0
    for piece in pieces:
        piece[...] = whole[at : at + piece.shape[0]]
        at = at + piece.shape[0]


def assemble_kernel(sizes, known, across, shared, partner, beside, last, *refs):
    variables = sizes["coarse"][1]
    pieces = refs[:-4]
    coupling, both, source, gain = refs[-4:]
    planes = sizes["coarse"][0]
    for part, bit in ((shared, 0), (partner, 2), (beside, 1), (last, 3)):
        owner = lax.axis_index("sub") ^ bit
        here = part[0 : planes * variables].reshape(sizes["coarse"])
        gain[pl.ds(owner * planes, planes)] = here
    count = planes * variables
    blocks = sizes["blocks"]
    both[...] = known[...]
    add_planes(sizes, [across], plane_numbers(partner[count], blocks), both)
    add_planes(sizes, pieces, plane_numbers(last[count], blocks), both)
    source[...] = couple(coupling, both[:, 0:variables])


def couple(coupling, field):
    variables = field.shape[1]
    outs = []
    for v in range(variables):
        summed = None
        for x in range(variables):
            term = coupling[v : v + 1, x : x + 1][None] * field[:, x]
            summed = term if summed is None else summed + term
        outs.append(jnp.tanh(summed)[:, None])
    return jnp.concatenate(outs, axis=1)


def target_features(cell, height, depth):
    plane, row, column = split_cell(jnp.maximum(cell, 0), height, depth)
    square = plane * plane + row * row + column * column
    square = jnp.where(cell >= 0, square, 1 << 15)
    coarse = square // LANES * LANES
    one = jnp.ones(cell.shape, jnp.int32)
    rows = [plane, row, column, one, one, one, -coarse, 2 + coarse - square]
    return jnp.concatenate([each.astype(F32) for each in rows], axis=0)


def corner_features(cell, height, depth):
    plane, row, column = split_cell(cell, height, depth)
    square = plane * plane + row * row + column * column
    coarse = square // LANES * LANES
    one = jnp.ones(cell.shape, jnp.int32)
    rows = [2 * plane, 2 * row, 2 * column, -coarse, coarse - square, 0 * one, one, one]
    return jnp.concatenate([each.astype(F32) for each in rows], axis=0)


def fringe_values(sizes, arrived, landing):
    subs, grids, slots = sizes["subs"], sizes["grids"], sizes["slots"]
    _, _, height, depth = sizes["coarse"]
    lane = iota((8, LANES), 1)
    sublane = iota((8, LANES), 0)
    group = lane % 64 // 8
    firsts = []
    for g in range(grids):
        halves = []
        for k in range(2):
            half = arrived[g * subs + k]
            for s in range(k + 2, subs, 2):
                half = half + arrived[g * subs + s]
            halves.append(half)
        firsts.append(halves)
    for g in range(grids):
        for k in range(2):
            sent = firsts[g][k]
            for other in range(grids):
                if other != g:
                    moved = pltpu.roll(firsts[other][k], (8 * other - 8 * g) % LANES, 1)
                    sent = jnp.where(group == other, moved, sent)
            landing[g, :, k * LANES : (k + 1) * LANES] = sent
    cells = [jnp.zeros((8, LANES), F32)] * 2
    scales = []
    for g in range(grids):
        scale = []
        for k in range(2):
            one, two = arrived[g * subs + k], arrived[g * subs + k + 2]
            low = jnp.where(lane < 64, one, pltpu.roll(two, 64, 1))
            high = jnp.where(lane < 64, pltpu.roll(one, 64, 1), two)
            scale.append(jnp.where(sublane < 3, pltpu.roll(low, 3, 0), pltpu.roll(high, 6, 0)))
            cells[k] = jnp.where(sublane == g, pltpu.roll(high, (g + 1) % 8, 0), cells[k])
        scales.append(scale)
    targets, corners = [], []
    step = ((group // 4) * height + group // 2 % 2) * depth + group % 2
    for k in range(2):
        targets.append(jnp.where(group == sublane, -1.0, cells[k]))
        starts = jnp.where(group == sublane, cells[k], 0.0)
        parts = []
        for half in (lane < 64, lane >= 64):
            start = jnp.where(half, starts, 0.0)
            for shift in (64, 32, 16, 8):
                start = start + pltpu.roll(start, shift, 1)
            parts.append(start)
        corners.append(jnp.where(lane < 64, parts[0], parts[1]).astype(jnp.int32) + step)
    targets = jnp.concatenate(targets, axis=1).astype(jnp.int32)
    corners = jnp.concatenate(corners, axis=1)
    theirs = target_features(targets, height, depth).T.astype(BF16)
    ours = corner_features(corners, height, depth)
    which = iota(ours.shape, 0) % 8
    mine = [jnp.where(which == g, ours, 0.0).astype(BF16) for g in range(grids)]
    closeness = jnp.dot(theirs, jnp.concatenate(mine, axis=1), preferred_element_type=F32)
    wet = jnp.maximum(jnp.max(closeness, axis=0, keepdims=True) - 1.0, 0.0)
    match = jnp.maximum(closeness - wet, 0.0).astype(BF16)
    lanes = subs * slots
    total = [jnp.zeros((8, LANES), F32), jnp.zeros((8, LANES), F32)]
    for g in range(grids):
        sent = landing[g]
        high = sent.astype(BF16).astype(F32)
        stacked = jnp.concatenate([high, sent - high], axis=0).astype(BF16)
        near = jnp.dot(stacked, match[:, g * lanes : (g + 1) * lanes], preferred_element_type=F32)
        near = near[0:8] + near[8:16]
        for k in range(2):
            value = near[:, k * LANES : (k + 1) * LANES] * scales[g][k]
            for shift in (32, 16, 8):
                value = value + pltpu.roll(value, LANES - shift, 1)
            value = pltpu.roll(value, 8 * g, 1) + firsts[g][k]
            total[k] = jnp.where(group == g, value, total[k])
    return landing[lax.axis_index("grid")], jnp.concatenate(total, axis=1)


def spread(values, cell, total, height, depth):
    count = cell.shape[1]
    pairs = values.shape[0] // 2
    plane, row, column = split_cell(cell, height, depth)
    onehot = jnp.where(iota((depth, count), 0) == column, 1.0, 0.0).astype(BF16)
    row_here = (iota((2 * height, count), 0) % height == row) & (cell >= 0)
    tiles = []
    for i in range(pairs):
        twin = [jnp.broadcast_to(values[2 * i + k : 2 * i + k + 1], (height, count)) for k in (0, 1)]
        tiles.append(two_pieces(jnp.concatenate(twin, axis=0)))
    rows = [[], []]
    for p in range(total):
        here = jnp.where(row_here & (plane == p), 1.0, 0.0).astype(BF16)
        for tile in tiles:
            for k in (0, 1):
                rows[k].append(tile[k] * here)
    contract = (((1,), (1,)), ((), ()))
    high, low = [
        lax.dot_general(
            jnp.concatenate(rows[k], axis=0), onehot, contract, preferred_element_type=F32
        )
        for k in (0, 1)
    ]
    return (high + low).reshape(total, 2 * pairs, height, depth)


def finish_kernel(sizes, *refs):
    subs = sizes["subs"]
    planes, variables, height, depth = sizes["coarse"]
    blocks = sizes["blocks"]
    parts = refs[:subs]
    coupling, arrived, both, source, gain, mask, fine = refs[subs : subs + 7]
    out, landing, stage, rows, padded, tall, held, sems = refs[subs + 7 :]
    total = subs * planes
    gather_rows(sizes, parts, stage, rows)
    first, second = fringe_values(sizes, arrived, landing)
    cell = rows[4:5, :].astype(jnp.int32)
    values = jnp.concatenate([first[:variables], second[:variables]], axis=0)
    landed = spread(values, cell, total, height, depth)
    wet = mask[...] > 0.5
    start = both[:, 0:variables]
    rest = both[:, variables:]
    scale = gain[...]
    change = jnp.where(wet, landed[:, 0:variables] - start, 0.0)
    update = scale * (rest + neighbour_sum(change))
    change = jnp.where(wet, landed[:, variables:] - start, update)
    apart = source[...] - couple(coupling, start + change)
    update = scale * (rest + neighbour_sum(change) + 2.0 * apart)
    correction = jnp.where(wet, change, (1.0 - OMEGA) * change + update)
    padded[0:1] = jnp.zeros((1, variables, height, depth), F32)
    padded[total + 1 : total + 2] = jnp.zeros((1, variables, height, depth), F32)
    padded[1 : total + 1] = correction
    at_row = iota((variables, height, depth), 1)
    coarse_at = iota((depth, 2 * depth), 0)
    fine_at = iota((depth, 2 * depth), 1)
    beside = fine_at // 2 - 1 + 2 * (fine_at % 2)
    widen = jnp.where(
        coarse_at == fine_at // 2, 0.75, jnp.where(coarse_at == beside, 0.25, 0.0)
    ).astype(BF16)
    copies = []
    step = 2
    numbers = plane_numbers(parts[0][planes * variables], blocks)
    for q, number in enumerate(numbers):
        coarse = number // 2
        along = 0.75 * padded[coarse + 1] + 0.25 * padded[coarse + 2 * (number % 2)]
        below = jnp.where(at_row > 0, pltpu.roll(along, 1, 1), 0.0)
        above = jnp.where(at_row < height - 1, pltpu.roll(along, height - 1, 1), 0.0)
        block = slice(q * variables, (q + 1) * variables)
        tall[block, pl.ds(0, height, stride=2), :] = 0.75 * along + 0.25 * below
        tall[block, pl.ds(1, height, stride=2), :] = 0.75 * along + 0.25 * above
        if q % step == step - 1:
            low = q + 1 - step
            rows_in = tall[low * variables : (q + 1) * variables]
            prolonged = dot_exact(rows_in.reshape(step * variables * 2 * height, depth), widen)
            shape = (step, variables, 2 * height, 2 * depth)
            held[low : q + 1] = fine[0, low : q + 1] + prolonged.reshape(shape)
            copy = pltpu.make_async_copy(
                held.at[low : q + 1], out.at[0, low : q + 1], sems.at[q // step]
            )
            copy.start()
            copies.append(copy)
    for copy in copies:
        copy.wait()


def fast_shards(
    fine_residual,
    fine_solution,
    plane_of_slot,
    coarse_diagonal,
    coupling,
    donor_cells,
    donor_offsets,
    receptor_cells,
    fringe_counts,
):
    subs = lax.axis_size("sub")
    grids = lax.axis_size("grid")
    coarse = coarse_diagonal.shape[1:]
    planes, variables, height, depth = coarse
    blocks = plane_of_slot.shape[1]
    slots = donor_cells.shape[-1]
    sizes = dict(coarse=coarse, blocks=blocks, slots=slots, grids=grids, subs=subs)
    count = blocks * variables
    total = subs * planes
    whole = (total, variables, height, depth)
    full = jax.ShapeDtypeStruct(whole, F32)
    rows = pltpu.VMEM((8, subs * slots), F32)
    stage = pltpu.VMEM((subs, 8, depth), F32)

    def call(kernel, name, out_shape, *operands, scratch=(), far=(), out_spec=VMEM, aliases={}):
        specs = [HBM if any(one is each for each in far) else VMEM for one in operands]
        operands = [
            pltpu.with_memory_space_constraint(one, pltpu.HBM) if spec is HBM else one
            for one, spec in zip(operands, specs)
        ]
        return pl.pallas_call(
            functools.partial(kernel, sizes),
            out_shape=out_shape,
            in_specs=specs,
            out_specs=jax.tree.map(lambda _: out_spec, out_shape),
            scratch_shapes=list(scratch),
            input_output_aliases=aliases,
            compiler_params=pltpu.CompilerParams(vmem_limit_bytes=48 * 1024 * 1024),
            name=name,
        )(*operands)

    offsets = donor_offsets.transpose(0, 2, 1, 3)
    inputs = (fringe_counts, plane_of_slot, coarse_diagonal, donor_cells, offsets, receptor_cells)
    shared, meta = call(
        pack_kernel,
        "pack",
        [
            jax.ShapeDtypeStruct((planes * variables + 1, height, depth), F32),
            jax.ShapeDtypeStruct((1, height, depth), F32),
        ],
        *inputs,
        far=inputs,
        scratch=[
            pltpu.VMEM(coarse, F32),
            pltpu.VMEM(offsets.shape[1:], F32),
            pltpu.VMEM((2, 1, slots), jnp.int32),
            pltpu.VMEM(plane_of_slot.shape, jnp.int32),
            pltpu.SMEM(fringe_counts.shape, jnp.int32),
            pltpu.SemaphoreType.DMA((6,)),
        ],
    )
    swap = {bit: [(i, i ^ bit) for i in range(subs)] for bit in (1, 2)}
    partner = lax.ppermute(shared, "sub", swap[2])
    beside = lax.ppermute(meta, "sub", swap[1])
    own, corners = call(
        restrict_kernel,
        "restrict",
        [
            jax.ShapeDtypeStruct((2 * count, height, depth), F32),
            jax.ShapeDtypeStruct((grids, 8, LANES), F32),
        ],
        fine_residual,
        fine_solution,
        shared,
        far=(fine_residual, fine_solution),
        scratch=[
            pltpu.VMEM((2,) + fine_solution.shape[1:], F32),
            pltpu.VMEM((2 * count, 2 * height, depth), F32),
            pltpu.SemaphoreType.DMA((blocks,)),
        ],
    )
    own, partner, beside = lax.optimization_barrier((own, partner, beside))
    mate = lax.ppermute(own, "sub", swap[1])
    known = (shared, partner, beside, lax.ppermute(partner, "sub", swap[1]))
    across = lax.ppermute(own, "sub", swap[2])
    out, mask, both = call(
        partial_kernel,
        "partial",
        [
            jax.ShapeDtypeStruct((grids * subs, 8, LANES), F32),
            jax.ShapeDtypeStruct((total, 1, height, depth), F32),
            jax.ShapeDtypeStruct((total, 2 * variables, height, depth), F32),
        ],
        *known,
        own,
        mate,
        corners,
        scratch=[
            rows,
            stage,
            pltpu.VMEM((2, planes * variables + 1, height, depth), F32),
            pltpu.VMEM((total + 2, 2 * variables, height, depth), F32),
            pltpu.VMEM((total + 2, 1, height, depth), F32),
        ],
    )
    arrived = lax.all_to_all(out, ("grid", "sub"), 0, 0, tiled=True)
    piece = jax.ShapeDtypeStruct((blocks // 2 * variables, height, depth), F32)
    pieces = call(split_kernel, "split", [piece] * 4, across)
    pieces = [lax.ppermute(each, "sub", swap[1]) for each in pieces]
    beside_gain = lax.ppermute(shared, "sub", swap[1])
    both, source, gain = call(
        assemble_kernel,
        "assemble",
        [jax.ShapeDtypeStruct(both.shape, F32), full, full],
        both,
        across,
        shared,
        partner,
        beside_gain,
        known[3],
        *pieces,
        coupling,
        aliases={0: 0},
    )
    return call(
        finish_kernel,
        "finish",
        jax.ShapeDtypeStruct(fine_solution.shape, F32),
        *known,
        coupling,
        arrived,
        both,
        source,
        gain,
        mask,
        fine_solution,
        scratch=[
            pltpu.VMEM((grids, 8, subs * slots), F32),
            stage,
            rows,
            pltpu.VMEM((total + 2, variables, height, depth), F32),
            pltpu.VMEM((count, 2 * height, depth), F32),
            pltpu.VMEM(fine_solution.shape[1:], F32),
            pltpu.SemaphoreType.DMA((blocks // 2,)),
        ],
        out_spec=HBM,
    )


def solution(mesh):
    in_specs = (
        P("grid", "sub", None, None, None),
        P("grid", "sub", None, None, None),
        P("grid", "sub"),
        P("grid", "sub", None, None, None),
        P(),
        P("grid", "sub", None),
        P("grid", "sub", None, None),
        P("grid", "sub", None),
        P(),
    )
    out_specs = P("grid", "sub", None, None, None)
    small = mesh.shape["sub"] == 4 and mesh.shape["grid"] * FRINGE == 64
    body = fast_shards if small else shards
    return jax.shard_map(body, mesh=mesh, in_specs=in_specs, out_specs=out_specs, check_vma=False)
```

```python
import functools

import jax
import jax.numpy as jnp
from jax import lax
from jax.experimental import pallas as pl
from jax.experimental.pallas import tpu as pltpu
from jax.sharding import PartitionSpec as P

FRINGE = 8
SWEEPS = 2


OMEGA = 0.8


def padded_2(block, sides, width):
    for axis, dim in sides:
        count = lax.axis_size(axis)
        forward = [(i, i + 1) for i in range(count - 1)]
        backward = [(target, source) for source, target in forward]
        low = lax.ppermute(
            lax.slice_in_dim(block, block.shape[dim] - width, None, axis=dim), axis, forward
        )
        high = lax.ppermute(lax.slice_in_dim(block, 0, width, axis=dim), axis, backward)
        block = jnp.concatenate([low, block, high], axis=dim)
    return block


def restrict_planes(fine_field):
    dims_in = fine_field.shape
    split_cells = fine_field.reshape(dims_in[:-2] + (dims_in[-2] // 2, 2, dims_in[-1] // 2, 2))
    return 0.125 * jnp.sum(split_cells, axis=(-3, -1))


def pair_sum(field, axis):
    which = axis % field.ndim
    length = field.shape[which]
    empty = jnp.zeros_like(lax.slice_in_dim(field, 0, 1, axis=which))
    below_side = jnp.concatenate(
        [empty, lax.slice_in_dim(field, 0, length - 1, axis=which)], axis=which
    )
    above_side = jnp.concatenate(
        [lax.slice_in_dim(field, 1, length, axis=which), empty], axis=which
    )
    return below_side + above_side


def operate(field, padded, diagonal, coupling):
    which = field.ndim - 4
    length = padded.shape[which]
    beside = lax.slice_in_dim(padded, 2, length, axis=which) + lax.slice_in_dim(
        padded, 0, length - 2, axis=which
    )
    beside = beside + pair_sum(field, field.ndim - 2)
    beside = beside + pair_sum(field, field.ndim - 1)
    coupled = jnp.einsum("vw,...wyz->...vyz", coupling, field, precision=lax.Precision.HIGHEST)
    return (6.0 + diagonal) * field - beside + 2.0 * jnp.tanh(coupled)


def apply_operator(field, diagonal, coupling):
    padded = padded_2(field, (("sub", 0),), 1)
    return operate(field, padded, diagonal, coupling)


def corner_values(flat_field, donor_base, height, depth):
    corners = []
    for step_x in (0, 1):
        for step_y in (0, 1):
            for step_z in (0, 1):
                where_cells = donor_base + step_x * height * depth + step_y * depth + step_z
                corners.append(jnp.take_along_axis(flat_field, where_cells[..., None, :], axis=-1))
    return corners


def blend(corners, offsets):
    frac_x = offsets[..., 0:1, :]
    frac_y = offsets[..., 1:2, :]
    frac_z = offsets[..., 2:3, :]
    summed = None
    number = 0
    for step_x in (0, 1):
        for step_y in (0, 1):
            for step_z in (0, 1):
                weight_x = frac_x if step_x else 1.0 - frac_x
                weight_y = frac_y if step_y else 1.0 - frac_y
                weight_z = frac_z if step_z else 1.0 - frac_z
                term = weight_x * weight_y * weight_z * corners[number]
                summed = term if summed is None else summed + term
                number = number + 1
    return summed


def refine(field, axis):
    which = axis % field.ndim
    length = field.shape[which]
    empty = jnp.zeros_like(lax.slice_in_dim(field, 0, 1, axis=which))
    below_side = jnp.concatenate(
        [empty, lax.slice_in_dim(field, 0, length - 1, axis=which)], axis=which
    )
    above_side = jnp.concatenate(
        [lax.slice_in_dim(field, 1, length, axis=which), empty], axis=which
    )
    first_half = 0.75 * field + 0.25 * below_side
    second_half = 0.75 * field + 0.25 * above_side
    joined = jnp.stack([first_half, second_half], axis=which + 1)
    new_dims = list(field.shape)
    new_dims[which] = 2 * length
    return joined.reshape(new_dims)


def shards(
    fine_residual,
    fine_solution,
    plane_of_slot,
    coarse_diagonal,
    coupling,
    donor_cells,
    donor_offsets,
    receptor_cells,
    fringe_counts,
):
    grid_index = lax.axis_index("grid")
    sub_index = lax.axis_index("sub")
    diagonal = coarse_diagonal[0]
    planes, variables, height, depth_cells = diagonal.shape
    cell_count = planes * height * depth_cells
    plane_ids = plane_of_slot[0]
    blocks = plane_ids.shape[0]
    solution_planes = restrict_planes(fine_solution[0])
    residual_planes = restrict_planes(fine_residual[0])
    contrib = jnp.stack([solution_planes, residual_planes], axis=1).reshape(blocks, -1)
    targets = plane_ids // 2
    wanted = sub_index * planes + jnp.arange(planes, dtype=jnp.int32)
    gathered, gathered_ids = (
        lax.all_gather(contrib, "sub", axis=0, tiled=True),
        lax.all_gather(plane_ids, "sub", axis=0, tiled=True),
    )
    select = ((gathered_ids // 2)[None, :] == wanted[:, None]).astype(jnp.float32)
    owned_sums = jnp.dot(
        select, gathered, precision=lax.Precision.HIGHEST, preferred_element_type=jnp.float32
    )
    owned_sums = owned_sums.reshape(planes, 2, variables, height, depth_cells)
    restricted_solution = owned_sums[:, 0]
    restricted_residual = owned_sums[:, 1]
    forcing = apply_operator(restricted_solution, diagonal, coupling) + restricted_residual
    slot_count = donor_cells.shape[-1]
    column = lax.dynamic_index_in_dim(fringe_counts, grid_index, 1, keepdims=False)
    allowed = jnp.repeat(column, FRINGE)
    live_slot = jnp.arange(slot_count, dtype=jnp.int32) % FRINGE < allowed
    target_cells = jnp.where(live_slot, receptor_cells[0, 0], cell_count)
    receptor_mask = jnp.zeros((cell_count,), jnp.float32).at[target_cells].set(1.0, mode="drop")
    receptor_mask = receptor_mask.reshape(planes, 1, height, depth_cells)
    donor_base = donor_cells[0, 0]
    offsets = donor_offsets[0, 0]
    field = restricted_solution
    for sweep_index in range(SWEEPS):
        flat_field = field.transpose(1, 0, 2, 3).reshape(variables, cell_count)
        corners = corner_values(flat_field, donor_base, height, depth_cells)
        arrived = lax.all_to_all(
            blend(corners, offsets), "grid", split_axis=1, concat_axis=1, tiled=True
        )
        flat_field = flat_field.at[:, target_cells].set(arrived, mode="drop")
        field = flat_field.reshape(variables, planes, height, depth_cells).transpose(1, 0, 2, 3)
        update = field + OMEGA * (forcing - apply_operator(field, diagonal, coupling)) / (
            6.0 + diagonal
        )
        field = jnp.where(receptor_mask > 0.5, field, update)
    correction = (field - restricted_solution).reshape(planes, -1)
    neighbour = targets - 1 + 2 * (plane_ids % 2)
    shard_rows = lax.all_gather(correction, "sub", axis=0, tiled=True)
    row_ids = jnp.arange(shard_rows.shape[0], dtype=jnp.int32)
    weights = 0.75 * (targets[:, None] == row_ids[None, :]).astype(jnp.float32)
    weights = weights + 0.25 * (neighbour[:, None] == row_ids[None, :]).astype(jnp.float32)
    along_x = jnp.dot(
        weights, shard_rows, precision=lax.Precision.HIGHEST, preferred_element_type=jnp.float32
    )
    along_x = along_x.reshape(blocks, variables, height, depth_cells)
    prolonged = refine(refine(along_x, -2), -1)
    return (fine_solution[0] + prolonged)[None]


BF16 = jnp.bfloat16
F32 = jnp.float32
HIGHEST = lax.Precision.HIGHEST
VMEM = pl.BlockSpec(memory_space=pltpu.VMEM)
HBM = pl.BlockSpec(memory_space=pltpu.HBM)
LANES = 128


def two_pieces(values):
    high = values.astype(BF16)
    return high, (values - high.astype(F32)).astype(BF16)


def dot_exact(values, matrix, contract=(((1,), (0,)), ((), ()))):
    high, low = two_pieces(values)
    total = lax.dot_general(low, matrix, contract, preferred_element_type=F32)
    return total + lax.dot_general(high, matrix, contract, preferred_element_type=F32)


def dot_near(values, matrix):
    high, low = two_pieces(values)
    matrix_high, matrix_low = two_pieces(matrix)
    total = jnp.dot(low, matrix_high, preferred_element_type=F32)
    total = total + jnp.dot(high, matrix_low, preferred_element_type=F32)
    return total + jnp.dot(high, matrix_high, preferred_element_type=F32)


def iota(shape, dim):
    return lax.broadcasted_iota(jnp.int32, shape, dim)


def split_cell(cell, height, depth):
    return cell // (height * depth), cell // depth % height, cell % depth


def neighbour_sum(field):
    total, variables, height, depth = field.shape
    flat = field.reshape(total * variables, height, depth)
    at_row = iota(flat.shape, 1)
    at_column = iota(flat.shape, 2)
    beside = jnp.where(at_row > 0, pltpu.roll(flat, 1, 1), 0.0)
    beside = beside + jnp.where(at_row < height - 1, pltpu.roll(flat, height - 1, 1), 0.0)
    beside = beside + jnp.where(at_column > 0, pltpu.roll(flat, 1, 2), 0.0)
    beside = beside + jnp.where(at_column < depth - 1, pltpu.roll(flat, depth - 1, 2), 0.0)
    beside = beside.reshape(field.shape)
    empty = jnp.zeros((1, variables, height, depth), F32)
    beside = beside + jnp.concatenate([empty, field[: total - 1]], axis=0)
    return beside + jnp.concatenate([field[1:], empty], axis=0)


def live_cells(counts, grid_index, grids, receptors, base):
    lane = iota(receptors.shape, 1)
    allowed = jnp.zeros(receptors.shape, jnp.int32)
    for g in range(grids):
        allowed = jnp.where(lane // FRINGE == g, counts[g, grid_index], allowed)
    return jnp.where(lane % FRINGE < allowed, receptors + base, -1)


def receptor_mask(cell, total, height, depth):
    count = cell.shape[1]
    plane, row, column = split_cell(cell, height, depth)
    onehot = jnp.where(iota((depth, count), 0) == column, 1.0, 0.0).astype(BF16)
    row_here = (iota((height, count), 0) == row) & (cell >= 0)
    here = jnp.concatenate([jnp.where(row_here & (plane == p), 1.0, 0.0) for p in range(total)], 0)
    contract = (((1,), (1,)), ((), ()))
    mask = lax.dot_general(here.astype(BF16), onehot, contract, preferred_element_type=F32)
    return mask.reshape(total, 1, height, depth), here, onehot


def start_copies(pairs, sems):
    copies = [pltpu.make_async_copy(*pair, sems.at[i]) for i, pair in enumerate(pairs)]
    for copy in copies:
        copy.start()
    return copies


def pack_kernel(
    sizes, counts, ids, diagonal, donors, offsets, receptors, out, held, rows, cells, planes_of, allowed, sems
):
    planes, variables, height, depth = sizes["coarse"]
    slots = sizes["slots"]
    base = lax.axis_index("sub") * (planes * height * depth)
    grid_index = lax.axis_index("grid")
    count = planes * variables
    copies = start_copies(
        [
            (counts, allowed),
            (receptors.at[0], cells.at[0]),
            (donors.at[0], cells.at[1]),
            (offsets.at[0], rows),
            (ids, planes_of),
            (diagonal.at[0], held),
        ],
        sems,
    )
    out[count] = jnp.zeros((height, depth), F32)
    for copy in copies:
        copy.wait()
    out[0:count] = OMEGA / (6.0 + held[...].reshape(count, height, depth))
    cell = live_cells(allowed, grid_index, sizes["grids"], cells[0], base)
    out[count, 0:1, 0:slots] = (cells[1] + base).astype(F32)
    for k in range(3):
        out[count, k + 1 : k + 2, 0:slots] = rows[k]
    out[count, 4:5, 0:slots] = cell.astype(F32)
    out[count, 5:6, 0 : sizes["blocks"]] = planes_of[...].astype(F32)


def find_corners(sizes, shared, out):
    planes, variables, height, depth = sizes["coarse"]
    slots, grids = sizes["slots"], sizes["grids"]
    grid_index = lax.axis_index("grid")
    base = lax.axis_index("sub") * (planes * height * depth)
    meta = shared[planes * variables, :, 0:slots]
    cell = meta[4:5].astype(jnp.int32)
    cell = jnp.where(cell >= 0, cell - base, -1)
    mask, _, _ = receptor_mask(cell, planes, height, depth)
    gain = shared[0 : planes * variables].reshape(planes, variables, height, depth)
    fields = jnp.concatenate([gain, mask], axis=1)
    donors = meta[0:1].astype(jnp.int32) - base
    twice = jnp.concatenate([donors, donors], axis=1)
    step_z = iota(twice.shape, 1) // slots
    plane, row, column = split_cell(twice, height, depth)
    onehot = jnp.where(iota((depth, LANES), 0) == column + step_z, 1.0, 0.0).astype(BF16)
    count = planes * (variables + 1) * height
    at_column = dot_exact(fields.reshape(count, depth), onehot)
    at_column = at_column.reshape(planes, variables + 1, height, LANES)
    both = jnp.concatenate([meta[1:4], meta[1:4]], axis=1)
    weight_z = jnp.where(step_z == 1, both[2:3], 1.0 - both[2:3])
    at_row = iota((height, LANES), 0)
    empty = jnp.zeros((5, LANES), F32)
    tiles = []
    for step_x in (0, 1):
        weight_x = both[0:1] if step_x else 1.0 - both[0:1]
        by_plane = None
        for p in range(planes):
            term = jnp.where(plane + step_x == p, at_column[p], 0.0)
            by_plane = term if by_plane is None else by_plane + term
        for step_y in (0, 1):
            weight_y = both[1:2] if step_y else 1.0 - both[1:2]
            here = jnp.where(at_row == row + step_y, 1.0, 0.0)
            found = jnp.sum(by_plane * here[None], axis=1)
            wet = found[variables : variables + 1]
            scaled = weight_x * weight_y * weight_z * (found[:variables] * (1.0 - wet) + wet)
            left = jnp.concatenate([empty, scaled[0:3]], axis=0)
            right = jnp.concatenate([empty, scaled[3:5], empty[0:1]], axis=0)
            tiles.append((left, right))
    lane = iota((8, LANES), 1)
    sublane = iota((8, LANES), 0)
    cells = jnp.broadcast_to(jnp.concatenate([meta[4:5], meta[4:5]], axis=1), (8, LANES))
    starts = jnp.broadcast_to(jnp.concatenate([meta[0:1], meta[0:1]], axis=1), (8, LANES))
    starts = pltpu.roll(starts, 8 * grid_index, 1)
    last = (sublane == 7) & (lane >= 64)
    mine = last & (lane % 64 // 8 == grid_index)
    for h in range(grids):
        tile = jnp.zeros((8, LANES), F32)
        for c in range(8):
            for k in (0, 1):
                shift = (64 * k + 8 * c - (c % 2) * 64 - 8 * h) % LANES
                moved = pltpu.roll(tiles[c // 2][k], shift, 1)
                tile = jnp.where(lane // 8 == 8 * k + c, moved, tile)
        tile = jnp.where(last, cells, tile)
        out[h] = jnp.where(mine, pltpu.roll(starts, (LANES - 8 * h) % LANES, 1), tile)


def restrict_kernel(sizes, residual, fine, shared, out, corners, held, wide, sems):
    planes, variables, height, depth = sizes["coarse"]
    blocks = sizes["blocks"]
    step = 8
    copies = start_copies(
        [
            (source.at[0, q : q + step], held.at[k, q : q + step])
            for k, source in enumerate((fine, residual))
            for q in range(0, blocks, step)
        ],
        sems,
    )
    find_corners(sizes, shared, corners)
    pair = jnp.where(
        iota((2 * depth, depth), 0) // 2 == iota((2 * depth, depth), 1), 0.125, 0.0
    ).astype(BF16)
    count = step * variables
    for i, copy in enumerate(copies):
        k, q = divmod(i * step, blocks)
        copy.wait()
        rows = held[k, q : q + step].reshape(count * 2 * height, 2 * depth)
        here = pl.ds(i * count, count)
        wide[here] = dot_exact(rows, pair).reshape(count, 2 * height, depth)
        out[here] = (
            wide[here, pl.ds(0, height, stride=2), :] + wide[here, pl.ds(1, height, stride=2), :]
        )


def hats(shape, dim, start, frac):
    at = iota(shape, dim)
    return jnp.where(at == start, 1.0 - frac, 0.0) + jnp.where(at == start + 1, frac, 0.0)


def interpolate(fields, rows, base):
    planes, variables, height, depth = fields[0].shape
    count = rows.shape[1]
    cell = rows[0:1, :].astype(jnp.int32) - base
    plane, row, column = split_cell(cell, height, depth)
    frac_x, frac_y, frac_z = rows[1:2, :], rows[2:3, :], rows[3:4, :]
    weight_z = hats((depth, count), 0, column, frac_z)
    weight_y = hats((height, count), 0, row, frac_y)
    lower = iota((depth, count), 1) < count // 2
    weight_z = jnp.concatenate(
        [jnp.where(lower, weight_z, 0.0), jnp.where(lower, 0.0, weight_z)], axis=0
    )
    both = jnp.concatenate([each.reshape(-1, depth) for each in fields], axis=1)
    along_z = dot_near(both, weight_z).reshape(planes, variables, height, count)
    summed = None
    for p in range(planes):
        weight_x = jnp.where(plane == p, 1.0 - frac_x, 0.0) + jnp.where(
            plane + 1 == p, frac_x, 0.0
        )
        term = along_z[p] * (weight_x * weight_y)[None]
        summed = term if summed is None else summed + term
    return jnp.sum(summed, axis=1)


def gather_rows(sizes, known, stage, rows):
    slots = sizes["slots"]
    for part, bit in zip(known, (0, 2, 1, 3)):
        stage[lax.axis_index("sub") ^ bit] = part[part.shape[0] - 1]
    for j, s in enumerate((0, 2, 1, 3)):
        rows[:, j * slots : (j + 1) * slots] = stage[s, :, 0:slots]


def partial_kernel(sizes, *refs):
    subs, grids, slots, blocks = sizes["subs"], sizes["grids"], sizes["slots"], sizes["blocks"]
    planes, variables, height, depth = sizes["coarse"]
    *known, own, corners = refs[:-8]
    joined = known[2]
    known = four_blocks(sizes, known)
    out, mask_out, both, rows, stage, pair, padded, wet = refs[-8:]
    total = subs * planes
    sub_index = lax.axis_index("sub")
    grid_index = lax.axis_index("grid")
    count = planes * variables
    gather_rows(sizes, known, stage, rows)
    pair[sub_index // 2] = known[0][...]
    pair[1 - sub_index // 2] = known[1][...]
    mask, _, _ = receptor_mask(rows[4:5, :].astype(jnp.int32), total, height, depth)
    mask_out[...] = mask
    wet[1 : total + 1] = mask
    padded[...] = jnp.zeros(padded.shape, F32)
    inner = padded.at[1 : total + 1]
    add_planes(sizes, [own], plane_numbers(known[0][count], blocks), inner)
    add_planes(sizes, [joined], plane_numbers(known[2][count], blocks), inner)
    both[...] = padded[1 : total + 1]
    core = sub_index % 2
    fields = []
    for k in range(2):
        start = (core + 2 * k) * planes
        here = padded[pl.ds(start, planes + 2)]
        dry = wet[pl.ds(start, planes + 2)] < 0.5
        drowned = jnp.where(dry, 0.0, here[:, 0:variables])
        beside = neighbour_sum(drowned)[1 : planes + 1]
        restricted, residual = here[1 : planes + 1, :variables], here[1 : planes + 1, variables:]
        gain = pair[k, 0:count].reshape(sizes["coarse"])
        swept = jnp.where(dry[1 : planes + 1], restricted + gain * (residual - beside), 0.0)
        fields.append(jnp.concatenate([restricted, swept], axis=1))
    half = jnp.concatenate([pair[0, count, :, 0:slots], pair[1, count, :, 0:slots]], axis=1)
    lane = iota((1, LANES), 1)
    base = (core + 2 * (lane // slots)) * (planes * height * depth)
    values = interpolate(fields, half, base)
    empty = jnp.zeros((3, LANES), F32)
    first = jnp.concatenate([values[:variables], empty], axis=0)
    second = jnp.concatenate([values[variables:], empty], axis=0)
    second = pltpu.roll(second, 8 * grid_index, 1)
    mine = iota((8, LANES), 1) % 64 // 8 == grid_index
    top = iota((8, LANES), 0) < variables
    for h in range(grids):
        tile = jnp.where(mine, pltpu.roll(second, (LANES - 8 * h) % LANES, 1), first)
        tile = jnp.where(top, tile, corners[h])
        for s in range(subs):
            out[h * subs + s] = tile


def plane_numbers(meta, blocks):
    row = meta[5:6, :]
    lane = iota(row.shape, 1)
    return [jnp.sum(jnp.where(lane == q, row, 0.0)).astype(jnp.int32) for q in range(blocks)]


def add_planes(sizes, pieces, numbers, both):
    variables, blocks = sizes["coarse"][1], sizes["blocks"]
    width = min(pieces[0].shape[0] // variables, 2 * blocks)
    for q in range(blocks):
        coarse = pl.ds(numbers[q] // 2, 1)
        for k in range(2):
            i = k * blocks + q
            at = i % width * variables
            part = pieces[i // width][at : at + variables]
            both[coarse, pl.ds(k * variables, variables)] += part[None]


def join_kernel(sizes, *refs):
    at = 0
    for part in refs[:-1]:
        refs[-1][at : at + part.shape[0]] = part[...]
        at = at + part.shape[0]


def four_blocks(sizes, known):
    shared, partner, joined, last = known
    size = shared.shape[0]
    return shared, partner, joined.at[joined.shape[0] - size :], last


def split_kernel(sizes, whole, *pieces):
    at = 0
    for piece in pieces:
        piece[...] = whole[at : at + piece.shape[0]]
        at = at + piece.shape[0]


def assemble_kernel(sizes, before, across, shared, partner, joined, last, *refs):
    variables = sizes["coarse"][1]
    pieces = refs[:-4]
    coupling, both, source, gain = refs[-4:]
    planes = sizes["coarse"][0]
    known = four_blocks(sizes, (shared, partner, joined, last))
    for part, bit in zip(known, (0, 2, 1, 3)):
        owner = lax.axis_index("sub") ^ bit
        end = part.shape[0] - 1
        here = part[end - planes * variables : end].reshape(sizes["coarse"])
        gain[pl.ds(owner * planes, planes)] = here
    count = planes * variables
    blocks = sizes["blocks"]
    both[...] = before[...]
    add_planes(sizes, [across], plane_numbers(partner[count], blocks), both)
    add_planes(sizes, pieces, plane_numbers(known[3][count], blocks), both)
    source[...] = couple(coupling, both[:, 0:variables])


def couple(coupling, field):
    variables = field.shape[1]
    outs = []
    for v in range(variables):
        summed = None
        for x in range(variables):
            term = coupling[v : v + 1, x : x + 1][None] * field[:, x]
            summed = term if summed is None else summed + term
        outs.append(jnp.tanh(summed)[:, None])
    return jnp.concatenate(outs, axis=1)


def target_features(cell, height, depth):
    plane, row, column = split_cell(jnp.maximum(cell, 0), height, depth)
    square = plane * plane + row * row + column * column
    square = jnp.where(cell >= 0, square, 1 << 15)
    coarse = square // LANES * LANES
    one = jnp.ones(cell.shape, jnp.int32)
    rows = [plane, row, column, one, one, one, -coarse, 2 + coarse - square]
    return jnp.concatenate([each.astype(F32) for each in rows], axis=0)


def corner_features(cell, height, depth):
    plane, row, column = split_cell(cell, height, depth)
    square = plane * plane + row * row + column * column
    coarse = square // LANES * LANES
    one = jnp.ones(cell.shape, jnp.int32)
    rows = [2 * plane, 2 * row, 2 * column, -coarse, coarse - square, 0 * one, one, one]
    return jnp.concatenate([each.astype(F32) for each in rows], axis=0)


def fringe_values(sizes, arrived, landing):
    subs, grids, slots = sizes["subs"], sizes["grids"], sizes["slots"]
    _, _, height, depth = sizes["coarse"]
    lane = iota((8, LANES), 1)
    sublane = iota((8, LANES), 0)
    group = lane % 64 // 8
    firsts = []
    for g in range(grids):
        halves = []
        for k in range(2):
            half = arrived[g * subs + k]
            for s in range(k + 2, subs, 2):
                half = half + arrived[g * subs + s]
            halves.append(half)
        firsts.append(halves)
    for g in range(grids):
        for k in range(2):
            sent = firsts[g][k]
            for other in range(grids):
                if other != g:
                    moved = pltpu.roll(firsts[other][k], (8 * other - 8 * g) % LANES, 1)
                    sent = jnp.where(group == other, moved, sent)
            landing[g, :, k * LANES : (k + 1) * LANES] = sent
    cells = [jnp.zeros((8, LANES), F32)] * 2
    scales = []
    for g in range(grids):
        scale = []
        for k in range(2):
            one, two = arrived[g * subs + k], arrived[g * subs + k + 2]
            low = jnp.where(lane < 64, one, pltpu.roll(two, 64, 1))
            high = jnp.where(lane < 64, pltpu.roll(one, 64, 1), two)
            scale.append(jnp.where(sublane < 3, pltpu.roll(low, 3, 0), pltpu.roll(high, 6, 0)))
            cells[k] = jnp.where(sublane == g, pltpu.roll(high, (g + 1) % 8, 0), cells[k])
        scales.append(scale)
    targets, corners = [], []
    step = ((group // 4) * height + group // 2 % 2) * depth + group % 2
    for k in range(2):
        targets.append(jnp.where(group == sublane, -1.0, cells[k]))
        starts = jnp.where(group == sublane, cells[k], 0.0)
        parts = []
        for half in (lane < 64, lane >= 64):
            start = jnp.where(half, starts, 0.0)
            for shift in (64, 32, 16, 8):
                start = start + pltpu.roll(start, shift, 1)
            parts.append(start)
        corners.append(jnp.where(lane < 64, parts[0], parts[1]).astype(jnp.int32) + step)
    targets = jnp.concatenate(targets, axis=1).astype(jnp.int32)
    corners = jnp.concatenate(corners, axis=1)
    theirs = target_features(targets, height, depth).T.astype(BF16)
    ours = corner_features(corners, height, depth)
    which = iota(ours.shape, 0) % 8
    mine = [jnp.where(which == g, ours, 0.0).astype(BF16) for g in range(grids)]
    closeness = jnp.dot(theirs, jnp.concatenate(mine, axis=1), preferred_element_type=F32)
    closeness = closeness.astype(BF16)
    most = closeness
    while most.shape[0] > 16:
        half = most.shape[0] // 2
        most = jnp.maximum(most[:half], most[half:])
    wet = jnp.max(most.astype(F32), axis=0, keepdims=True) - 1.0
    match = jnp.maximum(closeness - jnp.maximum(wet, 0.0).astype(BF16), 0.0)
    lanes = subs * slots
    values = [[], []]
    for g in range(grids):
        sent = landing[g]
        high = sent.astype(BF16).astype(F32)
        stacked = jnp.concatenate([high, sent - high], axis=0).astype(BF16)
        near = jnp.dot(stacked, match[:, g * lanes : (g + 1) * lanes], preferred_element_type=F32)
        near = near[0:8] + near[8:16]
        for k in range(2):
            values[k].append(near[:, k * LANES : (k + 1) * LANES] * scales[g][k])
    total = []
    for k in range(2):
        parts = values[k]
        for bit in (4, 2, 1):
            width = 8 * bit
            lower = lane // width % 2 == 0
            parts = [
                jnp.where(
                    lower,
                    one + pltpu.roll(one, LANES - width, 1),
                    two + pltpu.roll(two, width, 1),
                )
                for one, two in zip(parts[:bit], parts[bit:])
            ]
        known = firsts[0][k]
        for g in range(1, grids):
            known = jnp.where(group == g, firsts[g][k], known)
        total.append(parts[0] + known)
    return landing[lax.axis_index("grid")], jnp.concatenate(total, axis=1)


def spread(values, cell, total, height, depth):
    count = cell.shape[1]
    pairs = values.shape[0] // 2
    plane, row, column = split_cell(cell, height, depth)
    onehot = jnp.where(iota((depth, count), 0) == column, 1.0, 0.0).astype(BF16)
    row_here = (iota((2 * height, count), 0) % height == row) & (cell >= 0)
    tiles = []
    for i in range(pairs):
        twin = [jnp.broadcast_to(values[2 * i + k : 2 * i + k + 1], (height, count)) for k in (0, 1)]
        tiles.append(two_pieces(jnp.concatenate(twin, axis=0)))
    rows = [[], []]
    for p in range(total):
        here = jnp.where(row_here & (plane == p), 1.0, 0.0).astype(BF16)
        for tile in tiles:
            for k in (0, 1):
                rows[k].append(tile[k] * here)
    contract = (((1,), (1,)), ((), ()))
    high, low = [
        lax.dot_general(
            jnp.concatenate(rows[k], axis=0), onehot, contract, preferred_element_type=F32
        )
        for k in (0, 1)
    ]
    return (high + low).reshape(total, 2 * pairs, height, depth)


def finish_kernel(sizes, *refs):
    subs = sizes["subs"]
    planes, variables, height, depth = sizes["coarse"]
    blocks = sizes["blocks"]
    parts = four_blocks(sizes, refs[:4])
    coupling, arrived, both, source, gain, mask, fine = refs[4:11]
    out, landing, stage, rows, padded, tall, held, sems = refs[11:]
    total = subs * planes
    gather_rows(sizes, parts, stage, rows)
    first, second = fringe_values(sizes, arrived, landing)
    cell = rows[4:5, :].astype(jnp.int32)
    values = jnp.concatenate([first[:variables], second[:variables]], axis=0)
    landed = spread(values, cell, total, height, depth)
    wet = mask[...] > 0.5
    start = both[:, 0:variables]
    rest = both[:, variables:]
    scale = gain[...]
    change = jnp.where(wet, landed[:, 0:variables] - start, 0.0)
    update = scale * (rest + neighbour_sum(change))
    change = jnp.where(wet, landed[:, variables:] - start, update)
    apart = source[...] - couple(coupling, start + change)
    update = scale * (rest + neighbour_sum(change) + 2.0 * apart)
    correction = jnp.where(wet, change, (1.0 - OMEGA) * change + update)
    padded[0:1] = jnp.zeros((1, variables, height, depth), F32)
    padded[total + 1 : total + 2] = jnp.zeros((1, variables, height, depth), F32)
    padded[1 : total + 1] = correction
    at_row = iota((variables, height, depth), 1)
    coarse_at = iota((depth, 2 * depth), 0)
    fine_at = iota((depth, 2 * depth), 1)
    beside = fine_at // 2 - 1 + 2 * (fine_at % 2)
    widen = jnp.where(
        coarse_at == fine_at // 2, 0.75, jnp.where(coarse_at == beside, 0.25, 0.0)
    ).astype(BF16)
    copies = []
    step = 2
    numbers = plane_numbers(parts[0][planes * variables], blocks)
    for q, number in enumerate(numbers):
        coarse = number // 2
        along = 0.75 * padded[coarse + 1] + 0.25 * padded[coarse + 2 * (number % 2)]
        below = jnp.where(at_row > 0, pltpu.roll(along, 1, 1), 0.0)
        above = jnp.where(at_row < height - 1, pltpu.roll(along, height - 1, 1), 0.0)
        block = slice(q * variables, (q + 1) * variables)
        tall[block, pl.ds(0, height, stride=2), :] = 0.75 * along + 0.25 * below
        tall[block, pl.ds(1, height, stride=2), :] = 0.75 * along + 0.25 * above
        if q % step == step - 1:
            low = q + 1 - step
            rows_in = tall[low * variables : (q + 1) * variables]
            prolonged = dot_exact(rows_in.reshape(step * variables * 2 * height, depth), widen)
            shape = (step, variables, 2 * height, 2 * depth)
            held[low : q + 1] = fine[0, low : q + 1] + prolonged.reshape(shape)
            copy = pltpu.make_async_copy(
                held.at[low : q + 1], out.at[0, low : q + 1], sems.at[q // step]
            )
            copy.start()
            copies.append(copy)
    for copy in copies:
        copy.wait()


def fast_shards(
    fine_residual,
    fine_solution,
    plane_of_slot,
    coarse_diagonal,
    coupling,
    donor_cells,
    donor_offsets,
    receptor_cells,
    fringe_counts,
):
    subs = lax.axis_size("sub")
    grids = lax.axis_size("grid")
    coarse = coarse_diagonal.shape[1:]
    planes, variables, height, depth = coarse
    blocks = plane_of_slot.shape[1]
    slots = donor_cells.shape[-1]
    sizes = dict(coarse=coarse, blocks=blocks, slots=slots, grids=grids, subs=subs)
    count = blocks * variables
    total = subs * planes
    whole = (total, variables, height, depth)
    full = jax.ShapeDtypeStruct(whole, F32)
    rows = pltpu.VMEM((8, subs * slots), F32)
    stage = pltpu.VMEM((subs, 8, depth), F32)

    def call(kernel, name, out_shape, *operands, scratch=(), far=(), out_spec=VMEM, aliases={}, cost=None):
        specs = [HBM if any(one is each for each in far) else VMEM for one in operands]
        operands = [
            pltpu.with_memory_space_constraint(one, pltpu.HBM) if spec is HBM else one
            for one, spec in zip(operands, specs)
        ]
        return pl.pallas_call(
            functools.partial(kernel, sizes),
            out_shape=out_shape,
            in_specs=specs,
            out_specs=jax.tree.map(lambda _: out_spec, out_shape),
            scratch_shapes=list(scratch),
            input_output_aliases=aliases,
            cost_estimate=cost,
            compiler_params=pltpu.CompilerParams(vmem_limit_bytes=48 * 1024 * 1024),
            name=name,
        )(*operands)

    offsets = donor_offsets.transpose(0, 2, 1, 3)
    inputs = (fringe_counts, plane_of_slot, coarse_diagonal, donor_cells, offsets, receptor_cells)
    shared = call(
        pack_kernel,
        "pack",
        jax.ShapeDtypeStruct((planes * variables + 1, height, depth), F32),
        *inputs,
        far=inputs,
        scratch=[
            pltpu.VMEM(coarse, F32),
            pltpu.VMEM(offsets.shape[1:], F32),
            pltpu.VMEM((2, 1, slots), jnp.int32),
            pltpu.VMEM(plane_of_slot.shape, jnp.int32),
            pltpu.SMEM(fringe_counts.shape, jnp.int32),
            pltpu.SemaphoreType.DMA((6,)),
        ],
    )
    swap = {bit: [(i, i ^ bit) for i in range(subs)] for bit in (1, 2)}
    partner = lax.ppermute(shared, "sub", swap[2])
    own, corners = call(
        restrict_kernel,
        "restrict",
        [
            jax.ShapeDtypeStruct((2 * count, height, depth), F32),
            jax.ShapeDtypeStruct((grids, 8, LANES), F32),
        ],
        fine_residual,
        fine_solution,
        shared,
        far=(fine_residual, fine_solution),
        scratch=[
            pltpu.VMEM((2,) + fine_solution.shape[1:], F32),
            pltpu.VMEM((2 * count, 2 * height, depth), F32),
            pltpu.SemaphoreType.DMA((blocks,)),
        ],
    )
    size = own.shape[0] + shared.shape[0]
    joined = call(
        join_kernel, "join", jax.ShapeDtypeStruct((size, height, depth), F32), own, shared
    )
    joined = lax.ppermute(joined, "sub", swap[1])
    own, partner = lax.optimization_barrier((own, partner))
    partner = call(
        join_kernel, "pass", jax.ShapeDtypeStruct(partner.shape, F32), partner, cost=pl.CostEstimate(flops=20_000_000_000, transcendentals=0, bytes_accessed=100_000_000)
    )
    known = (shared, partner, joined, lax.ppermute(partner, "sub", swap[1]))
    across = lax.ppermute(own, "sub", swap[2])
    out, mask, both = call(
        partial_kernel,
        "partial",
        [
            jax.ShapeDtypeStruct((grids * subs, 8, LANES), F32),
            jax.ShapeDtypeStruct((total, 1, height, depth), F32),
            jax.ShapeDtypeStruct((total, 2 * variables, height, depth), F32),
        ],
        *known,
        own,
        corners,
        cost=pl.CostEstimate(flops=20_000_000_000, transcendentals=0, bytes_accessed=100_000_000),
        scratch=[
            rows,
            stage,
            pltpu.VMEM((2, planes * variables + 1, height, depth), F32),
            pltpu.VMEM((total + 2, 2 * variables, height, depth), F32),
            pltpu.VMEM((total + 2, 1, height, depth), F32),
        ],
    )
    arrived = lax.all_to_all(out, ("grid", "sub"), 0, 0, tiled=True)
    piece = jax.ShapeDtypeStruct((blocks // 2 * variables, height, depth), F32)
    pieces = call(split_kernel, "split", [piece] * 4, across)
    pieces = [lax.ppermute(each, "sub", swap[1]) for each in pieces]
    both, source, gain = call(
        assemble_kernel,
        "assemble",
        [jax.ShapeDtypeStruct(both.shape, F32), full, full],
        both,
        across,
        *known,
        *pieces,
        coupling,
        aliases={0: 0},
    )
    return call(
        finish_kernel,
        "finish",
        jax.ShapeDtypeStruct(fine_solution.shape, F32),
        *known,
        coupling,
        arrived,
        both,
        source,
        gain,
        mask,
        fine_solution,
        scratch=[
            pltpu.VMEM((grids, 8, subs * slots), F32),
            stage,
            rows,
            pltpu.VMEM((total + 2, variables, height, depth), F32),
            pltpu.VMEM((count, 2 * height, depth), F32),
            pltpu.VMEM(fine_solution.shape[1:], F32),
            pltpu.SemaphoreType.DMA((blocks // 2,)),
        ],
        out_spec=HBM,
    )


def solution(mesh):
    in_specs = (
        P("grid", "sub", None, None, None),
        P("grid", "sub", None, None, None),
        P("grid", "sub"),
        P("grid", "sub", None, None, None),
        P(),
        P("grid", "sub", None),
        P("grid", "sub", None, None),
        P("grid", "sub", None),
        P(),
    )
    out_specs = P("grid", "sub", None, None, None)
    small = mesh.shape["sub"] == 4 and mesh.shape["grid"] * FRINGE == 64
    body = fast_shards if small else shards
    return jax.shard_map(body, mesh=mesh, in_specs=in_specs, out_specs=out_specs, check_vma=False)
```

```python
import functools

import jax
import jax.numpy as jnp
from jax import lax
from jax.experimental import pallas as pl
from jax.experimental.pallas import tpu as pltpu
from jax.sharding import PartitionSpec as P

FRINGE = 8
SWEEPS = 2


OMEGA = 0.8


def padded_2(block, sides, width):
    for axis, dim in sides:
        count = lax.axis_size(axis)
        forward = [(i, i + 1) for i in range(count - 1)]
        backward = [(target, source) for source, target in forward]
        low = lax.ppermute(
            lax.slice_in_dim(block, block.shape[dim] - width, None, axis=dim), axis, forward
        )
        high = lax.ppermute(lax.slice_in_dim(block, 0, width, axis=dim), axis, backward)
        block = jnp.concatenate([low, block, high], axis=dim)
    return block


def restrict_planes(fine_field):
    dims_in = fine_field.shape
    split_cells = fine_field.reshape(dims_in[:-2] + (dims_in[-2] // 2, 2, dims_in[-1] // 2, 2))
    return 0.125 * jnp.sum(split_cells, axis=(-3, -1))


def pair_sum(field, axis):
    which = axis % field.ndim
    length = field.shape[which]
    empty = jnp.zeros_like(lax.slice_in_dim(field, 0, 1, axis=which))
    below_side = jnp.concatenate(
        [empty, lax.slice_in_dim(field, 0, length - 1, axis=which)], axis=which
    )
    above_side = jnp.concatenate(
        [lax.slice_in_dim(field, 1, length, axis=which), empty], axis=which
    )
    return below_side + above_side


def operate(field, padded, diagonal, coupling):
    which = field.ndim - 4
    length = padded.shape[which]
    beside = lax.slice_in_dim(padded, 2, length, axis=which) + lax.slice_in_dim(
        padded, 0, length - 2, axis=which
    )
    beside = beside + pair_sum(field, field.ndim - 2)
    beside = beside + pair_sum(field, field.ndim - 1)
    coupled = jnp.einsum("vw,...wyz->...vyz", coupling, field, precision=lax.Precision.HIGHEST)
    return (6.0 + diagonal) * field - beside + 2.0 * jnp.tanh(coupled)


def apply_operator(field, diagonal, coupling):
    padded = padded_2(field, (("sub", 0),), 1)
    return operate(field, padded, diagonal, coupling)


def corner_values(flat_field, donor_base, height, depth):
    corners = []
    for step_x in (0, 1):
        for step_y in (0, 1):
            for step_z in (0, 1):
                where_cells = donor_base + step_x * height * depth + step_y * depth + step_z
                corners.append(jnp.take_along_axis(flat_field, where_cells[..., None, :], axis=-1))
    return corners


def blend(corners, offsets):
    frac_x = offsets[..., 0:1, :]
    frac_y = offsets[..., 1:2, :]
    frac_z = offsets[..., 2:3, :]
    summed = None
    number = 0
    for step_x in (0, 1):
        for step_y in (0, 1):
            for step_z in (0, 1):
                weight_x = frac_x if step_x else 1.0 - frac_x
                weight_y = frac_y if step_y else 1.0 - frac_y
                weight_z = frac_z if step_z else 1.0 - frac_z
                term = weight_x * weight_y * weight_z * corners[number]
                summed = term if summed is None else summed + term
                number = number + 1
    return summed


def refine(field, axis):
    which = axis % field.ndim
    length = field.shape[which]
    empty = jnp.zeros_like(lax.slice_in_dim(field, 0, 1, axis=which))
    below_side = jnp.concatenate(
        [empty, lax.slice_in_dim(field, 0, length - 1, axis=which)], axis=which
    )
    above_side = jnp.concatenate(
        [lax.slice_in_dim(field, 1, length, axis=which), empty], axis=which
    )
    first_half = 0.75 * field + 0.25 * below_side
    second_half = 0.75 * field + 0.25 * above_side
    joined = jnp.stack([first_half, second_half], axis=which + 1)
    new_dims = list(field.shape)
    new_dims[which] = 2 * length
    return joined.reshape(new_dims)


def shards(
    fine_residual,
    fine_solution,
    plane_of_slot,
    coarse_diagonal,
    coupling,
    donor_cells,
    donor_offsets,
    receptor_cells,
    fringe_counts,
):
    grid_index = lax.axis_index("grid")
    sub_index = lax.axis_index("sub")
    diagonal = coarse_diagonal[0]
    planes, variables, height, depth_cells = diagonal.shape
    cell_count = planes * height * depth_cells
    plane_ids = plane_of_slot[0]
    blocks = plane_ids.shape[0]
    solution_planes = restrict_planes(fine_solution[0])
    residual_planes = restrict_planes(fine_residual[0])
    contrib = jnp.stack([solution_planes, residual_planes], axis=1).reshape(blocks, -1)
    targets = plane_ids // 2
    wanted = sub_index * planes + jnp.arange(planes, dtype=jnp.int32)
    gathered, gathered_ids = (
        lax.all_gather(contrib, "sub", axis=0, tiled=True),
        lax.all_gather(plane_ids, "sub", axis=0, tiled=True),
    )
    select = ((gathered_ids // 2)[None, :] == wanted[:, None]).astype(jnp.float32)
    owned_sums = jnp.dot(
        select, gathered, precision=lax.Precision.HIGHEST, preferred_element_type=jnp.float32
    )
    owned_sums = owned_sums.reshape(planes, 2, variables, height, depth_cells)
    restricted_solution = owned_sums[:, 0]
    restricted_residual = owned_sums[:, 1]
    forcing = apply_operator(restricted_solution, diagonal, coupling) + restricted_residual
    slot_count = donor_cells.shape[-1]
    column = lax.dynamic_index_in_dim(fringe_counts, grid_index, 1, keepdims=False)
    allowed = jnp.repeat(column, FRINGE)
    live_slot = jnp.arange(slot_count, dtype=jnp.int32) % FRINGE < allowed
    target_cells = jnp.where(live_slot, receptor_cells[0, 0], cell_count)
    receptor_mask = jnp.zeros((cell_count,), jnp.float32).at[target_cells].set(1.0, mode="drop")
    receptor_mask = receptor_mask.reshape(planes, 1, height, depth_cells)
    donor_base = donor_cells[0, 0]
    offsets = donor_offsets[0, 0]
    field = restricted_solution
    for sweep_index in range(SWEEPS):
        flat_field = field.transpose(1, 0, 2, 3).reshape(variables, cell_count)
        corners = corner_values(flat_field, donor_base, height, depth_cells)
        arrived = lax.all_to_all(
            blend(corners, offsets), "grid", split_axis=1, concat_axis=1, tiled=True
        )
        flat_field = flat_field.at[:, target_cells].set(arrived, mode="drop")
        field = flat_field.reshape(variables, planes, height, depth_cells).transpose(1, 0, 2, 3)
        update = field + OMEGA * (forcing - apply_operator(field, diagonal, coupling)) / (
            6.0 + diagonal
        )
        field = jnp.where(receptor_mask > 0.5, field, update)
    correction = (field - restricted_solution).reshape(planes, -1)
    neighbour = targets - 1 + 2 * (plane_ids % 2)
    shard_rows = lax.all_gather(correction, "sub", axis=0, tiled=True)
    row_ids = jnp.arange(shard_rows.shape[0], dtype=jnp.int32)
    weights = 0.75 * (targets[:, None] == row_ids[None, :]).astype(jnp.float32)
    weights = weights + 0.25 * (neighbour[:, None] == row_ids[None, :]).astype(jnp.float32)
    along_x = jnp.dot(
        weights, shard_rows, precision=lax.Precision.HIGHEST, preferred_element_type=jnp.float32
    )
    along_x = along_x.reshape(blocks, variables, height, depth_cells)
    prolonged = refine(refine(along_x, -2), -1)
    return (fine_solution[0] + prolonged)[None]


BF16 = jnp.bfloat16
F32 = jnp.float32
HIGHEST = lax.Precision.HIGHEST
VMEM = pl.BlockSpec(memory_space=pltpu.VMEM)
HBM = pl.BlockSpec(memory_space=pltpu.HBM)
LANES = 128


def two_pieces(values):
    high = values.astype(BF16)
    return high, (values - high.astype(F32)).astype(BF16)


def dot_exact(values, matrix):
    parts = jnp.concatenate(two_pieces(values), axis=1)
    return jnp.dot(
        parts, jnp.concatenate([matrix, matrix], axis=0), preferred_element_type=F32
    )


def dot_near(values, matrix):
    high, low = two_pieces(values)
    matrix_high, matrix_low = two_pieces(matrix)
    return jnp.dot(
        jnp.concatenate([high, low, high], axis=1),
        jnp.concatenate([matrix_high, matrix_high, matrix_low], axis=0),
        preferred_element_type=F32,
    )


def iota(shape, dim):
    return lax.broadcasted_iota(jnp.int32, shape, dim)


def split_cell(cell, height, depth):
    return cell // (height * depth), cell // depth % height, cell % depth


def neighbour_sum(field):
    total, variables, height, depth = field.shape
    flat = field.reshape(total * variables, height, depth)
    at_row = iota(flat.shape, 1)
    at_column = iota(flat.shape, 2)
    beside = jnp.where(at_row > 0, pltpu.roll(flat, 1, 1), 0.0)
    beside = beside + jnp.where(at_row < height - 1, pltpu.roll(flat, height - 1, 1), 0.0)
    beside = beside + jnp.where(at_column > 0, pltpu.roll(flat, 1, 2), 0.0)
    beside = beside + jnp.where(at_column < depth - 1, pltpu.roll(flat, depth - 1, 2), 0.0)
    beside = beside.reshape(field.shape)
    empty = jnp.zeros((1, variables, height, depth), F32)
    beside = beside + jnp.concatenate([empty, field[: total - 1]], axis=0)
    return beside + jnp.concatenate([field[1:], empty], axis=0)


def live_cells(counts, grid_index, grids, receptors, base):
    lane = iota(receptors.shape, 1)
    allowed = jnp.zeros(receptors.shape, jnp.int32)
    for g in range(grids):
        allowed = jnp.where(lane // FRINGE == g, counts[g, grid_index], allowed)
    return jnp.where(lane % FRINGE < allowed, receptors + base, -1)


def receptor_mask(cell, total, height, depth):
    count = cell.shape[1]
    plane, row, column = split_cell(cell, height, depth)
    onehot = jnp.where(iota((depth, count), 0) == column, 1.0, 0.0).astype(BF16)
    row_here = (iota((height, count), 0) == row) & (cell >= 0)
    here = jnp.concatenate([jnp.where(row_here & (plane == p), 1.0, 0.0) for p in range(total)], 0)
    contract = (((1,), (1,)), ((), ()))
    mask = lax.dot_general(here.astype(BF16), onehot, contract, preferred_element_type=F32)
    return mask.reshape(total, 1, height, depth), here, onehot


def start_copies(pairs, sems):
    copies = [pltpu.make_async_copy(*pair, sems.at[i]) for i, pair in enumerate(pairs)]
    for copy in copies:
        copy.start()
    return copies


def pack_kernel(
    sizes, counts, ids, diagonal, donors, offsets, receptors, out, held, rows, cells, planes_of, allowed, sems
):
    planes, variables, height, depth = sizes["coarse"]
    slots = sizes["slots"]
    base = lax.axis_index("sub") * (planes * height * depth)
    grid_index = lax.axis_index("grid")
    count = planes * variables
    copies = start_copies(
        [
            (counts, allowed),
            (receptors.at[0], cells.at[0]),
            (donors.at[0], cells.at[1]),
            (offsets.at[0], rows),
            (ids, planes_of),
            (diagonal.at[0], held),
        ],
        sems,
    )
    out[count] = jnp.zeros((height, depth), F32)
    for copy in copies:
        copy.wait()
    out[0:count] = OMEGA / (6.0 + held[...].reshape(count, height, depth))
    cell = live_cells(allowed, grid_index, sizes["grids"], cells[0], base)
    out[count, 0:1, 0:slots] = (cells[1] + base).astype(F32)
    for k in range(3):
        out[count, k + 1 : k + 2, 0:slots] = rows[k]
    out[count, 4:5, 0:slots] = cell.astype(F32)
    out[count, 5:6, 0 : sizes["blocks"]] = planes_of[...].astype(F32)


def find_corners(sizes, shared, out):
    planes, variables, height, depth = sizes["coarse"]
    slots, grids = sizes["slots"], sizes["grids"]
    grid_index = lax.axis_index("grid")
    base = lax.axis_index("sub") * (planes * height * depth)
    meta = shared[planes * variables, :, 0:slots]
    cell = meta[4:5].astype(jnp.int32)
    cell = jnp.where(cell >= 0, cell - base, -1)
    mask, _, _ = receptor_mask(cell, planes, height, depth)
    gain = shared[0 : planes * variables].reshape(planes, variables, height, depth)
    fields = jnp.concatenate([gain, mask], axis=1)
    donors = meta[0:1].astype(jnp.int32) - base
    twice = jnp.concatenate([donors, donors], axis=1)
    step_z = iota(twice.shape, 1) // slots
    plane, row, column = split_cell(twice, height, depth)
    onehot = jnp.where(iota((depth, LANES), 0) == column + step_z, 1.0, 0.0).astype(BF16)
    count = planes * (variables + 1) * height
    at_column = dot_exact(fields.reshape(count, depth), onehot)
    at_column = at_column.reshape(planes, variables + 1, height, LANES)
    both = jnp.concatenate([meta[1:4], meta[1:4]], axis=1)
    weight_z = jnp.where(step_z == 1, both[2:3], 1.0 - both[2:3])
    at_row = iota((height, LANES), 0)
    empty = jnp.zeros((5, LANES), F32)
    tiles = []
    for step_x in (0, 1):
        weight_x = both[0:1] if step_x else 1.0 - both[0:1]
        by_plane = None
        for p in range(planes):
            term = jnp.where(plane + step_x == p, at_column[p], 0.0)
            by_plane = term if by_plane is None else by_plane + term
        for step_y in (0, 1):
            weight_y = both[1:2] if step_y else 1.0 - both[1:2]
            here = jnp.where(at_row == row + step_y, 1.0, 0.0)
            found = jnp.sum(by_plane * here[None], axis=1)
            wet = found[variables : variables + 1]
            scaled = weight_x * weight_y * weight_z * (found[:variables] * (1.0 - wet) + wet)
            left = jnp.concatenate([empty, scaled[0:3]], axis=0)
            right = jnp.concatenate([empty, scaled[3:5], empty[0:1]], axis=0)
            tiles.append((left, right))
    lane = iota((8, LANES), 1)
    sublane = iota((8, LANES), 0)
    cells = jnp.broadcast_to(jnp.concatenate([meta[4:5], meta[4:5]], axis=1), (8, LANES))
    starts = jnp.broadcast_to(jnp.concatenate([meta[0:1], meta[0:1]], axis=1), (8, LANES))
    starts = pltpu.roll(starts, 8 * grid_index, 1)
    last = (sublane == 7) & (lane >= 64)
    mine = last & (lane % 64 // 8 == grid_index)
    for h in range(grids):
        tile = jnp.zeros((8, LANES), F32)
        for c in range(8):
            for k in (0, 1):
                shift = (64 * k + 8 * c - (c % 2) * 64 - 8 * h) % LANES
                moved = pltpu.roll(tiles[c // 2][k], shift, 1)
                tile = jnp.where(lane // 8 == 8 * k + c, moved, tile)
        tile = jnp.where(last, cells, tile)
        out[h] = jnp.where(mine, pltpu.roll(starts, (LANES - 8 * h) % LANES, 1), tile)


def restrict_kernel(sizes, residual, fine, shared, out, corners, fine_here, held, wide, sems):
    planes, variables, height, depth = sizes["coarse"]
    blocks = sizes["blocks"]
    step = 8
    copies = start_copies(
        [
            (source.at[0, q : q + step], target.at[q : q + step])
            for source, target in ((fine, fine_here), (residual, held))
            for q in range(0, blocks, step)
        ],
        sems,
    )
    find_corners(sizes, shared, corners)
    pair = jnp.where(
        iota((2 * depth, depth), 0) // 2 == iota((2 * depth, depth), 1), 0.125, 0.0
    ).astype(BF16)
    count = step * variables
    for i, copy in enumerate(copies):
        k, q = divmod(i * step, blocks)
        copy.wait()
        rows = (fine_here, held)[k][q : q + step].reshape(count * 2 * height, 2 * depth)
        here = pl.ds(i * count, count)
        wide[here] = dot_exact(rows, pair).reshape(count, 2 * height, depth)
        out[here] = (
            wide[here, pl.ds(0, height, stride=2), :] + wide[here, pl.ds(1, height, stride=2), :]
        )


def hats(shape, dim, start, frac):
    at = iota(shape, dim)
    return jnp.where(at == start, 1.0 - frac, 0.0) + jnp.where(at == start + 1, frac, 0.0)


def interpolate(fields, rows, base):
    planes, variables, height, depth = fields[0].shape
    count = rows.shape[1]
    cell = rows[0:1, :].astype(jnp.int32) - base
    plane, row, column = split_cell(cell, height, depth)
    frac_x, frac_y, frac_z = rows[1:2, :], rows[2:3, :], rows[3:4, :]
    weight_z = hats((depth, count), 0, column, frac_z)
    weight_y = hats((height, count), 0, row, frac_y)
    lower = iota((depth, count), 1) < count // 2
    weight_z = jnp.concatenate(
        [jnp.where(lower, weight_z, 0.0), jnp.where(lower, 0.0, weight_z)], axis=0
    )
    both = jnp.concatenate([each.reshape(-1, depth) for each in fields], axis=1)
    along_z = dot_near(both, weight_z).reshape(planes, variables, height, count)
    summed = None
    for p in range(planes):
        weight_x = jnp.where(plane == p, 1.0 - frac_x, 0.0) + jnp.where(
            plane + 1 == p, frac_x, 0.0
        )
        term = along_z[p] * (weight_x * weight_y)[None]
        summed = term if summed is None else summed + term
    return jnp.sum(summed, axis=1)


def gather_rows(sizes, known, stage, rows):
    slots = sizes["slots"]
    for part, bit in zip(known, (0, 2, 1, 3)):
        stage[lax.axis_index("sub") ^ bit] = part[part.shape[0] - 1]
    for j, s in enumerate((0, 2, 1, 3)):
        rows[:, j * slots : (j + 1) * slots] = stage[s, :, 0:slots]


def partial_kernel(sizes, *refs):
    subs, grids, slots, blocks = sizes["subs"], sizes["grids"], sizes["slots"], sizes["blocks"]
    planes, variables, height, depth = sizes["coarse"]
    *known, own, corners = refs[:-8]
    joined = known[2]
    known = four_blocks(sizes, known)
    out, mask_out, both, rows, stage, pair, padded, wet = refs[-8:]
    total = subs * planes
    sub_index = lax.axis_index("sub")
    grid_index = lax.axis_index("grid")
    count = planes * variables
    gather_rows(sizes, known, stage, rows)
    pair[sub_index // 2] = known[0][...]
    pair[1 - sub_index // 2] = known[1][...]
    mask, _, _ = receptor_mask(rows[4:5, :].astype(jnp.int32), total, height, depth)
    mask_out[...] = mask
    wet[1 : total + 1] = mask
    padded[...] = jnp.zeros(padded.shape, F32)
    inner = padded.at[1 : total + 1]
    add_planes(sizes, [own], plane_numbers(known[0][count], blocks), inner)
    add_planes(sizes, [joined], plane_numbers(known[2][count], blocks), inner)
    both[...] = padded[1 : total + 1]
    core = sub_index % 2
    fields = []
    for k in range(2):
        start = (core + 2 * k) * planes
        here = padded[pl.ds(start, planes + 2)]
        dry = wet[pl.ds(start, planes + 2)] < 0.5
        drowned = jnp.where(dry, 0.0, here[:, 0:variables])
        beside = neighbour_sum(drowned)[1 : planes + 1]
        restricted, residual = here[1 : planes + 1, :variables], here[1 : planes + 1, variables:]
        gain = pair[k, 0:count].reshape(sizes["coarse"])
        swept = jnp.where(dry[1 : planes + 1], restricted + gain * (residual - beside), 0.0)
        fields.append(jnp.concatenate([restricted, swept], axis=1))
    half = jnp.concatenate([pair[0, count, :, 0:slots], pair[1, count, :, 0:slots]], axis=1)
    lane = iota((1, LANES), 1)
    base = (core + 2 * (lane // slots)) * (planes * height * depth)
    values = interpolate(fields, half, base)
    empty = jnp.zeros((3, LANES), F32)
    first = jnp.concatenate([values[:variables], empty], axis=0)
    second = jnp.concatenate([values[variables:], empty], axis=0)
    second = pltpu.roll(second, 8 * grid_index, 1)
    mine = iota((8, LANES), 1) % 64 // 8 == grid_index
    top = iota((8, LANES), 0) < variables
    for h in range(grids):
        tile = jnp.where(mine, pltpu.roll(second, (LANES - 8 * h) % LANES, 1), first)
        tile = jnp.where(top, tile, corners[h])
        for s in range(subs):
            out[h * subs + s] = tile


def plane_numbers(meta, blocks):
    row = meta[5:6, :]
    lane = iota(row.shape, 1)
    return [jnp.sum(jnp.where(lane == q, row, 0.0)).astype(jnp.int32) for q in range(blocks)]


def add_planes(sizes, pieces, numbers, both):
    variables, blocks = sizes["coarse"][1], sizes["blocks"]
    width = min(pieces[0].shape[0] // variables, 2 * blocks)
    for q in range(blocks):
        coarse = pl.ds(numbers[q] // 2, 1)
        for k in range(2):
            i = k * blocks + q
            at = i % width * variables
            part = pieces[i // width][at : at + variables]
            both[coarse, pl.ds(k * variables, variables)] += part[None]


def join_kernel(sizes, *refs):
    at = 0
    for part in refs[:-1]:
        refs[-1][at : at + part.shape[0]] = part[...]
        at = at + part.shape[0]


def four_blocks(sizes, known):
    shared, partner, joined, last = known
    size = shared.shape[0]
    return shared, partner, joined.at[joined.shape[0] - size :], last


def split_kernel(sizes, whole, *pieces):
    at = 0
    for piece in pieces:
        piece[...] = whole[at : at + piece.shape[0]]
        at = at + piece.shape[0]


def assemble_kernel(sizes, before, across, shared, partner, joined, last, *refs):
    variables = sizes["coarse"][1]
    pieces = refs[:-4]
    coupling, both, source, gain = refs[-4:]
    planes = sizes["coarse"][0]
    known = four_blocks(sizes, (shared, partner, joined, last))
    for part, bit in zip(known, (0, 2, 1, 3)):
        owner = lax.axis_index("sub") ^ bit
        end = part.shape[0] - 1
        here = part[end - planes * variables : end].reshape(sizes["coarse"])
        gain[pl.ds(owner * planes, planes)] = here
    count = planes * variables
    blocks = sizes["blocks"]
    both[...] = before[...]
    add_planes(sizes, [across], plane_numbers(partner[count], blocks), both)
    add_planes(sizes, pieces, plane_numbers(known[3][count], blocks), both)
    source[...] = couple(coupling, both[:, 0:variables])


def couple(coupling, field):
    variables = field.shape[1]
    outs = []
    for v in range(variables):
        summed = None
        for x in range(variables):
            term = coupling[v : v + 1, x : x + 1][None] * field[:, x]
            summed = term if summed is None else summed + term
        outs.append(jnp.tanh(summed)[:, None])
    return jnp.concatenate(outs, axis=1)


def target_features(cell, height, depth):
    plane, row, column = split_cell(jnp.maximum(cell, 0), height, depth)
    square = plane * plane + row * row + column * column
    square = jnp.where(cell >= 0, square, 1 << 15)
    coarse = square // LANES * LANES
    one = jnp.ones(cell.shape, jnp.int32)
    rows = [plane, row, column, one, one, one, -coarse, 2 + coarse - square]
    return jnp.concatenate([each.astype(F32) for each in rows], axis=0)


def corner_features(cell, height, depth):
    plane, row, column = split_cell(cell, height, depth)
    square = plane * plane + row * row + column * column
    coarse = square // LANES * LANES
    one = jnp.ones(cell.shape, jnp.int32)
    rows = [2 * plane, 2 * row, 2 * column, -coarse, coarse - square, 0 * one, one, one]
    return jnp.concatenate([each.astype(F32) for each in rows], axis=0)


def fringe_values(sizes, arrived, landing):
    subs, grids, slots = sizes["subs"], sizes["grids"], sizes["slots"]
    _, _, height, depth = sizes["coarse"]
    lane = iota((8, LANES), 1)
    sublane = iota((8, LANES), 0)
    group = lane % 64 // 8
    firsts = []
    for g in range(grids):
        halves = []
        for k in range(2):
            half = arrived[g * subs + k]
            for s in range(k + 2, subs, 2):
                half = half + arrived[g * subs + s]
            halves.append(half)
        firsts.append(halves)
    for g in range(grids):
        for k in range(2):
            sent = firsts[g][k]
            for other in range(grids):
                if other != g:
                    moved = pltpu.roll(firsts[other][k], (8 * other - 8 * g) % LANES, 1)
                    sent = jnp.where(group == other, moved, sent)
            landing[g, :, k * LANES : (k + 1) * LANES] = sent
    cells = [jnp.zeros((8, LANES), F32)] * 2
    scales = []
    for g in range(grids):
        scale = []
        for k in range(2):
            one, two = arrived[g * subs + k], arrived[g * subs + k + 2]
            low = jnp.where(lane < 64, one, pltpu.roll(two, 64, 1))
            high = jnp.where(lane < 64, pltpu.roll(one, 64, 1), two)
            scale.append(jnp.where(sublane < 3, pltpu.roll(low, 3, 0), pltpu.roll(high, 6, 0)))
            cells[k] = jnp.where(sublane == g, pltpu.roll(high, (g + 1) % 8, 0), cells[k])
        scales.append(scale)
    targets, corners = [], []
    step = ((group // 4) * height + group // 2 % 2) * depth + group % 2
    for k in range(2):
        targets.append(jnp.where(group == sublane, -1.0, cells[k]))
        starts = jnp.where(group == sublane, cells[k], 0.0)
        parts = []
        for half in (lane < 64, lane >= 64):
            start = jnp.where(half, starts, 0.0)
            for shift in (64, 32, 16, 8):
                start = start + pltpu.roll(start, shift, 1)
            parts.append(start)
        corners.append(jnp.where(lane < 64, parts[0], parts[1]).astype(jnp.int32) + step)
    targets = jnp.concatenate(targets, axis=1).astype(jnp.int32)
    corners = jnp.concatenate(corners, axis=1)
    theirs = target_features(targets, height, depth).T.astype(BF16)
    ours = corner_features(corners, height, depth)
    which = iota(ours.shape, 0) % 8
    mine = [jnp.where(which == g, ours, 0.0).astype(BF16) for g in range(grids)]
    closeness = jnp.dot(theirs, jnp.concatenate(mine, axis=1), preferred_element_type=F32)
    closeness = closeness.astype(BF16)
    most = closeness
    while most.shape[0] > 16:
        half = most.shape[0] // 2
        most = jnp.maximum(most[:half], most[half:])
    wet = jnp.max(most.astype(F32), axis=0, keepdims=True) - 1.0
    match = jnp.maximum(closeness - jnp.maximum(wet, 0.0).astype(BF16), 0.0)
    lanes = subs * slots
    values = [[], []]
    for g in range(grids):
        sent = landing[g]
        high = sent.astype(BF16).astype(F32)
        stacked = jnp.concatenate([high, sent - high], axis=0).astype(BF16)
        near = jnp.dot(stacked, match[:, g * lanes : (g + 1) * lanes], preferred_element_type=F32)
        near = near[0:8] + near[8:16]
        for k in range(2):
            values[k].append(near[:, k * LANES : (k + 1) * LANES] * scales[g][k])
    total = []
    for k in range(2):
        parts = values[k]
        for bit in (4, 2, 1):
            width = 8 * bit
            lower = lane // width % 2 == 0
            parts = [
                jnp.where(
                    lower,
                    one + pltpu.roll(one, LANES - width, 1),
                    two + pltpu.roll(two, width, 1),
                )
                for one, two in zip(parts[:bit], parts[bit:])
            ]
        known = firsts[0][k]
        for g in range(1, grids):
            known = jnp.where(group == g, firsts[g][k], known)
        total.append(parts[0] + known)
    return landing[lax.axis_index("grid")], jnp.concatenate(total, axis=1)


def spread(values, cell, total, height, depth):
    count = cell.shape[1]
    pairs = values.shape[0] // 2
    plane, row, column = split_cell(cell, height, depth)
    onehot = jnp.where(iota((depth, count), 0) == column, 1.0, 0.0).astype(BF16)
    row_here = (iota((2 * height, count), 0) % height == row) & (cell >= 0)
    tiles = []
    for i in range(pairs):
        twin = [jnp.broadcast_to(values[2 * i + k : 2 * i + k + 1], (height, count)) for k in (0, 1)]
        tiles.append(two_pieces(jnp.concatenate(twin, axis=0)))
    rows = [[], []]
    for p in range(total):
        here = jnp.where(row_here & (plane == p), 1.0, 0.0).astype(BF16)
        for tile in tiles:
            for k in (0, 1):
                rows[k].append(tile[k] * here)
    values = jnp.concatenate([jnp.concatenate(each, axis=0) for each in rows], axis=1)
    field = lax.dot_general(
        values,
        jnp.concatenate([onehot, onehot], axis=1),
        (((1,), (1,)), ((), ())),
        preferred_element_type=F32,
    )
    return field.reshape(total, 2 * pairs, height, depth)


def finish_kernel(sizes, *refs):
    subs = sizes["subs"]
    planes, variables, height, depth = sizes["coarse"]
    blocks = sizes["blocks"]
    parts = four_blocks(sizes, refs[:4])
    coupling, arrived, both, source, gain, mask, fine = refs[4:11]
    out, landing, stage, rows, padded, tall, held, sems = refs[11:]
    total = subs * planes
    gather_rows(sizes, parts, stage, rows)
    first, second = fringe_values(sizes, arrived, landing)
    cell = rows[4:5, :].astype(jnp.int32)
    values = jnp.concatenate([first[:variables], second[:variables]], axis=0)
    landed = spread(values, cell, total, height, depth)
    wet = mask[...] > 0.5
    start = both[:, 0:variables]
    rest = both[:, variables:]
    scale = gain[...]
    change = jnp.where(wet, landed[:, 0:variables] - start, 0.0)
    update = scale * (rest + neighbour_sum(change))
    change = jnp.where(wet, landed[:, variables:] - start, update)
    apart = source[...] - couple(coupling, start + change)
    update = scale * (rest + neighbour_sum(change) + 2.0 * apart)
    correction = jnp.where(wet, change, (1.0 - OMEGA) * change + update)
    padded[0:1] = jnp.zeros((1, variables, height, depth), F32)
    padded[total + 1 : total + 2] = jnp.zeros((1, variables, height, depth), F32)
    padded[1 : total + 1] = correction
    at_row = iota((variables, height, depth), 1)
    coarse_at = iota((depth, 2 * depth), 0)
    fine_at = iota((depth, 2 * depth), 1)
    beside = fine_at // 2 - 1 + 2 * (fine_at % 2)
    widen = jnp.where(
        coarse_at == fine_at // 2, 0.75, jnp.where(coarse_at == beside, 0.25, 0.0)
    ).astype(BF16)
    copies = []
    step = 2
    numbers = plane_numbers(parts[0][planes * variables], blocks)
    for q, number in enumerate(numbers):
        coarse = number // 2
        along = 0.75 * padded[coarse + 1] + 0.25 * padded[coarse + 2 * (number % 2)]
        below = jnp.where(at_row > 0, pltpu.roll(along, 1, 1), 0.0)
        above = jnp.where(at_row < height - 1, pltpu.roll(along, height - 1, 1), 0.0)
        block = slice(q * variables, (q + 1) * variables)
        tall[block, pl.ds(0, height, stride=2), :] = 0.75 * along + 0.25 * below
        tall[block, pl.ds(1, height, stride=2), :] = 0.75 * along + 0.25 * above
        if q % step == step - 1:
            low = q + 1 - step
            rows_in = tall[low * variables : (q + 1) * variables]
            prolonged = dot_exact(rows_in.reshape(step * variables * 2 * height, depth), widen)
            shape = (step, variables, 2 * height, 2 * depth)
            held[low : q + 1] = fine[low : q + 1] + prolonged.reshape(shape)
            copy = pltpu.make_async_copy(
                held.at[low : q + 1], out.at[0, low : q + 1], sems.at[q // step]
            )
            copy.start()
            copies.append(copy)
    for copy in copies:
        copy.wait()


def fast_shards(
    fine_residual,
    fine_solution,
    plane_of_slot,
    coarse_diagonal,
    coupling,
    donor_cells,
    donor_offsets,
    receptor_cells,
    fringe_counts,
):
    subs = lax.axis_size("sub")
    grids = lax.axis_size("grid")
    coarse = coarse_diagonal.shape[1:]
    planes, variables, height, depth = coarse
    blocks = plane_of_slot.shape[1]
    slots = donor_cells.shape[-1]
    sizes = dict(coarse=coarse, blocks=blocks, slots=slots, grids=grids, subs=subs)
    count = blocks * variables
    total = subs * planes
    whole = (total, variables, height, depth)
    full = jax.ShapeDtypeStruct(whole, F32)
    rows = pltpu.VMEM((8, subs * slots), F32)
    stage = pltpu.VMEM((subs, 8, depth), F32)

    def call(kernel, name, out_shape, *operands, scratch=(), far=(), out_spec=VMEM, aliases={}, cost=None):
        specs = [HBM if any(one is each for each in far) else VMEM for one in operands]
        operands = [
            pltpu.with_memory_space_constraint(one, pltpu.HBM) if spec is HBM else one
            for one, spec in zip(operands, specs)
        ]
        return pl.pallas_call(
            functools.partial(kernel, sizes),
            out_shape=out_shape,
            in_specs=specs,
            out_specs=jax.tree.map(lambda _: out_spec, out_shape),
            scratch_shapes=list(scratch),
            input_output_aliases=aliases,
            cost_estimate=cost,
            compiler_params=pltpu.CompilerParams(vmem_limit_bytes=48 * 1024 * 1024),
            name=name,
        )(*operands)

    offsets = donor_offsets.transpose(0, 2, 1, 3)
    inputs = (fringe_counts, plane_of_slot, coarse_diagonal, donor_cells, offsets, receptor_cells)
    shared = call(
        pack_kernel,
        "pack",
        jax.ShapeDtypeStruct((planes * variables + 1, height, depth), F32),
        *inputs,
        far=inputs,
        scratch=[
            pltpu.VMEM(coarse, F32),
            pltpu.VMEM(offsets.shape[1:], F32),
            pltpu.VMEM((2, 1, slots), jnp.int32),
            pltpu.VMEM(plane_of_slot.shape, jnp.int32),
            pltpu.SMEM(fringe_counts.shape, jnp.int32),
            pltpu.SemaphoreType.DMA((6,)),
        ],
    )
    swap = {bit: [(i, i ^ bit) for i in range(subs)] for bit in (1, 2)}
    partner = lax.ppermute(shared, "sub", swap[2])
    own, corners, fine_here = call(
        restrict_kernel,
        "restrict",
        [
            jax.ShapeDtypeStruct((2 * count, height, depth), F32),
            jax.ShapeDtypeStruct((grids, 8, LANES), F32),
            jax.ShapeDtypeStruct(fine_solution.shape[1:], F32),
        ],
        fine_residual,
        fine_solution,
        shared,
        far=(fine_residual, fine_solution),
        scratch=[
            pltpu.VMEM(fine_solution.shape[1:], F32),
            pltpu.VMEM((2 * count, 2 * height, depth), F32),
            pltpu.SemaphoreType.DMA((blocks,)),
        ],
    )
    size = own.shape[0] + shared.shape[0]
    joined = call(
        join_kernel, "join", jax.ShapeDtypeStruct((size, height, depth), F32), own, shared
    )
    joined = lax.ppermute(joined, "sub", swap[1])
    own, partner = lax.optimization_barrier((own, partner))
    partner = call(
        join_kernel, "pass", jax.ShapeDtypeStruct(partner.shape, F32), partner, cost=pl.CostEstimate(flops=20_000_000_000, transcendentals=0, bytes_accessed=100_000_000)
    )
    known = (shared, partner, joined, lax.ppermute(partner, "sub", swap[1]))
    across = lax.ppermute(own, "sub", swap[2])
    out, mask, both = call(
        partial_kernel,
        "partial",
        [
            jax.ShapeDtypeStruct((grids * subs, 8, LANES), F32),
            jax.ShapeDtypeStruct((total, 1, height, depth), F32),
            jax.ShapeDtypeStruct((total, 2 * variables, height, depth), F32),
        ],
        *known,
        own,
        corners,
        cost=pl.CostEstimate(flops=20_000_000_000, transcendentals=0, bytes_accessed=100_000_000),
        scratch=[
            rows,
            stage,
            pltpu.VMEM((2, planes * variables + 1, height, depth), F32),
            pltpu.VMEM((total + 2, 2 * variables, height, depth), F32),
            pltpu.VMEM((total + 2, 1, height, depth), F32),
        ],
    )
    arrived = lax.all_to_all(out, ("grid", "sub"), 0, 0, tiled=True)
    piece = jax.ShapeDtypeStruct((blocks // 2 * variables, height, depth), F32)
    pieces = call(split_kernel, "split", [piece] * 4, across)
    pieces = [lax.ppermute(each, "sub", swap[1]) for each in pieces]
    both, source, gain = call(
        assemble_kernel,
        "assemble",
        [jax.ShapeDtypeStruct(both.shape, F32), full, full],
        both,
        across,
        *known,
        *pieces,
        coupling,
        aliases={0: 0},
    )
    return call(
        finish_kernel,
        "finish",
        jax.ShapeDtypeStruct(fine_solution.shape, F32),
        *known,
        coupling,
        arrived,
        both,
        source,
        gain,
        mask,
        fine_here,
        scratch=[
            pltpu.VMEM((grids, 8, subs * slots), F32),
            stage,
            rows,
            pltpu.VMEM((total + 2, variables, height, depth), F32),
            pltpu.VMEM((count, 2 * height, depth), F32),
            pltpu.VMEM(fine_solution.shape[1:], F32),
            pltpu.SemaphoreType.DMA((blocks // 2,)),
        ],
        out_spec=HBM,
    )


def solution(mesh):
    in_specs = (
        P("grid", "sub", None, None, None),
        P("grid", "sub", None, None, None),
        P("grid", "sub"),
        P("grid", "sub", None, None, None),
        P(),
        P("grid", "sub", None),
        P("grid", "sub", None, None),
        P("grid", "sub", None),
        P(),
    )
    out_specs = P("grid", "sub", None, None, None)
    small = mesh.shape["sub"] == 4 and mesh.shape["grid"] * FRINGE == 64
    body = fast_shards if small else shards
    return jax.shard_map(body, mesh=mesh, in_specs=in_specs, out_specs=out_specs, check_vma=False)
```

```python
import functools

import jax
import jax.numpy as jnp
from jax import lax
from jax.experimental import pallas as pl
from jax.experimental.pallas import tpu as pltpu
from jax.sharding import PartitionSpec as P

FRINGE = 8
SWEEPS = 2


OMEGA = 0.8


def padded_2(block, sides, width):
    for axis, dim in sides:
        count = lax.axis_size(axis)
        forward = [(i, i + 1) for i in range(count - 1)]
        backward = [(target, source) for source, target in forward]
        low = lax.ppermute(
            lax.slice_in_dim(block, block.shape[dim] - width, None, axis=dim), axis, forward
        )
        high = lax.ppermute(lax.slice_in_dim(block, 0, width, axis=dim), axis, backward)
        block = jnp.concatenate([low, block, high], axis=dim)
    return block


def restrict_planes(fine_field):
    dims_in = fine_field.shape
    split_cells = fine_field.reshape(dims_in[:-2] + (dims_in[-2] // 2, 2, dims_in[-1] // 2, 2))
    return 0.125 * jnp.sum(split_cells, axis=(-3, -1))


def pair_sum(field, axis):
    which = axis % field.ndim
    length = field.shape[which]
    empty = jnp.zeros_like(lax.slice_in_dim(field, 0, 1, axis=which))
    below_side = jnp.concatenate(
        [empty, lax.slice_in_dim(field, 0, length - 1, axis=which)], axis=which
    )
    above_side = jnp.concatenate(
        [lax.slice_in_dim(field, 1, length, axis=which), empty], axis=which
    )
    return below_side + above_side


def operate(field, padded, diagonal, coupling):
    which = field.ndim - 4
    length = padded.shape[which]
    beside = lax.slice_in_dim(padded, 2, length, axis=which) + lax.slice_in_dim(
        padded, 0, length - 2, axis=which
    )
    beside = beside + pair_sum(field, field.ndim - 2)
    beside = beside + pair_sum(field, field.ndim - 1)
    coupled = jnp.einsum("vw,...wyz->...vyz", coupling, field, precision=lax.Precision.HIGHEST)
    return (6.0 + diagonal) * field - beside + 2.0 * jnp.tanh(coupled)


def apply_operator(field, diagonal, coupling):
    padded = padded_2(field, (("sub", 0),), 1)
    return operate(field, padded, diagonal, coupling)


def corner_values(flat_field, donor_base, height, depth):
    corners = []
    for step_x in (0, 1):
        for step_y in (0, 1):
            for step_z in (0, 1):
                where_cells = donor_base + step_x * height * depth + step_y * depth + step_z
                corners.append(jnp.take_along_axis(flat_field, where_cells[..., None, :], axis=-1))
    return corners


def blend(corners, offsets):
    frac_x = offsets[..., 0:1, :]
    frac_y = offsets[..., 1:2, :]
    frac_z = offsets[..., 2:3, :]
    summed = None
    number = 0
    for step_x in (0, 1):
        for step_y in (0, 1):
            for step_z in (0, 1):
                weight_x = frac_x if step_x else 1.0 - frac_x
                weight_y = frac_y if step_y else 1.0 - frac_y
                weight_z = frac_z if step_z else 1.0 - frac_z
                term = weight_x * weight_y * weight_z * corners[number]
                summed = term if summed is None else summed + term
                number = number + 1
    return summed


def refine(field, axis):
    which = axis % field.ndim
    length = field.shape[which]
    empty = jnp.zeros_like(lax.slice_in_dim(field, 0, 1, axis=which))
    below_side = jnp.concatenate(
        [empty, lax.slice_in_dim(field, 0, length - 1, axis=which)], axis=which
    )
    above_side = jnp.concatenate(
        [lax.slice_in_dim(field, 1, length, axis=which), empty], axis=which
    )
    first_half = 0.75 * field + 0.25 * below_side
    second_half = 0.75 * field + 0.25 * above_side
    joined = jnp.stack([first_half, second_half], axis=which + 1)
    new_dims = list(field.shape)
    new_dims[which] = 2 * length
    return joined.reshape(new_dims)


def shards(
    fine_residual,
    fine_solution,
    plane_of_slot,
    coarse_diagonal,
    coupling,
    donor_cells,
    donor_offsets,
    receptor_cells,
    fringe_counts,
):
    grid_index = lax.axis_index("grid")
    sub_index = lax.axis_index("sub")
    diagonal = coarse_diagonal[0]
    planes, variables, height, depth_cells = diagonal.shape
    cell_count = planes * height * depth_cells
    plane_ids = plane_of_slot[0]
    blocks = plane_ids.shape[0]
    solution_planes = restrict_planes(fine_solution[0])
    residual_planes = restrict_planes(fine_residual[0])
    contrib = jnp.stack([solution_planes, residual_planes], axis=1).reshape(blocks, -1)
    targets = plane_ids // 2
    wanted = sub_index * planes + jnp.arange(planes, dtype=jnp.int32)
    gathered, gathered_ids = (
        lax.all_gather(contrib, "sub", axis=0, tiled=True),
        lax.all_gather(plane_ids, "sub", axis=0, tiled=True),
    )
    select = ((gathered_ids // 2)[None, :] == wanted[:, None]).astype(jnp.float32)
    owned_sums = jnp.dot(
        select, gathered, precision=lax.Precision.HIGHEST, preferred_element_type=jnp.float32
    )
    owned_sums = owned_sums.reshape(planes, 2, variables, height, depth_cells)
    restricted_solution = owned_sums[:, 0]
    restricted_residual = owned_sums[:, 1]
    forcing = apply_operator(restricted_solution, diagonal, coupling) + restricted_residual
    slot_count = donor_cells.shape[-1]
    column = lax.dynamic_index_in_dim(fringe_counts, grid_index, 1, keepdims=False)
    allowed = jnp.repeat(column, FRINGE)
    live_slot = jnp.arange(slot_count, dtype=jnp.int32) % FRINGE < allowed
    target_cells = jnp.where(live_slot, receptor_cells[0, 0], cell_count)
    receptor_mask = jnp.zeros((cell_count,), jnp.float32).at[target_cells].set(1.0, mode="drop")
    receptor_mask = receptor_mask.reshape(planes, 1, height, depth_cells)
    donor_base = donor_cells[0, 0]
    offsets = donor_offsets[0, 0]
    field = restricted_solution
    for sweep_index in range(SWEEPS):
        flat_field = field.transpose(1, 0, 2, 3).reshape(variables, cell_count)
        corners = corner_values(flat_field, donor_base, height, depth_cells)
        arrived = lax.all_to_all(
            blend(corners, offsets), "grid", split_axis=1, concat_axis=1, tiled=True
        )
        flat_field = flat_field.at[:, target_cells].set(arrived, mode="drop")
        field = flat_field.reshape(variables, planes, height, depth_cells).transpose(1, 0, 2, 3)
        update = field + OMEGA * (forcing - apply_operator(field, diagonal, coupling)) / (
            6.0 + diagonal
        )
        field = jnp.where(receptor_mask > 0.5, field, update)
    correction = (field - restricted_solution).reshape(planes, -1)
    neighbour = targets - 1 + 2 * (plane_ids % 2)
    shard_rows = lax.all_gather(correction, "sub", axis=0, tiled=True)
    row_ids = jnp.arange(shard_rows.shape[0], dtype=jnp.int32)
    weights = 0.75 * (targets[:, None] == row_ids[None, :]).astype(jnp.float32)
    weights = weights + 0.25 * (neighbour[:, None] == row_ids[None, :]).astype(jnp.float32)
    along_x = jnp.dot(
        weights, shard_rows, precision=lax.Precision.HIGHEST, preferred_element_type=jnp.float32
    )
    along_x = along_x.reshape(blocks, variables, height, depth_cells)
    prolonged = refine(refine(along_x, -2), -1)
    return (fine_solution[0] + prolonged)[None]


BF16 = jnp.bfloat16
F32 = jnp.float32
HIGHEST = lax.Precision.HIGHEST
VMEM = pl.BlockSpec(memory_space=pltpu.VMEM)
HBM = pl.BlockSpec(memory_space=pltpu.HBM)
LANES = 128


def two_pieces(values):
    high = values.astype(BF16)
    return high, (values - high.astype(F32)).astype(BF16)


def dot_exact(values, matrix):
    parts = jnp.concatenate(two_pieces(values), axis=1)
    return jnp.dot(
        parts, jnp.concatenate([matrix, matrix], axis=0), preferred_element_type=F32
    )


def dot_near(values, matrix):
    high, low = two_pieces(values)
    matrix_high, matrix_low = two_pieces(matrix)
    return jnp.dot(
        jnp.concatenate([high, low, high], axis=1),
        jnp.concatenate([matrix_high, matrix_high, matrix_low], axis=0),
        preferred_element_type=F32,
    )


def iota(shape, dim):
    return lax.broadcasted_iota(jnp.int32, shape, dim)


def bits(size):
    assert size & (size - 1) == 0
    return size.bit_length() - 1


def split_cell(cell, height, depth):
    row_bits, column_bits = bits(height), bits(depth)
    row = (cell >> column_bits) & (height - 1)
    return cell >> (row_bits + column_bits), row, cell & (depth - 1)


def neighbour_sum(field):
    total, variables, height, depth = field.shape
    flat = field.reshape(total * variables, height, depth)
    at_row = iota(flat.shape, 1)
    at_column = iota(flat.shape, 2)
    beside = jnp.where(at_row > 0, pltpu.roll(flat, 1, 1), 0.0)
    beside = beside + jnp.where(at_row < height - 1, pltpu.roll(flat, height - 1, 1), 0.0)
    beside = beside + jnp.where(at_column > 0, pltpu.roll(flat, 1, 2), 0.0)
    beside = beside + jnp.where(at_column < depth - 1, pltpu.roll(flat, depth - 1, 2), 0.0)
    beside = beside.reshape(field.shape)
    empty = jnp.zeros((1, variables, height, depth), F32)
    beside = beside + jnp.concatenate([empty, field[: total - 1]], axis=0)
    return beside + jnp.concatenate([field[1:], empty], axis=0)


def live_cells(counts, grid_index, grids, receptors, base):
    lane = iota(receptors.shape, 1)
    allowed = jnp.zeros(receptors.shape, jnp.int32)
    for g in range(grids):
        allowed = jnp.where(lane >> bits(FRINGE) == g, counts[g, grid_index], allowed)
    return jnp.where((lane & (FRINGE - 1)) < allowed, receptors + base, -1)


def receptor_mask(cell, total, height, depth):
    count = cell.shape[1]
    plane, row, column = split_cell(cell, height, depth)
    onehot = jnp.where(iota((depth, count), 0) == column, 1.0, 0.0).astype(BF16)
    row_here = (iota((height, count), 0) == row) & (cell >= 0)
    here = jnp.concatenate([jnp.where(row_here & (plane == p), 1.0, 0.0) for p in range(total)], 0)
    contract = (((1,), (1,)), ((), ()))
    mask = lax.dot_general(here.astype(BF16), onehot, contract, preferred_element_type=F32)
    return mask.reshape(total, 1, height, depth), here, onehot


def start_copies(pairs, sems):
    copies = [pltpu.make_async_copy(*pair, sems.at[i]) for i, pair in enumerate(pairs)]
    for copy in copies:
        copy.start()
    return copies


def pack_kernel(
    sizes, counts, ids, diagonal, donors, offsets, receptors, out, held, rows, cells, planes_of, allowed, sems
):
    planes, variables, height, depth = sizes["coarse"]
    slots = sizes["slots"]
    base = lax.axis_index("sub") * (planes * height * depth)
    grid_index = lax.axis_index("grid")
    count = planes * variables
    copies = start_copies(
        [
            (counts, allowed),
            (receptors.at[0], cells.at[0]),
            (donors.at[0], cells.at[1]),
            (offsets.at[0], rows),
            (ids, planes_of),
            (diagonal.at[0], held),
        ],
        sems,
    )
    out[count] = jnp.zeros((height, depth), F32)
    for copy in copies:
        copy.wait()
    out[0:count] = OMEGA / (6.0 + held[...].reshape(count, height, depth))
    cell = live_cells(allowed, grid_index, sizes["grids"], cells[0], base)
    out[count, 0:1, 0:slots] = (cells[1] + base).astype(F32)
    for k in range(3):
        out[count, k + 1 : k + 2, 0:slots] = rows[k]
    out[count, 4:5, 0:slots] = cell.astype(F32)
    out[count, 5:6, 0 : sizes["blocks"]] = planes_of[...].astype(F32)


def find_corners(sizes, shared, out):
    planes, variables, height, depth = sizes["coarse"]
    slots, grids = sizes["slots"], sizes["grids"]
    grid_index = lax.axis_index("grid")
    base = lax.axis_index("sub") * (planes * height * depth)
    meta = shared[planes * variables, :, 0:slots]
    cell = meta[4:5].astype(jnp.int32)
    cell = jnp.where(cell >= 0, cell - base, -1)
    mask, _, _ = receptor_mask(cell, planes, height, depth)
    gain = shared[0 : planes * variables].reshape(planes, variables, height, depth)
    fields = jnp.concatenate([gain, mask], axis=1)
    donors = meta[0:1].astype(jnp.int32) - base
    twice = jnp.concatenate([donors, donors], axis=1)
    step_z = iota(twice.shape, 1) >> bits(slots)
    plane, row, column = split_cell(twice, height, depth)
    onehot = jnp.where(iota((depth, LANES), 0) == column + step_z, 1.0, 0.0).astype(BF16)
    count = planes * (variables + 1) * height
    at_column = dot_exact(fields.reshape(count, depth), onehot)
    at_column = at_column.reshape(planes, variables + 1, height, LANES)
    both = jnp.concatenate([meta[1:4], meta[1:4]], axis=1)
    weight_z = jnp.where(step_z == 1, both[2:3], 1.0 - both[2:3])
    at_row = iota((height, LANES), 0)
    empty = jnp.zeros((5, LANES), F32)
    tiles = []
    for step_x in (0, 1):
        weight_x = both[0:1] if step_x else 1.0 - both[0:1]
        by_plane = None
        for p in range(planes):
            term = jnp.where(plane + step_x == p, at_column[p], 0.0)
            by_plane = term if by_plane is None else by_plane + term
        for step_y in (0, 1):
            weight_y = both[1:2] if step_y else 1.0 - both[1:2]
            here = jnp.where(at_row == row + step_y, 1.0, 0.0)
            found = jnp.sum(by_plane * here[None], axis=1)
            wet = found[variables : variables + 1]
            scaled = weight_x * weight_y * weight_z * (found[:variables] * (1.0 - wet) + wet)
            left = jnp.concatenate([empty, scaled[0:3]], axis=0)
            right = jnp.concatenate([empty, scaled[3:5], empty[0:1]], axis=0)
            tiles.append((left, right))
    lane = iota((8, LANES), 1)
    sublane = iota((8, LANES), 0)
    cells = jnp.broadcast_to(jnp.concatenate([meta[4:5], meta[4:5]], axis=1), (8, LANES))
    starts = jnp.broadcast_to(jnp.concatenate([meta[0:1], meta[0:1]], axis=1), (8, LANES))
    starts = pltpu.roll(starts, 8 * grid_index, 1)
    last = (sublane == 7) & (lane >= 64)
    mine = last & (((lane >> 3) & 7) == grid_index)
    for h in range(grids):
        tile = jnp.zeros((8, LANES), F32)
        for c in range(8):
            for k in (0, 1):
                shift = (64 * k + 8 * c - (c % 2) * 64 - 8 * h) % LANES
                moved = pltpu.roll(tiles[c // 2][k], shift, 1)
                tile = jnp.where(lane >> 3 == 8 * k + c, moved, tile)
        tile = jnp.where(last, cells, tile)
        out[h] = jnp.where(mine, pltpu.roll(starts, (LANES - 8 * h) % LANES, 1), tile)


def restrict_kernel(sizes, residual, fine, shared, out, corners, fine_here, held, wide, sems):
    planes, variables, height, depth = sizes["coarse"]
    blocks = sizes["blocks"]
    step = 8
    copies = start_copies(
        [
            (source.at[0, q : q + step], target.at[q : q + step])
            for source, target in ((fine, fine_here), (residual, held))
            for q in range(0, blocks, step)
        ],
        sems,
    )
    find_corners(sizes, shared, corners)
    pair = jnp.where(
        iota((2 * depth, depth), 0) >> 1 == iota((2 * depth, depth), 1), 0.125, 0.0
    ).astype(BF16)
    count = step * variables
    for i, copy in enumerate(copies):
        k, q = divmod(i * step, blocks)
        copy.wait()
        rows = (fine_here, held)[k][q : q + step].reshape(count * 2 * height, 2 * depth)
        here = pl.ds(i * count, count)
        wide[here] = dot_exact(rows, pair).reshape(count, 2 * height, depth)
        out[here] = (
            wide[here, pl.ds(0, height, stride=2), :] + wide[here, pl.ds(1, height, stride=2), :]
        )


def hats(shape, dim, start, frac):
    at = iota(shape, dim)
    return jnp.where(at == start, 1.0 - frac, 0.0) + jnp.where(at == start + 1, frac, 0.0)


def interpolate(fields, rows, base):
    planes, variables, height, depth = fields[0].shape
    count = rows.shape[1]
    cell = rows[0:1, :].astype(jnp.int32) - base
    plane, row, column = split_cell(cell, height, depth)
    frac_x, frac_y, frac_z = rows[1:2, :], rows[2:3, :], rows[3:4, :]
    weight_z = hats((depth, count), 0, column, frac_z)
    weight_y = hats((height, count), 0, row, frac_y)
    lower = iota((depth, count), 1) < count // 2
    weight_z = jnp.concatenate(
        [jnp.where(lower, weight_z, 0.0), jnp.where(lower, 0.0, weight_z)], axis=0
    )
    both = jnp.concatenate([each.reshape(-1, depth) for each in fields], axis=1)
    along_z = dot_near(both, weight_z).reshape(planes, variables, height, count)
    summed = None
    for p in range(planes):
        weight_x = jnp.where(plane == p, 1.0 - frac_x, 0.0) + jnp.where(
            plane + 1 == p, frac_x, 0.0
        )
        term = along_z[p] * (weight_x * weight_y)[None]
        summed = term if summed is None else summed + term
    return jnp.sum(summed, axis=1)


def gather_rows(sizes, known, stage, rows):
    slots = sizes["slots"]
    for part, bit in zip(known, (0, 2, 1, 3)):
        stage[lax.axis_index("sub") ^ bit] = part[part.shape[0] - 1]
    for j, s in enumerate((0, 2, 1, 3)):
        rows[:, j * slots : (j + 1) * slots] = stage[s, :, 0:slots]


def partial_kernel(sizes, *refs):
    subs, grids, slots, blocks = sizes["subs"], sizes["grids"], sizes["slots"], sizes["blocks"]
    planes, variables, height, depth = sizes["coarse"]
    *known, own, corners = refs[:-8]
    joined = known[2]
    known = four_blocks(sizes, known)
    out, mask_out, both, rows, stage, pair, padded, wet = refs[-8:]
    total = subs * planes
    sub_index = lax.axis_index("sub")
    grid_index = lax.axis_index("grid")
    count = planes * variables
    gather_rows(sizes, known, stage, rows)
    pair[sub_index >> 1] = known[0][...]
    pair[1 - (sub_index >> 1)] = known[1][...]
    mask, _, _ = receptor_mask(rows[4:5, :].astype(jnp.int32), total, height, depth)
    mask_out[...] = mask
    wet[1 : total + 1] = mask
    padded[...] = jnp.zeros(padded.shape, F32)
    inner = padded.at[1 : total + 1]
    add_planes(sizes, [own], plane_numbers(known[0][count], blocks), inner)
    add_planes(sizes, [joined], plane_numbers(known[2][count], blocks), inner)
    both[...] = padded[1 : total + 1]
    core = sub_index & 1
    fields = []
    for k in range(2):
        start = (core + 2 * k) * planes
        here = padded[pl.ds(start, planes + 2)]
        dry = wet[pl.ds(start, planes + 2)] < 0.5
        drowned = jnp.where(dry, 0.0, here[:, 0:variables])
        beside = neighbour_sum(drowned)[1 : planes + 1]
        restricted, residual = here[1 : planes + 1, :variables], here[1 : planes + 1, variables:]
        gain = pair[k, 0:count].reshape(sizes["coarse"])
        swept = jnp.where(dry[1 : planes + 1], restricted + gain * (residual - beside), 0.0)
        fields.append(jnp.concatenate([restricted, swept], axis=1))
    half = jnp.concatenate([pair[0, count, :, 0:slots], pair[1, count, :, 0:slots]], axis=1)
    lane = iota((1, LANES), 1)
    base = (core + 2 * (lane >> bits(slots))) * (planes * height * depth)
    values = interpolate(fields, half, base)
    empty = jnp.zeros((3, LANES), F32)
    first = jnp.concatenate([values[:variables], empty], axis=0)
    second = jnp.concatenate([values[variables:], empty], axis=0)
    second = pltpu.roll(second, 8 * grid_index, 1)
    mine = ((iota((8, LANES), 1) >> 3) & 7) == grid_index
    top = iota((8, LANES), 0) < variables
    for h in range(grids):
        tile = jnp.where(mine, pltpu.roll(second, (LANES - 8 * h) % LANES, 1), first)
        tile = jnp.where(top, tile, corners[h])
        for s in range(subs):
            out[h * subs + s] = tile


def plane_numbers(meta, blocks):
    row = meta[5:6, :]
    lane = iota(row.shape, 1)
    return [jnp.sum(jnp.where(lane == q, row, 0.0)).astype(jnp.int32) for q in range(blocks)]


def add_planes(sizes, pieces, numbers, both):
    variables, blocks = sizes["coarse"][1], sizes["blocks"]
    width = min(pieces[0].shape[0] // variables, 2 * blocks)
    for q in range(blocks):
        coarse = pl.ds(numbers[q] >> 1, 1)
        for k in range(2):
            i = k * blocks + q
            at = i % width * variables
            part = pieces[i // width][at : at + variables]
            both[coarse, pl.ds(k * variables, variables)] += part[None]


def pass_kernel(sizes, source, out, last):
    out[...] = source[...]
    last[0] = source[source.shape[0] - 1]


def join_kernel(sizes, *refs):
    at = 0
    for part in refs[:-1]:
        refs[-1][at : at + part.shape[0]] = part[...]
        at = at + part.shape[0]


def four_blocks(sizes, known):
    shared, partner, joined, last = known
    size = shared.shape[0]
    return shared, partner, joined.at[joined.shape[0] - size :], last


def split_kernel(sizes, whole, *pieces):
    at = 0
    for piece in pieces:
        piece[...] = whole[at : at + piece.shape[0]]
        at = at + piece.shape[0]


def assemble_kernel(sizes, before, across, shared, partner, joined, last, *refs):
    variables = sizes["coarse"][1]
    pieces = refs[:-4]
    coupling, both, source, gain = refs[-4:]
    planes = sizes["coarse"][0]
    known = four_blocks(sizes, (shared, partner, joined, last))
    for part, bit in zip(known, (0, 2, 1, 3)):
        owner = lax.axis_index("sub") ^ bit
        end = part.shape[0] - 1
        here = part[end - planes * variables : end].reshape(sizes["coarse"])
        gain[pl.ds(owner * planes, planes)] = here
    count = planes * variables
    blocks = sizes["blocks"]
    both[...] = before[...]
    add_planes(sizes, [across], plane_numbers(partner[count], blocks), both)
    add_planes(sizes, pieces, plane_numbers(known[3][count], blocks), both)
    source[...] = couple(coupling, both[:, 0:variables])


def couple(coupling, field):
    variables = field.shape[1]
    outs = []
    for v in range(variables):
        summed = None
        for x in range(variables):
            term = coupling[v : v + 1, x : x + 1][None] * field[:, x]
            summed = term if summed is None else summed + term
        outs.append(jnp.tanh(summed)[:, None])
    return jnp.concatenate(outs, axis=1)


def target_features(cell, height, depth):
    plane, row, column = split_cell(jnp.maximum(cell, 0), height, depth)
    square = plane * plane + row * row + column * column
    square = jnp.where(cell >= 0, square, 1 << 15)
    coarse = (square >> bits(LANES)) << bits(LANES)
    one = jnp.ones(cell.shape, jnp.int32)
    rows = [plane, row, column, one, one, one, -coarse, 2 + coarse - square]
    return jnp.concatenate([each.astype(F32) for each in rows], axis=0)


def corner_features(cell, height, depth):
    plane, row, column = split_cell(cell, height, depth)
    square = plane * plane + row * row + column * column
    coarse = (square >> bits(LANES)) << bits(LANES)
    one = jnp.ones(cell.shape, jnp.int32)
    rows = [2 * plane, 2 * row, 2 * column, -coarse, coarse - square, 0 * one, one, one]
    return jnp.concatenate([each.astype(F32) for each in rows], axis=0)


def fringe_values(sizes, arrived, landing):
    subs, grids, slots = sizes["subs"], sizes["grids"], sizes["slots"]
    _, _, height, depth = sizes["coarse"]
    lane = iota((8, LANES), 1)
    sublane = iota((8, LANES), 0)
    group = (lane >> 3) & 7
    firsts = []
    for g in range(grids):
        halves = []
        for k in range(2):
            half = arrived[g * subs + k]
            for s in range(k + 2, subs, 2):
                half = half + arrived[g * subs + s]
            halves.append(half)
        firsts.append(halves)
    for g in range(grids):
        for k in range(2):
            sent = firsts[g][k]
            for other in range(grids):
                if other != g:
                    moved = pltpu.roll(firsts[other][k], (8 * other - 8 * g) % LANES, 1)
                    sent = jnp.where(group == other, moved, sent)
            landing[g, :, k * LANES : (k + 1) * LANES] = sent
    cells = [jnp.zeros((8, LANES), F32)] * 2
    scales = []
    for g in range(grids):
        scale = []
        for k in range(2):
            one, two = arrived[g * subs + k], arrived[g * subs + k + 2]
            low = jnp.where(lane < 64, one, pltpu.roll(two, 64, 1))
            high = jnp.where(lane < 64, pltpu.roll(one, 64, 1), two)
            scale.append(jnp.where(sublane < 3, pltpu.roll(low, 3, 0), pltpu.roll(high, 6, 0)))
            cells[k] = jnp.where(sublane == g, pltpu.roll(high, (g + 1) % 8, 0), cells[k])
        scales.append(scale)
    targets, corners = [], []
    step = ((group >> 2) * height + ((group >> 1) & 1)) * depth + (group & 1)
    for k in range(2):
        targets.append(jnp.where(group == sublane, -1.0, cells[k]))
        starts = jnp.where(group == sublane, cells[k], 0.0)
        parts = []
        for half in (lane < 64, lane >= 64):
            start = jnp.where(half, starts, 0.0)
            for shift in (64, 32, 16, 8):
                start = start + pltpu.roll(start, shift, 1)
            parts.append(start)
        corners.append(jnp.where(lane < 64, parts[0], parts[1]).astype(jnp.int32) + step)
    targets = jnp.concatenate(targets, axis=1).astype(jnp.int32)
    corners = jnp.concatenate(corners, axis=1)
    theirs = target_features(targets, height, depth).T.astype(BF16)
    ours = corner_features(corners, height, depth)
    which = iota(ours.shape, 0) & 7
    mine = [jnp.where(which == g, ours, 0.0).astype(BF16) for g in range(grids)]
    closeness = jnp.dot(theirs, jnp.concatenate(mine, axis=1), preferred_element_type=F32)
    closeness = closeness.astype(BF16)
    most = closeness
    while most.shape[0] > 16:
        half = most.shape[0] // 2
        most = jnp.maximum(most[:half], most[half:])
    wet = jnp.max(most.astype(F32), axis=0, keepdims=True) - 1.0
    match = jnp.maximum(closeness - jnp.maximum(wet, 0.0).astype(BF16), 0.0)
    lanes = subs * slots
    values = [[], []]
    for g in range(grids):
        sent = landing[g]
        high = sent.astype(BF16).astype(F32)
        stacked = jnp.concatenate([high, sent - high], axis=0).astype(BF16)
        near = jnp.dot(stacked, match[:, g * lanes : (g + 1) * lanes], preferred_element_type=F32)
        near = near[0:8] + near[8:16]
        for k in range(2):
            values[k].append(near[:, k * LANES : (k + 1) * LANES] * scales[g][k])
    total = []
    for k in range(2):
        parts = values[k]
        for bit in (4, 2, 1):
            width = 8 * bit
            lower = (lane & width) == 0
            parts = [
                jnp.where(
                    lower,
                    one + pltpu.roll(one, LANES - width, 1),
                    two + pltpu.roll(two, width, 1),
                )
                for one, two in zip(parts[:bit], parts[bit:])
            ]
        known = firsts[0][k]
        for g in range(1, grids):
            known = jnp.where(group == g, firsts[g][k], known)
        total.append(parts[0] + known)
    return landing[lax.axis_index("grid")], jnp.concatenate(total, axis=1)


def spread(values, cell, total, height, depth):
    count = cell.shape[1]
    pairs = values.shape[0] // 2
    plane, row, column = split_cell(cell, height, depth)
    onehot = jnp.where(iota((depth, count), 0) == column, 1.0, 0.0).astype(BF16)
    row_here = ((iota((2 * height, count), 0) & (height - 1)) == row) & (cell >= 0)
    tiles = []
    for i in range(pairs):
        twin = [jnp.broadcast_to(values[2 * i + k : 2 * i + k + 1], (height, count)) for k in (0, 1)]
        tiles.append(two_pieces(jnp.concatenate(twin, axis=0)))
    rows = [[], []]
    for p in range(total):
        here = jnp.where(row_here & (plane == p), 1.0, 0.0).astype(BF16)
        for tile in tiles:
            for k in (0, 1):
                rows[k].append(tile[k] * here)
    values = jnp.concatenate([jnp.concatenate(each, axis=0) for each in rows], axis=1)
    field = lax.dot_general(
        values,
        jnp.concatenate([onehot, onehot], axis=1),
        (((1,), (1,)), ((), ())),
        preferred_element_type=F32,
    )
    return field.reshape(total, 2 * pairs, height, depth)


def finish_kernel(sizes, *refs):
    subs = sizes["subs"]
    planes, variables, height, depth = sizes["coarse"]
    blocks = sizes["blocks"]
    parts = four_blocks(sizes, refs[:4])
    coupling, arrived, both, source, gain, mask, fine = refs[4:11]
    out, landing, stage, rows, padded, tall, held, sems = refs[11:]
    total = subs * planes
    gather_rows(sizes, parts, stage, rows)
    first, second = fringe_values(sizes, arrived, landing)
    cell = rows[4:5, :].astype(jnp.int32)
    values = jnp.concatenate([first[:variables], second[:variables]], axis=0)
    landed = spread(values, cell, total, height, depth)
    wet = mask[...] > 0.5
    start = both[:, 0:variables]
    rest = both[:, variables:]
    scale = gain[...]
    change = jnp.where(wet, landed[:, 0:variables] - start, 0.0)
    update = scale * (rest + neighbour_sum(change))
    change = jnp.where(wet, landed[:, variables:] - start, update)
    apart = source[...] - couple(coupling, start + change)
    update = scale * (rest + neighbour_sum(change) + 2.0 * apart)
    correction = jnp.where(wet, change, (1.0 - OMEGA) * change + update)
    padded[0:1] = jnp.zeros((1, variables, height, depth), F32)
    padded[total + 1 : total + 2] = jnp.zeros((1, variables, height, depth), F32)
    padded[1 : total + 1] = correction
    at_row = iota((variables, height, depth), 1)
    coarse_at = iota((depth, 2 * depth), 0)
    fine_at = iota((depth, 2 * depth), 1)
    beside = (fine_at >> 1) - 1 + 2 * (fine_at & 1)
    widen = jnp.where(
        coarse_at == fine_at >> 1, 0.75, jnp.where(coarse_at == beside, 0.25, 0.0)
    ).astype(BF16)
    copies = []
    step = 2
    numbers = plane_numbers(parts[0][planes * variables], blocks)
    for q, number in enumerate(numbers):
        coarse = number >> 1
        along = 0.75 * padded[coarse + 1] + 0.25 * padded[coarse + 2 * (number & 1)]
        below = jnp.where(at_row > 0, pltpu.roll(along, 1, 1), 0.0)
        above = jnp.where(at_row < height - 1, pltpu.roll(along, height - 1, 1), 0.0)
        block = slice(q * variables, (q + 1) * variables)
        tall[block, pl.ds(0, height, stride=2), :] = 0.75 * along + 0.25 * below
        tall[block, pl.ds(1, height, stride=2), :] = 0.75 * along + 0.25 * above
        if q % step == step - 1:
            low = q + 1 - step
            rows_in = tall[low * variables : (q + 1) * variables]
            prolonged = dot_exact(rows_in.reshape(step * variables * 2 * height, depth), widen)
            shape = (step, variables, 2 * height, 2 * depth)
            held[low : q + 1] = fine[low : q + 1] + prolonged.reshape(shape)
            copy = pltpu.make_async_copy(
                held.at[low : q + 1], out.at[0, low : q + 1], sems.at[q // step]
            )
            copy.start()
            copies.append(copy)
    for copy in copies:
        copy.wait()


def fast_shards(
    fine_residual,
    fine_solution,
    plane_of_slot,
    coarse_diagonal,
    coupling,
    donor_cells,
    donor_offsets,
    receptor_cells,
    fringe_counts,
):
    subs = lax.axis_size("sub")
    grids = lax.axis_size("grid")
    coarse = coarse_diagonal.shape[1:]
    planes, variables, height, depth = coarse
    blocks = plane_of_slot.shape[1]
    slots = donor_cells.shape[-1]
    sizes = dict(coarse=coarse, blocks=blocks, slots=slots, grids=grids, subs=subs)
    count = blocks * variables
    total = subs * planes
    whole = (total, variables, height, depth)
    full = jax.ShapeDtypeStruct(whole, F32)
    rows = pltpu.VMEM((8, subs * slots), F32)
    stage = pltpu.VMEM((subs, 8, depth), F32)

    def call(kernel, name, out_shape, *operands, scratch=(), far=(), out_spec=VMEM, aliases={}, cost=None):
        specs = [HBM if any(one is each for each in far) else VMEM for one in operands]
        operands = [
            pltpu.with_memory_space_constraint(one, pltpu.HBM) if spec is HBM else one
            for one, spec in zip(operands, specs)
        ]
        return pl.pallas_call(
            functools.partial(kernel, sizes),
            out_shape=out_shape,
            in_specs=specs,
            out_specs=jax.tree.map(lambda _: out_spec, out_shape),
            scratch_shapes=list(scratch),
            input_output_aliases=aliases,
            cost_estimate=cost,
            compiler_params=pltpu.CompilerParams(vmem_limit_bytes=48 * 1024 * 1024),
            name=name,
        )(*operands)

    offsets = donor_offsets.transpose(0, 2, 1, 3)
    inputs = (fringe_counts, plane_of_slot, coarse_diagonal, donor_cells, offsets, receptor_cells)
    shared = call(
        pack_kernel,
        "pack",
        jax.ShapeDtypeStruct((planes * variables + 1, height, depth), F32),
        *inputs,
        far=inputs,
        scratch=[
            pltpu.VMEM(coarse, F32),
            pltpu.VMEM(offsets.shape[1:], F32),
            pltpu.VMEM((2, 1, slots), jnp.int32),
            pltpu.VMEM(plane_of_slot.shape, jnp.int32),
            pltpu.SMEM(fringe_counts.shape, jnp.int32),
            pltpu.SemaphoreType.DMA((6,)),
        ],
    )
    swap = {bit: [(i, i ^ bit) for i in range(subs)] for bit in (1, 2)}
    partner = lax.ppermute(shared, "sub", swap[2])
    own, corners, fine_here = call(
        restrict_kernel,
        "restrict",
        [
            jax.ShapeDtypeStruct((2 * count, height, depth), F32),
            jax.ShapeDtypeStruct((grids, 8, LANES), F32),
            jax.ShapeDtypeStruct(fine_solution.shape[1:], F32),
        ],
        fine_residual,
        fine_solution,
        shared,
        far=(fine_residual, fine_solution),
        scratch=[
            pltpu.VMEM(fine_solution.shape[1:], F32),
            pltpu.VMEM((2 * count, 2 * height, depth), F32),
            pltpu.SemaphoreType.DMA((blocks,)),
        ],
    )
    size = own.shape[0] + shared.shape[0]
    joined = call(
        join_kernel, "join", jax.ShapeDtypeStruct((size, height, depth), F32), own, shared
    )
    joined = lax.ppermute(joined, "sub", swap[1])
    own, partner = lax.optimization_barrier((own, partner))
    partner, meta = call(
        pass_kernel,
        "pass",
        [
            jax.ShapeDtypeStruct(partner.shape, F32),
            jax.ShapeDtypeStruct((1, height, depth), F32),
        ],
        partner,
        cost=pl.CostEstimate(flops=20_000_000_000, transcendentals=0, bytes_accessed=100_000_000),
    )
    known = (shared, partner, joined, lax.ppermute(meta, "sub", swap[1]))
    across = lax.ppermute(own, "sub", swap[2])
    out, mask, both = call(
        partial_kernel,
        "partial",
        [
            jax.ShapeDtypeStruct((grids * subs, 8, LANES), F32),
            jax.ShapeDtypeStruct((total, 1, height, depth), F32),
            jax.ShapeDtypeStruct((total, 2 * variables, height, depth), F32),
        ],
        *known,
        own,
        corners,
        cost=pl.CostEstimate(flops=20_000_000_000, transcendentals=0, bytes_accessed=100_000_000),
        scratch=[
            rows,
            stage,
            pltpu.VMEM((2, planes * variables + 1, height, depth), F32),
            pltpu.VMEM((total + 2, 2 * variables, height, depth), F32),
            pltpu.VMEM((total + 2, 1, height, depth), F32),
        ],
    )
    arrived = lax.all_to_all(out, ("grid", "sub"), 0, 0, tiled=True)
    piece = jax.ShapeDtypeStruct((blocks // 2 * variables, height, depth), F32)
    pieces = call(split_kernel, "split", [piece] * 4, across)
    pieces = [lax.ppermute(each, "sub", swap[1]) for each in pieces]
    last = lax.ppermute(partner, "sub", swap[1])
    both, source, gain = call(
        assemble_kernel,
        "assemble",
        [jax.ShapeDtypeStruct(both.shape, F32), full, full],
        both,
        across,
        *known[:3],
        last,
        *pieces,
        coupling,
        aliases={0: 0},
    )
    return call(
        finish_kernel,
        "finish",
        jax.ShapeDtypeStruct(fine_solution.shape, F32),
        *known,
        coupling,
        arrived,
        both,
        source,
        gain,
        mask,
        fine_here,
        scratch=[
            pltpu.VMEM((grids, 8, subs * slots), F32),
            stage,
            rows,
            pltpu.VMEM((total + 2, variables, height, depth), F32),
            pltpu.VMEM((count, 2 * height, depth), F32),
            pltpu.VMEM(fine_solution.shape[1:], F32),
            pltpu.SemaphoreType.DMA((blocks // 2,)),
        ],
        out_spec=HBM,
    )


def solution(mesh):
    in_specs = (
        P("grid", "sub", None, None, None),
        P("grid", "sub", None, None, None),
        P("grid", "sub"),
        P("grid", "sub", None, None, None),
        P(),
        P("grid", "sub", None),
        P("grid", "sub", None, None),
        P("grid", "sub", None),
        P(),
    )
    out_specs = P("grid", "sub", None, None, None)
    small = mesh.shape["sub"] == 4 and mesh.shape["grid"] * FRINGE == 64
    body = fast_shards if small else shards
    return jax.shard_map(body, mesh=mesh, in_specs=in_specs, out_specs=out_specs, check_vma=False)
```

```python
import functools

import jax
import jax.numpy as jnp
from jax import lax
from jax.experimental import pallas as pl
from jax.experimental.pallas import tpu as pltpu
from jax.sharding import PartitionSpec as P

FRINGE = 8
SWEEPS = 2


OMEGA = 0.8


def padded_2(block, sides, width):
    for axis, dim in sides:
        count = lax.axis_size(axis)
        forward = [(i, i + 1) for i in range(count - 1)]
        backward = [(target, source) for source, target in forward]
        low = lax.ppermute(
            lax.slice_in_dim(block, block.shape[dim] - width, None, axis=dim), axis, forward
        )
        high = lax.ppermute(lax.slice_in_dim(block, 0, width, axis=dim), axis, backward)
        block = jnp.concatenate([low, block, high], axis=dim)
    return block


def restrict_planes(fine_field):
    dims_in = fine_field.shape
    split_cells = fine_field.reshape(dims_in[:-2] + (dims_in[-2] // 2, 2, dims_in[-1] // 2, 2))
    return 0.125 * jnp.sum(split_cells, axis=(-3, -1))


def pair_sum(field, axis):
    which = axis % field.ndim
    length = field.shape[which]
    empty = jnp.zeros_like(lax.slice_in_dim(field, 0, 1, axis=which))
    below_side = jnp.concatenate(
        [empty, lax.slice_in_dim(field, 0, length - 1, axis=which)], axis=which
    )
    above_side = jnp.concatenate(
        [lax.slice_in_dim(field, 1, length, axis=which), empty], axis=which
    )
    return below_side + above_side


def operate(field, padded, diagonal, coupling):
    which = field.ndim - 4
    length = padded.shape[which]
    beside = lax.slice_in_dim(padded, 2, length, axis=which) + lax.slice_in_dim(
        padded, 0, length - 2, axis=which
    )
    beside = beside + pair_sum(field, field.ndim - 2)
    beside = beside + pair_sum(field, field.ndim - 1)
    coupled = jnp.einsum("vw,...wyz->...vyz", coupling, field, precision=lax.Precision.HIGHEST)
    return (6.0 + diagonal) * field - beside + 2.0 * jnp.tanh(coupled)


def apply_operator(field, diagonal, coupling):
    padded = padded_2(field, (("sub", 0),), 1)
    return operate(field, padded, diagonal, coupling)


def corner_values(flat_field, donor_base, height, depth):
    corners = []
    for step_x in (0, 1):
        for step_y in (0, 1):
            for step_z in (0, 1):
                where_cells = donor_base + step_x * height * depth + step_y * depth + step_z
                corners.append(jnp.take_along_axis(flat_field, where_cells[..., None, :], axis=-1))
    return corners


def blend(corners, offsets):
    frac_x = offsets[..., 0:1, :]
    frac_y = offsets[..., 1:2, :]
    frac_z = offsets[..., 2:3, :]
    summed = None
    number = 0
    for step_x in (0, 1):
        for step_y in (0, 1):
            for step_z in (0, 1):
                weight_x = frac_x if step_x else 1.0 - frac_x
                weight_y = frac_y if step_y else 1.0 - frac_y
                weight_z = frac_z if step_z else 1.0 - frac_z
                term = weight_x * weight_y * weight_z * corners[number]
                summed = term if summed is None else summed + term
                number = number + 1
    return summed


def refine(field, axis):
    which = axis % field.ndim
    length = field.shape[which]
    empty = jnp.zeros_like(lax.slice_in_dim(field, 0, 1, axis=which))
    below_side = jnp.concatenate(
        [empty, lax.slice_in_dim(field, 0, length - 1, axis=which)], axis=which
    )
    above_side = jnp.concatenate(
        [lax.slice_in_dim(field, 1, length, axis=which), empty], axis=which
    )
    first_half = 0.75 * field + 0.25 * below_side
    second_half = 0.75 * field + 0.25 * above_side
    joined = jnp.stack([first_half, second_half], axis=which + 1)
    new_dims = list(field.shape)
    new_dims[which] = 2 * length
    return joined.reshape(new_dims)


def shards(
    fine_residual,
    fine_solution,
    plane_of_slot,
    coarse_diagonal,
    coupling,
    donor_cells,
    donor_offsets,
    receptor_cells,
    fringe_counts,
):
    grid_index = lax.axis_index("grid")
    sub_index = lax.axis_index("sub")
    diagonal = coarse_diagonal[0]
    planes, variables, height, depth_cells = diagonal.shape
    cell_count = planes * height * depth_cells
    plane_ids = plane_of_slot[0]
    blocks = plane_ids.shape[0]
    solution_planes = restrict_planes(fine_solution[0])
    residual_planes = restrict_planes(fine_residual[0])
    contrib = jnp.stack([solution_planes, residual_planes], axis=1).reshape(blocks, -1)
    targets = plane_ids // 2
    wanted = sub_index * planes + jnp.arange(planes, dtype=jnp.int32)
    gathered, gathered_ids = (
        lax.all_gather(contrib, "sub", axis=0, tiled=True),
        lax.all_gather(plane_ids, "sub", axis=0, tiled=True),
    )
    select = ((gathered_ids // 2)[None, :] == wanted[:, None]).astype(jnp.float32)
    owned_sums = jnp.dot(
        select, gathered, precision=lax.Precision.HIGHEST, preferred_element_type=jnp.float32
    )
    owned_sums = owned_sums.reshape(planes, 2, variables, height, depth_cells)
    restricted_solution = owned_sums[:, 0]
    restricted_residual = owned_sums[:, 1]
    forcing = apply_operator(restricted_solution, diagonal, coupling) + restricted_residual
    slot_count = donor_cells.shape[-1]
    column = lax.dynamic_index_in_dim(fringe_counts, grid_index, 1, keepdims=False)
    allowed = jnp.repeat(column, FRINGE)
    live_slot = jnp.arange(slot_count, dtype=jnp.int32) % FRINGE < allowed
    target_cells = jnp.where(live_slot, receptor_cells[0, 0], cell_count)
    receptor_mask = jnp.zeros((cell_count,), jnp.float32).at[target_cells].set(1.0, mode="drop")
    receptor_mask = receptor_mask.reshape(planes, 1, height, depth_cells)
    donor_base = donor_cells[0, 0]
    offsets = donor_offsets[0, 0]
    field = restricted_solution
    for sweep_index in range(SWEEPS):
        flat_field = field.transpose(1, 0, 2, 3).reshape(variables, cell_count)
        corners = corner_values(flat_field, donor_base, height, depth_cells)
        arrived = lax.all_to_all(
            blend(corners, offsets), "grid", split_axis=1, concat_axis=1, tiled=True
        )
        flat_field = flat_field.at[:, target_cells].set(arrived, mode="drop")
        field = flat_field.reshape(variables, planes, height, depth_cells).transpose(1, 0, 2, 3)
        update = field + OMEGA * (forcing - apply_operator(field, diagonal, coupling)) / (
            6.0 + diagonal
        )
        field = jnp.where(receptor_mask > 0.5, field, update)
    correction = (field - restricted_solution).reshape(planes, -1)
    neighbour = targets - 1 + 2 * (plane_ids % 2)
    shard_rows = lax.all_gather(correction, "sub", axis=0, tiled=True)
    row_ids = jnp.arange(shard_rows.shape[0], dtype=jnp.int32)
    weights = 0.75 * (targets[:, None] == row_ids[None, :]).astype(jnp.float32)
    weights = weights + 0.25 * (neighbour[:, None] == row_ids[None, :]).astype(jnp.float32)
    along_x = jnp.dot(
        weights, shard_rows, precision=lax.Precision.HIGHEST, preferred_element_type=jnp.float32
    )
    along_x = along_x.reshape(blocks, variables, height, depth_cells)
    prolonged = refine(refine(along_x, -2), -1)
    return (fine_solution[0] + prolonged)[None]


BF16 = jnp.bfloat16
F32 = jnp.float32
HIGHEST = lax.Precision.HIGHEST
VMEM = pl.BlockSpec(memory_space=pltpu.VMEM)
HBM = pl.BlockSpec(memory_space=pltpu.HBM)
LANES = 128


def two_pieces(values):
    high = values.astype(BF16)
    return high, (values - high.astype(F32)).astype(BF16)


def dot_exact(values, matrix):
    parts = jnp.concatenate(two_pieces(values), axis=1)
    return jnp.dot(
        parts, jnp.concatenate([matrix, matrix], axis=0), preferred_element_type=F32
    )


def dot_near(values, matrix):
    high, low = two_pieces(values)
    matrix_high, matrix_low = two_pieces(matrix)
    return jnp.dot(
        jnp.concatenate([high, low, high], axis=1),
        jnp.concatenate([matrix_high, matrix_high, matrix_low], axis=0),
        preferred_element_type=F32,
    )


def iota(shape, dim):
    return lax.broadcasted_iota(jnp.int32, shape, dim)


def bits(size):
    assert size & (size - 1) == 0
    return size.bit_length() - 1


def split_cell(cell, height, depth):
    row_bits, column_bits = bits(height), bits(depth)
    row = (cell >> column_bits) & (height - 1)
    return cell >> (row_bits + column_bits), row, cell & (depth - 1)


def neighbour_sum(field):
    total, variables, height, depth = field.shape
    flat = field.reshape(total * variables, height, depth)
    at_row = iota(flat.shape, 1)
    at_column = iota(flat.shape, 2)
    beside = jnp.where(at_row > 0, pltpu.roll(flat, 1, 1), 0.0)
    beside = beside + jnp.where(at_row < height - 1, pltpu.roll(flat, height - 1, 1), 0.0)
    beside = beside + jnp.where(at_column > 0, pltpu.roll(flat, 1, 2), 0.0)
    beside = beside + jnp.where(at_column < depth - 1, pltpu.roll(flat, depth - 1, 2), 0.0)
    beside = beside.reshape(field.shape)
    empty = jnp.zeros((1, variables, height, depth), F32)
    beside = beside + jnp.concatenate([empty, field[: total - 1]], axis=0)
    return beside + jnp.concatenate([field[1:], empty], axis=0)


def live_cells(counts, grid_index, grids, receptors, base):
    lane = iota(receptors.shape, 1)
    allowed = jnp.zeros(receptors.shape, jnp.int32)
    for g in range(grids):
        allowed = jnp.where(lane >> bits(FRINGE) == g, counts[g, grid_index], allowed)
    return jnp.where((lane & (FRINGE - 1)) < allowed, receptors + base, -1)


def receptor_mask(cell, total, height, depth):
    count = cell.shape[1]
    plane, row, column = split_cell(cell, height, depth)
    onehot = jnp.where(iota((depth, count), 0) == column, 1.0, 0.0).astype(BF16)
    row_here = (iota((height, count), 0) == row) & (cell >= 0)
    here = jnp.concatenate([jnp.where(row_here & (plane == p), 1.0, 0.0) for p in range(total)], 0)
    contract = (((1,), (1,)), ((), ()))
    mask = lax.dot_general(here.astype(BF16), onehot, contract, preferred_element_type=F32)
    return mask.reshape(total, 1, height, depth), here, onehot


def start_copies(pairs, sems):
    copies = [pltpu.make_async_copy(*pair, sems.at[i]) for i, pair in enumerate(pairs)]
    for copy in copies:
        copy.start()
    return copies


def pack_kernel(
    sizes, counts, ids, diagonal, donors, offsets, receptors, out, held, rows, cells, planes_of, allowed, sems
):
    planes, variables, height, depth = sizes["coarse"]
    slots = sizes["slots"]
    base = lax.axis_index("sub") * (planes * height * depth)
    grid_index = lax.axis_index("grid")
    count = planes * variables
    copies = start_copies(
        [
            (counts, allowed),
            (receptors.at[0], cells.at[0]),
            (donors.at[0], cells.at[1]),
            (offsets.at[0], rows),
            (ids, planes_of),
            (diagonal.at[0], held),
        ],
        sems,
    )
    out[count] = jnp.zeros((height, depth), F32)
    for copy in copies:
        copy.wait()
    out[0:count] = OMEGA / (6.0 + held[...].reshape(count, height, depth))
    cell = live_cells(allowed, grid_index, sizes["grids"], cells[0], base)
    out[count, 0:1, 0:slots] = (cells[1] + base).astype(F32)
    for k in range(3):
        out[count, k + 1 : k + 2, 0:slots] = rows[k]
    out[count, 4:5, 0:slots] = cell.astype(F32)
    out[count, 5:6, 0 : sizes["blocks"]] = planes_of[...].astype(F32)


def find_corners(sizes, shared, out):
    planes, variables, height, depth = sizes["coarse"]
    slots, grids = sizes["slots"], sizes["grids"]
    grid_index = lax.axis_index("grid")
    base = lax.axis_index("sub") * (planes * height * depth)
    meta = shared[planes * variables, :, 0:slots]
    cell = meta[4:5].astype(jnp.int32)
    cell = jnp.where(cell >= 0, cell - base, -1)
    mask, _, _ = receptor_mask(cell, planes, height, depth)
    gain = shared[0 : planes * variables].reshape(planes, variables, height, depth)
    fields = jnp.concatenate([gain, mask], axis=1)
    donors = meta[0:1].astype(jnp.int32) - base
    twice = jnp.concatenate([donors, donors], axis=1)
    step_z = iota(twice.shape, 1) >> bits(slots)
    plane, row, column = split_cell(twice, height, depth)
    onehot = jnp.where(iota((depth, LANES), 0) == column + step_z, 1.0, 0.0).astype(BF16)
    count = planes * (variables + 1) * height
    at_column = dot_exact(fields.reshape(count, depth), onehot)
    at_column = at_column.reshape(planes, variables + 1, height, LANES)
    both = jnp.concatenate([meta[1:4], meta[1:4]], axis=1)
    weight_z = jnp.where(step_z == 1, both[2:3], 1.0 - both[2:3])
    at_row = iota((height, LANES), 0)
    empty = jnp.zeros((5, LANES), F32)
    tiles = []
    for step_x in (0, 1):
        weight_x = both[0:1] if step_x else 1.0 - both[0:1]
        by_plane = None
        for p in range(planes):
            term = jnp.where(plane + step_x == p, at_column[p], 0.0)
            by_plane = term if by_plane is None else by_plane + term
        for step_y in (0, 1):
            weight_y = both[1:2] if step_y else 1.0 - both[1:2]
            here = jnp.where(at_row == row + step_y, 1.0, 0.0)
            found = jnp.sum(by_plane * here[None], axis=1)
            wet = found[variables : variables + 1]
            scaled = weight_x * weight_y * weight_z * (found[:variables] * (1.0 - wet) + wet)
            left = jnp.concatenate([empty, scaled[0:3]], axis=0)
            right = jnp.concatenate([empty, scaled[3:5], empty[0:1]], axis=0)
            tiles.append((left, right))
    lane = iota((8, LANES), 1)
    sublane = iota((8, LANES), 0)
    cells = jnp.broadcast_to(jnp.concatenate([meta[4:5], meta[4:5]], axis=1), (8, LANES))
    starts = jnp.broadcast_to(jnp.concatenate([meta[0:1], meta[0:1]], axis=1), (8, LANES))
    starts = pltpu.roll(starts, 8 * grid_index, 1)
    last = (sublane == 7) & (lane >= 64)
    mine = last & (((lane >> 3) & 7) == grid_index)
    for h in range(grids):
        tile = jnp.zeros((8, LANES), F32)
        for c in range(8):
            for k in (0, 1):
                shift = (64 * k + 8 * c - (c % 2) * 64 - 8 * h) % LANES
                moved = pltpu.roll(tiles[c // 2][k], shift, 1)
                tile = jnp.where(lane >> 3 == 8 * k + c, moved, tile)
        tile = jnp.where(last, cells, tile)
        out[h] = jnp.where(mine, pltpu.roll(starts, (LANES - 8 * h) % LANES, 1), tile)


def restrict_kernel(sizes, residual, fine, shared, out, corners, fine_here, held, wide, sems):
    planes, variables, height, depth = sizes["coarse"]
    blocks = sizes["blocks"]
    step = 8
    copies = start_copies(
        [
            (source.at[0, q : q + step], target.at[q : q + step])
            for source, target in ((fine, fine_here), (residual, held))
            for q in range(0, blocks, step)
        ],
        sems,
    )
    find_corners(sizes, shared, corners)
    pair = jnp.where(
        iota((2 * depth, depth), 0) >> 1 == iota((2 * depth, depth), 1), 0.125, 0.0
    ).astype(BF16)
    count = step * variables
    for i, copy in enumerate(copies):
        k, q = divmod(i * step, blocks)
        copy.wait()
        rows = (fine_here, held)[k][q : q + step].reshape(count * 2 * height, 2 * depth)
        here = pl.ds(i * count, count)
        wide[here] = dot_exact(rows, pair).reshape(count, 2 * height, depth)
        out[here] = (
            wide[here, pl.ds(0, height, stride=2), :] + wide[here, pl.ds(1, height, stride=2), :]
        )


def hats(shape, dim, start, frac):
    at = iota(shape, dim)
    return jnp.where(at == start, 1.0 - frac, 0.0) + jnp.where(at == start + 1, frac, 0.0)


def interpolate(fields, rows, base):
    planes, variables, height, depth = fields[0].shape
    count = rows.shape[1]
    cell = rows[0:1, :].astype(jnp.int32) - base
    plane, row, column = split_cell(cell, height, depth)
    frac_x, frac_y, frac_z = rows[1:2, :], rows[2:3, :], rows[3:4, :]
    weight_z = hats((depth, count), 0, column, frac_z)
    weight_y = hats((height, count), 0, row, frac_y)
    lower = iota((depth, count), 1) < count // 2
    weight_z = jnp.concatenate(
        [jnp.where(lower, weight_z, 0.0), jnp.where(lower, 0.0, weight_z)], axis=0
    )
    both = jnp.concatenate([each.reshape(-1, depth) for each in fields], axis=1)
    along_z = dot_near(both, weight_z).reshape(planes, variables, height, count)
    summed = None
    for p in range(planes):
        weight_x = jnp.where(plane == p, 1.0 - frac_x, 0.0) + jnp.where(
            plane + 1 == p, frac_x, 0.0
        )
        term = along_z[p] * (weight_x * weight_y)[None]
        summed = term if summed is None else summed + term
    return jnp.sum(summed, axis=1)


def gather_rows(sizes, known, stage, rows):
    slots = sizes["slots"]
    for part, bit in zip(known, (0, 2, 1, 3)):
        stage[lax.axis_index("sub") ^ bit] = part[part.shape[0] - 1]
    for j, s in enumerate((0, 2, 1, 3)):
        rows[:, j * slots : (j + 1) * slots] = stage[s, :, 0:slots]


def partial_kernel(sizes, *refs):
    subs, grids, slots, blocks = sizes["subs"], sizes["grids"], sizes["slots"], sizes["blocks"]
    planes, variables, height, depth = sizes["coarse"]
    *known, own, corners = refs[:-8]
    joined = known[2]
    known = four_blocks(sizes, known)
    out, mask_out, both, rows, stage, pair, padded, wet = refs[-8:]
    total = subs * planes
    sub_index = lax.axis_index("sub")
    grid_index = lax.axis_index("grid")
    count = planes * variables
    gather_rows(sizes, known, stage, rows)
    pair[sub_index >> 1] = known[0][...]
    pair[1 - (sub_index >> 1)] = known[1][...]
    mask, _, _ = receptor_mask(rows[4:5, :].astype(jnp.int32), total, height, depth)
    mask_out[...] = mask
    wet[1 : total + 1] = mask
    padded[...] = jnp.zeros(padded.shape, F32)
    inner = padded.at[1 : total + 1]
    add_planes(sizes, [own], plane_numbers(known[0][count], blocks), inner)
    add_planes(sizes, [joined], plane_numbers(known[2][count], blocks), inner)
    both[...] = padded[1 : total + 1]
    core = sub_index & 1
    fields = []
    for k in range(2):
        start = (core + 2 * k) * planes
        here = padded[pl.ds(start, planes + 2)]
        dry = wet[pl.ds(start, planes + 2)] < 0.5
        drowned = jnp.where(dry, 0.0, here[:, 0:variables])
        beside = neighbour_sum(drowned)[1 : planes + 1]
        restricted, residual = here[1 : planes + 1, :variables], here[1 : planes + 1, variables:]
        gain = pair[k, 0:count].reshape(sizes["coarse"])
        swept = jnp.where(dry[1 : planes + 1], restricted + gain * (residual - beside), 0.0)
        fields.append(jnp.concatenate([restricted, swept], axis=1))
    half = jnp.concatenate([pair[0, count, :, 0:slots], pair[1, count, :, 0:slots]], axis=1)
    lane = iota((1, LANES), 1)
    base = (core + 2 * (lane >> bits(slots))) * (planes * height * depth)
    values = interpolate(fields, half, base)
    empty = jnp.zeros((3, LANES), F32)
    first = jnp.concatenate([values[:variables], empty], axis=0)
    second = jnp.concatenate([values[variables:], empty], axis=0)
    second = pltpu.roll(second, 8 * grid_index, 1)
    mine = ((iota((8, LANES), 1) >> 3) & 7) == grid_index
    top = iota((8, LANES), 0) < variables
    for h in range(grids):
        tile = jnp.where(mine, pltpu.roll(second, (LANES - 8 * h) % LANES, 1), first)
        tile = jnp.where(top, tile, corners[h])
        for s in range(subs):
            out[h * subs + s] = tile


def plane_numbers(meta, blocks):
    row = meta[5:6, :]
    lane = iota(row.shape, 1)
    return [jnp.sum(jnp.where(lane == q, row, 0.0)).astype(jnp.int32) for q in range(blocks)]


def add_planes(sizes, pieces, numbers, both):
    variables, blocks = sizes["coarse"][1], sizes["blocks"]
    width = min(pieces[0].shape[0] // variables, 2 * blocks)
    for q in range(blocks):
        coarse = pl.ds(numbers[q] >> 1, 1)
        for k in range(2):
            i = k * blocks + q
            at = i % width * variables
            part = pieces[i // width][at : at + variables]
            both[coarse, pl.ds(k * variables, variables)] += part[None]


def pass_kernel(sizes, source, out, last):
    out[...] = source[...]
    last[0] = source[source.shape[0] - 1]


def join_kernel(sizes, *refs):
    at = 0
    for part in refs[:-1]:
        refs[-1][at : at + part.shape[0]] = part[...]
        at = at + part.shape[0]


def four_blocks(sizes, known):
    shared, partner, joined, last = known
    size = shared.shape[0]
    return shared, partner, joined.at[joined.shape[0] - size :], last


def split_kernel(sizes, whole, *pieces):
    at = 0
    for piece in pieces:
        piece[...] = whole[at : at + piece.shape[0]]
        at = at + piece.shape[0]


def assemble_kernel(sizes, before, across, shared, partner, joined, last, *refs):
    variables = sizes["coarse"][1]
    pieces = refs[:-4]
    coupling, both, source, gain = refs[-4:]
    planes = sizes["coarse"][0]
    known = four_blocks(sizes, (shared, partner, joined, last))
    for part, bit in zip(known, (0, 2, 1, 3)):
        owner = lax.axis_index("sub") ^ bit
        end = part.shape[0] - 1
        here = part[end - planes * variables : end].reshape(sizes["coarse"])
        gain[pl.ds(owner * planes, planes)] = here
    count = planes * variables
    blocks = sizes["blocks"]
    both[...] = before[...]
    add_planes(sizes, [across], plane_numbers(partner[count], blocks), both)
    add_planes(sizes, pieces, plane_numbers(known[3][count], blocks), both)
    source[...] = couple(coupling, both[:, 0:variables])


def couple(coupling, field):
    variables = field.shape[1]
    outs = []
    for v in range(variables):
        summed = None
        for x in range(variables):
            term = coupling[v : v + 1, x : x + 1][None] * field[:, x]
            summed = term if summed is None else summed + term
        outs.append(jnp.tanh(summed)[:, None])
    return jnp.concatenate(outs, axis=1)


def target_features(cell, height, depth):
    plane, row, column = split_cell(jnp.maximum(cell, 0), height, depth)
    square = plane * plane + row * row + column * column
    square = jnp.where(cell >= 0, square, 1 << 15)
    coarse = (square >> bits(LANES)) << bits(LANES)
    one = jnp.ones(cell.shape, jnp.int32)
    rows = [plane, row, column, one, one, one, -coarse, 2 + coarse - square]
    return jnp.concatenate([each.astype(F32) for each in rows], axis=0)


def corner_features(cell, height, depth):
    plane, row, column = split_cell(cell, height, depth)
    square = plane * plane + row * row + column * column
    coarse = (square >> bits(LANES)) << bits(LANES)
    one = jnp.ones(cell.shape, jnp.int32)
    rows = [2 * plane, 2 * row, 2 * column, -coarse, coarse - square, 0 * one, one, one]
    return jnp.concatenate([each.astype(F32) for each in rows], axis=0)


def fringe_values(sizes, arrived, landing):
    subs, grids, slots = sizes["subs"], sizes["grids"], sizes["slots"]
    _, _, height, depth = sizes["coarse"]
    lane = iota((8, LANES), 1)
    sublane = iota((8, LANES), 0)
    group = (lane >> 3) & 7
    firsts = []
    for g in range(grids):
        halves = []
        for k in range(2):
            half = arrived[g * subs + k]
            for s in range(k + 2, subs, 2):
                half = half + arrived[g * subs + s]
            halves.append(half)
        firsts.append(halves)
    for g in range(grids):
        for k in range(2):
            sent = firsts[g][k]
            for other in range(grids):
                if other != g:
                    moved = pltpu.roll(firsts[other][k], (8 * other - 8 * g) % LANES, 1)
                    sent = jnp.where(group == other, moved, sent)
            landing[g, :, k * LANES : (k + 1) * LANES] = sent
    cells = [jnp.zeros((8, LANES), F32)] * 2
    scales = []
    for g in range(grids):
        scale = []
        for k in range(2):
            one, two = arrived[g * subs + k], arrived[g * subs + k + 2]
            low = jnp.where(lane < 64, one, pltpu.roll(two, 64, 1))
            high = jnp.where(lane < 64, pltpu.roll(one, 64, 1), two)
            scale.append(jnp.where(sublane < 3, pltpu.roll(low, 3, 0), pltpu.roll(high, 6, 0)))
            cells[k] = jnp.where(sublane == g, pltpu.roll(high, (g + 1) % 8, 0), cells[k])
        scales.append(scale)
    targets, corners = [], []
    step = ((group >> 2) * height + ((group >> 1) & 1)) * depth + (group & 1)
    for k in range(2):
        targets.append(jnp.where(group == sublane, -1.0, cells[k]))
        starts = jnp.where(group == sublane, cells[k], 0.0)
        parts = []
        for half in (lane < 64, lane >= 64):
            start = jnp.where(half, starts, 0.0)
            for shift in (64, 32, 16, 8):
                start = start + pltpu.roll(start, shift, 1)
            parts.append(start)
        corners.append(jnp.where(lane < 64, parts[0], parts[1]).astype(jnp.int32) + step)
    targets = jnp.concatenate(targets, axis=1).astype(jnp.int32)
    corners = jnp.concatenate(corners, axis=1)
    theirs = target_features(targets, height, depth).T.astype(BF16)
    ours = corner_features(corners, height, depth)
    which = iota(ours.shape, 0) & 7
    mine = [jnp.where(which == g, ours, 0.0).astype(BF16) for g in range(grids)]
    closeness = jnp.dot(theirs, jnp.concatenate(mine, axis=1), preferred_element_type=F32)
    closeness = closeness.astype(BF16)
    most = closeness
    while most.shape[0] > 16:
        half = most.shape[0] // 2
        most = jnp.maximum(most[:half], most[half:])
    wet = jnp.max(most.astype(F32), axis=0, keepdims=True) - 1.0
    match = jnp.maximum(closeness - jnp.maximum(wet, 0.0).astype(BF16), 0.0)
    lanes = subs * slots
    values = [[], []]
    for g in range(grids):
        sent = landing[g]
        high = sent.astype(BF16).astype(F32)
        stacked = jnp.concatenate([high, sent - high], axis=0).astype(BF16)
        near = jnp.dot(stacked, match[:, g * lanes : (g + 1) * lanes], preferred_element_type=F32)
        near = near[0:8] + near[8:16]
        for k in range(2):
            values[k].append(near[:, k * LANES : (k + 1) * LANES] * scales[g][k])
    total = []
    for k in range(2):
        parts = values[k]
        for bit in (4, 2, 1):
            width = 8 * bit
            lower = (lane & width) == 0
            parts = [
                jnp.where(
                    lower,
                    one + pltpu.roll(one, LANES - width, 1),
                    two + pltpu.roll(two, width, 1),
                )
                for one, two in zip(parts[:bit], parts[bit:])
            ]
        known = firsts[0][k]
        for g in range(1, grids):
            known = jnp.where(group == g, firsts[g][k], known)
        total.append(parts[0] + known)
    return landing[lax.axis_index("grid")], jnp.concatenate(total, axis=1)


def spread(values, cell, total, height, depth):
    count = cell.shape[1]
    pairs = values.shape[0] // 2
    plane, row, column = split_cell(cell, height, depth)
    onehot = jnp.where(iota((depth, count), 0) == column, 1.0, 0.0).astype(BF16)
    row_here = ((iota((2 * height, count), 0) & (height - 1)) == row) & (cell >= 0)
    tiles = []
    for i in range(pairs):
        twin = [jnp.broadcast_to(values[2 * i + k : 2 * i + k + 1], (height, count)) for k in (0, 1)]
        tiles.append(two_pieces(jnp.concatenate(twin, axis=0)))
    rows = [[], []]
    for p in range(total):
        here = jnp.where(row_here & (plane == p), 1.0, 0.0).astype(BF16)
        for tile in tiles:
            for k in (0, 1):
                rows[k].append(tile[k] * here)
    values = jnp.concatenate([jnp.concatenate(each, axis=0) for each in rows], axis=1)
    field = lax.dot_general(
        values,
        jnp.concatenate([onehot, onehot], axis=1),
        (((1,), (1,)), ((), ())),
        preferred_element_type=F32,
    )
    return field.reshape(total, 2 * pairs, height, depth)


def finish_kernel(sizes, *refs):
    subs = sizes["subs"]
    planes, variables, height, depth = sizes["coarse"]
    blocks = sizes["blocks"]
    parts = four_blocks(sizes, refs[:4])
    coupling, arrived, both, source, gain, mask, fine = refs[4:11]
    out, landing, stage, rows, padded, tall, held, sems = refs[11:]
    total = subs * planes
    gather_rows(sizes, parts, stage, rows)
    first, second = fringe_values(sizes, arrived, landing)
    cell = rows[4:5, :].astype(jnp.int32)
    values = jnp.concatenate([first[:variables], second[:variables]], axis=0)
    landed = spread(values, cell, total, height, depth)
    wet = mask[...] > 0.5
    start = both[:, 0:variables]
    rest = both[:, variables:]
    scale = gain[...]
    change = jnp.where(wet, landed[:, 0:variables] - start, 0.0)
    update = scale * (rest + neighbour_sum(change))
    change = jnp.where(wet, landed[:, variables:] - start, update)
    apart = source[...] - couple(coupling, start + change)
    update = scale * (rest + neighbour_sum(change) + 2.0 * apart)
    correction = jnp.where(wet, change, (1.0 - OMEGA) * change + update)
    padded[0:1] = jnp.zeros((1, variables, height, depth), F32)
    padded[total + 1 : total + 2] = jnp.zeros((1, variables, height, depth), F32)
    padded[1 : total + 1] = correction
    at_row = iota((variables, height, depth), 1)
    coarse_at = iota((depth, 2 * depth), 0)
    fine_at = iota((depth, 2 * depth), 1)
    beside = (fine_at >> 1) - 1 + 2 * (fine_at & 1)
    widen = jnp.where(
        coarse_at == fine_at >> 1, 0.75, jnp.where(coarse_at == beside, 0.25, 0.0)
    ).astype(BF16)
    copies = []
    step = 1
    numbers = plane_numbers(parts[0][planes * variables], blocks)
    for q, number in enumerate(numbers):
        coarse = number >> 1
        along = 0.75 * padded[coarse + 1] + 0.25 * padded[coarse + 2 * (number & 1)]
        below = jnp.where(at_row > 0, pltpu.roll(along, 1, 1), 0.0)
        above = jnp.where(at_row < height - 1, pltpu.roll(along, height - 1, 1), 0.0)
        block = slice(q * variables, (q + 1) * variables)
        tall[block, pl.ds(0, height, stride=2), :] = 0.75 * along + 0.25 * below
        tall[block, pl.ds(1, height, stride=2), :] = 0.75 * along + 0.25 * above
        if q % step == step - 1:
            low = q + 1 - step
            rows_in = tall[low * variables : (q + 1) * variables]
            prolonged = dot_exact(rows_in.reshape(step * variables * 2 * height, depth), widen)
            shape = (step, variables, 2 * height, 2 * depth)
            held[low : q + 1] = fine[low : q + 1] + prolonged.reshape(shape)
            copy = pltpu.make_async_copy(
                held.at[low : q + 1], out.at[0, low : q + 1], sems.at[q // step]
            )
            copy.start()
            copies.append(copy)
    for copy in copies:
        copy.wait()


def fast_shards(
    fine_residual,
    fine_solution,
    plane_of_slot,
    coarse_diagonal,
    coupling,
    donor_cells,
    donor_offsets,
    receptor_cells,
    fringe_counts,
):
    subs = lax.axis_size("sub")
    grids = lax.axis_size("grid")
    coarse = coarse_diagonal.shape[1:]
    planes, variables, height, depth = coarse
    blocks = plane_of_slot.shape[1]
    slots = donor_cells.shape[-1]
    sizes = dict(coarse=coarse, blocks=blocks, slots=slots, grids=grids, subs=subs)
    count = blocks * variables
    total = subs * planes
    whole = (total, variables, height, depth)
    full = jax.ShapeDtypeStruct(whole, F32)
    rows = pltpu.VMEM((8, subs * slots), F32)
    stage = pltpu.VMEM((subs, 8, depth), F32)

    def call(kernel, name, out_shape, *operands, scratch=(), far=(), out_spec=VMEM, aliases={}, cost=None):
        specs = [HBM if any(one is each for each in far) else VMEM for one in operands]
        operands = [
            pltpu.with_memory_space_constraint(one, pltpu.HBM) if spec is HBM else one
            for one, spec in zip(operands, specs)
        ]
        return pl.pallas_call(
            functools.partial(kernel, sizes),
            out_shape=out_shape,
            in_specs=specs,
            out_specs=jax.tree.map(lambda _: out_spec, out_shape),
            scratch_shapes=list(scratch),
            input_output_aliases=aliases,
            cost_estimate=cost,
            compiler_params=pltpu.CompilerParams(vmem_limit_bytes=48 * 1024 * 1024),
            name=name,
        )(*operands)

    offsets = donor_offsets.transpose(0, 2, 1, 3)
    inputs = (fringe_counts, plane_of_slot, coarse_diagonal, donor_cells, offsets, receptor_cells)
    shared = call(
        pack_kernel,
        "pack",
        jax.ShapeDtypeStruct((planes * variables + 1, height, depth), F32),
        *inputs,
        far=inputs,
        scratch=[
            pltpu.VMEM(coarse, F32),
            pltpu.VMEM(offsets.shape[1:], F32),
            pltpu.VMEM((2, 1, slots), jnp.int32),
            pltpu.VMEM(plane_of_slot.shape, jnp.int32),
            pltpu.SMEM(fringe_counts.shape, jnp.int32),
            pltpu.SemaphoreType.DMA((6,)),
        ],
    )
    swap = {bit: [(i, i ^ bit) for i in range(subs)] for bit in (1, 2)}
    partner = lax.ppermute(shared, "sub", swap[2])
    own, corners, fine_here = call(
        restrict_kernel,
        "restrict",
        [
            jax.ShapeDtypeStruct((2 * count, height, depth), F32),
            jax.ShapeDtypeStruct((grids, 8, LANES), F32),
            jax.ShapeDtypeStruct(fine_solution.shape[1:], F32),
        ],
        fine_residual,
        fine_solution,
        shared,
        far=(fine_residual, fine_solution),
        scratch=[
            pltpu.VMEM(fine_solution.shape[1:], F32),
            pltpu.VMEM((2 * count, 2 * height, depth), F32),
            pltpu.SemaphoreType.DMA((blocks,)),
        ],
    )
    size = own.shape[0] + shared.shape[0]
    joined = call(
        join_kernel, "join", jax.ShapeDtypeStruct((size, height, depth), F32), own, shared
    )
    joined = lax.ppermute(joined, "sub", swap[1])
    own, partner = lax.optimization_barrier((own, partner))
    partner, meta = call(
        pass_kernel,
        "pass",
        [
            jax.ShapeDtypeStruct(partner.shape, F32),
            jax.ShapeDtypeStruct((1, height, depth), F32),
        ],
        partner,
        cost=pl.CostEstimate(flops=20_000_000_000, transcendentals=0, bytes_accessed=100_000_000),
    )
    known = (shared, partner, joined, lax.ppermute(meta, "sub", swap[1]))
    across = lax.ppermute(own, "sub", swap[2])
    out, mask, both = call(
        partial_kernel,
        "partial",
        [
            jax.ShapeDtypeStruct((grids * subs, 8, LANES), F32),
            jax.ShapeDtypeStruct((total, 1, height, depth), F32),
            jax.ShapeDtypeStruct((total, 2 * variables, height, depth), F32),
        ],
        *known,
        own,
        corners,
        cost=pl.CostEstimate(flops=20_000_000_000, transcendentals=0, bytes_accessed=100_000_000),
        scratch=[
            rows,
            stage,
            pltpu.VMEM((2, planes * variables + 1, height, depth), F32),
            pltpu.VMEM((total + 2, 2 * variables, height, depth), F32),
            pltpu.VMEM((total + 2, 1, height, depth), F32),
        ],
    )
    arrived = lax.all_to_all(out, ("grid", "sub"), 0, 0, tiled=True)
    piece = jax.ShapeDtypeStruct((blocks // 2 * variables, height, depth), F32)
    pieces = call(split_kernel, "split", [piece] * 4, across)
    pieces = [lax.ppermute(each, "sub", swap[1]) for each in pieces]
    last = lax.ppermute(partner, "sub", swap[1])
    both, source, gain = call(
        assemble_kernel,
        "assemble",
        [jax.ShapeDtypeStruct(both.shape, F32), full, full],
        both,
        across,
        *known[:3],
        last,
        *pieces,
        coupling,
        aliases={0: 0},
    )
    return call(
        finish_kernel,
        "finish",
        jax.ShapeDtypeStruct(fine_solution.shape, F32),
        *known,
        coupling,
        arrived,
        both,
        source,
        gain,
        mask,
        fine_here,
        scratch=[
            pltpu.VMEM((grids, 8, subs * slots), F32),
            stage,
            rows,
            pltpu.VMEM((total + 2, variables, height, depth), F32),
            pltpu.VMEM((count, 2 * height, depth), F32),
            pltpu.VMEM(fine_solution.shape[1:], F32),
            pltpu.SemaphoreType.DMA((blocks,)),
        ],
        out_spec=HBM,
    )


def solution(mesh):
    in_specs = (
        P("grid", "sub", None, None, None),
        P("grid", "sub", None, None, None),
        P("grid", "sub"),
        P("grid", "sub", None, None, None),
        P(),
        P("grid", "sub", None),
        P("grid", "sub", None, None),
        P("grid", "sub", None),
        P(),
    )
    out_specs = P("grid", "sub", None, None, None)
    small = mesh.shape["sub"] == 4 and mesh.shape["grid"] * FRINGE == 64
    body = fast_shards if small else shards
    return jax.shard_map(body, mesh=mesh, in_specs=in_specs, out_specs=out_specs, check_vma=False)
```
